32 devices in a mesh: rows: 16 (over z, x, core), fsdp: 2 (over y).
Axes of the slice: x: 2, y: 2, z: 4, core: 2. Of those that a mesh axis runs over, the one named last changes fastest.
Arguments:
- tokens: bfloat16 [2, 4096, 512], P('fsdp', 'rows'), may hold values from -6 to 6
- w_qkv: bfloat16 [512, 1536], P(('rows', 'fsdp')), may hold values from -0.25 to 0.25
- w_out: bfloat16 [512, 512], P(('rows', 'fsdp')), may hold values from -0.75 to 0.75
- w_up: bfloat16 [512, 2048], P(('rows', 'fsdp')), may hold values from -0.25 to 0.25
- w_down: bfloat16 [2048, 512], P(('rows', 'fsdp')), may hold values from -0.125 to 0.125
- norm1_gain: bfloat16 [512], P(('rows', 'fsdp')), may hold values from 0.099609375 to 1.8984375
- norm1_bias: bfloat16 [512], P(('rows', 'fsdp')), may hold values from -4 to 4
- query_bias: bfloat16 [512], P(('rows', 'fsdp')), may hold values from -4 to 4
- value_bias: bfloat16 [512], P(('rows', 'fsdp')), may hold values from -4 to 4
- out_bias: bfloat16 [512], P(('rows', 'fsdp')), may hold values from -4 to 4
- norm2_gain: bfloat16 [512], P(('rows', 'fsdp')), may hold values from 0.099609375 to 1.8984375
- norm2_bias: bfloat16 [512], P(('rows', 'fsdp')), may hold values from -4 to 4
- up_bias: bfloat16 [2048], P(('rows', 'fsdp')), may hold values from -4 to 4
- down_bias: bfloat16 [512], P(('rows', 'fsdp')), may hold values from -4 to 4
- cotangent: bfloat16 [2, 4096, 512], P('fsdp', 'rows'), may hold values from -6 to 6
- table_start: int32 [2, 8], P('fsdp'), may hold values from 0 to 4064, as said below
- support_count: int32 [2, 8], P('fsdp'), may hold values from 1 to 2904, as said below
- query_count: int32 [2, 8], P('fsdp'), may hold values from 1 to 968, as said below
Outputs:
- outputs: bfloat16 [2, 4096, 512], P('fsdp', 'rows')
- grad_tokens: bfloat16 [2, 4096, 512], P('fsdp', 'rows')
- grad_w_qkv: float32 [512, 1536], P(('rows', 'fsdp'))
- grad_w_out: float32 [512, 512], P(('rows', 'fsdp'))
- grad_w_up: float32 [512, 2048], P(('rows', 'fsdp'))
- grad_w_down: float32 [2048, 512], P(('rows', 'fsdp'))
- grad_norm1_gain: float32 [512], P(('rows', 'fsdp'))
- grad_norm1_bias: float32 [512], P(('rows', 'fsdp'))
- grad_query_bias: float32 [512], P(('rows', 'fsdp'))
- grad_value_bias: float32 [512], P(('rows', 'fsdp'))
- grad_out_bias: float32 [512], P(('rows', 'fsdp'))
- grad_norm2_gain: float32 [512], P(('rows', 'fsdp'))
- grad_norm2_bias: float32 [512], P(('rows', 'fsdp'))
- grad_up_bias: float32 [2048], P(('rows', 'fsdp'))
- grad_down_bias: float32 [512], P(('rows', 'fsdp'))
The draws below stay inside these ranges and needn't reach their ends.
Inputs may be any that keep to these rules, and one draw needn't show every extreme that they name: `table_start`: in each group the starts rise, the first is 0, and each table runs up to the next start (the last up to 4096); the last table of every group has 32 rows. `support_count`: at least one support row in every table. `query_count`: support plus query rows never exceed the table's rows; the rest of a table is padding.
All inputs are finite; a program needn't handle non-finite values.
Results may differ from the reference program's by a relative error of at most 0.013.
Values may be sent and summed in bfloat16 or wider, within the bound.
No kernel may reach another device: no remote copies, remote signals or barrier semaphores. Data moves between devices by JAX's collectives and lax.ppermute only.
A program may use at most 128 MiB of HBM per device.

```python
import math
import jax
import jax.numpy as jnp
from jax import lax

D = 512
HEADS = 4
HEAD_DIM = 128
FF = 2048
NT = 8
SLOT = 32
GROUP_ROWS = 4096
N_FSDP = 2


def table_layout(key):
    longest = jax.random.randint(jax.random.fold_in(key, 101), (N_FSDP,), 0, NT - 1)
    slots = jnp.arange(NT, dtype=jnp.int32)
    is_longest = slots[None, :] == longest[:, None]
    lengths = jnp.where(is_longest, GROUP_ROWS - (NT - 1) * SLOT, SLOT).astype(jnp.int32)
    starts = (jnp.cumsum(lengths, axis=1) - lengths).astype(jnp.int32)
    drawn_support = jax.random.randint(jax.random.fold_in(key, 102), (N_FSDP, NT), lengths // 2, 3 * lengths // 4 + 1).astype(jnp.int32)
    support = jnp.where(is_longest, 3 * lengths // 4, drawn_support).astype(jnp.int32)
    drawn_query = jax.random.randint(jax.random.fold_in(key, 103), (N_FSDP, NT), jnp.maximum(lengths // 8, 1), lengths - support + 1).astype(jnp.int32)
    query_rows = jnp.where(is_longest, lengths - support, drawn_query).astype(jnp.int32)
    return (starts, support, query_rows)


def draw_table_start(key, part):
    layout = table_layout(key)
    return layout[0]


def draw_support_count(key, part):
    layout = table_layout(key)
    return layout[1]


def draw_query_count(key, part):
    layout = table_layout(key)
    return layout[2]


def block_levels(rng, shape, split, low, largest):
    level = 1.0
    for dim, blocks in split:
        steps = jax.random.uniform(jax.random.fold_in(jax.random.fold_in(rng, 6), dim), (blocks,), jnp.float32, low / len(split), largest / len(split))
        level = level * jnp.repeat(jnp.exp(steps), shape[dim] // blocks).reshape((-1,) + (1,) * (len(shape) - 1 - dim))
    return level


def scatter_about(stream_key, extent, width, reach, cuts=(), kind=jnp.bfloat16):
    factor_of = block_levels(stream_key, extent, cuts, -0.22, 0.18) if cuts else 1.0
    entries = jax.random.normal(stream_key, extent, jnp.float32) * width * factor_of
    return jnp.minimum(jnp.maximum(entries, -reach), reach).astype(kind)


def setup_inputs(seed: int = 0) -> dict:
    key_list = jax.random.split(jax.random.key(seed), 19)
    return {
        "tokens": scatter_about(key_list[0], (N_FSDP, GROUP_ROWS, D), 1.0, 6.0, ((0, 2), (1, 16))),
        "w_qkv": scatter_about(key_list[1], (D, 3 * D), D ** -0.5, 0.25, ((0, 32),)),
        "w_out": scatter_about(key_list[2], (D, D), (D // 8) ** -0.5, 0.75, ((0, 32),)),
        "w_up": scatter_about(key_list[3], (D, FF), D ** -0.5, 0.25, ((0, 32),)),
        "w_down": scatter_about(key_list[4], (FF, D), FF ** -0.5, 0.125, ((0, 32),)),
        "norm1_gain": jnp.clip(1.0 + 0.18 * jax.random.normal(key_list[5], (D,), jnp.float32), 0.099609375, 1.8984375).astype(jnp.bfloat16),
        "norm1_bias": scatter_about(key_list[6], (D,), 0.3, 4.0, ((0, 32),)),
        "query_bias": scatter_about(key_list[7], (D,), 0.3, 4.0, ((0, 32),)),
        "value_bias": scatter_about(key_list[8], (D,), 0.3, 4.0, ((0, 32),)),
        "out_bias": scatter_about(key_list[9], (D,), 0.3, 4.0, ((0, 32),)),
        "norm2_gain": jnp.clip(1.0 + 0.18 * jax.random.normal(key_list[10], (D,), jnp.float32), 0.099609375, 1.8984375).astype(jnp.bfloat16),
        "norm2_bias": scatter_about(key_list[11], (D,), 0.3, 4.0, ((0, 32),)),
        "up_bias": scatter_about(key_list[12], (FF,), 0.3, 4.0, ((0, 32),)),
        "down_bias": scatter_about(key_list[13], (D,), 0.3, 4.0, ((0, 32),)),
        "cotangent": scatter_about(key_list[14], (N_FSDP, GROUP_ROWS, D), 1.0, 6.0, ((0, 2), (1, 16))),
        "table_start": draw_table_start(jax.random.fold_in(key_list[18], 71), 0),
        "support_count": draw_support_count(jax.random.fold_in(key_list[18], 71), 0),
        "query_count": draw_query_count(jax.random.fold_in(key_list[18], 71), 0),
    }


EPS = 1e-05
NEG = -1e+30

@jax.custom_vjp
def low(v):
    return lax.optimization_barrier(v.astype(jnp.bfloat16)).astype(jnp.float32)

@jax.custom_vjp
def low_back(v):
    return v

def low_keep(v):
    return (low(v), None)

def low_pass(kept, grad):
    return (grad,)

def back_keep(v):
    return (v, None)

def back_low(kept, grad):
    return (low(grad),)
low.defvjp(low_keep, low_pass)
low_back.defvjp(back_keep, back_low)

def product(left, right):
    return jnp.dot(left, right, precision=lax.Precision.HIGHEST)

def layer_norm(values, gain_vec, bias_vec):
    centre = values - lax.optimization_barrier(jnp.mean(values, axis=-1, keepdims=True))
    spread = lax.optimization_barrier(jnp.mean(centre * centre, axis=-1, keepdims=True))
    return centre * lax.rsqrt(spread + EPS) * gain_vec + bias_vec

def table_bounds(starts, support, query_rows, positions):
    inside = positions[:, None] >= starts[None, :]
    table_index = lax.optimization_barrier(jnp.sum(inside.astype(jnp.int32), axis=1)) - 1
    onehot = table_index[:, None] == jnp.arange(starts.shape[0], dtype=jnp.int32)[None, :]
    table_low = lax.optimization_barrier(jnp.sum(jnp.where(onehot, starts[None, :], 0), axis=1)).astype(jnp.int32)
    table_high = table_low + lax.optimization_barrier(jnp.sum(jnp.where(onehot, support[None, :], 0), axis=1)).astype(jnp.int32)
    finish = table_high + lax.optimization_barrier(jnp.sum(jnp.where(onehot, query_rows[None, :], 0), axis=1)).astype(jnp.int32)
    live_rows = (positions < finish).astype(jnp.float32)
    return (table_low, table_high, live_rows)

def group_forward(inputs, table_low, table_high, live_rows, params):
    w_qkv, w_out, w_up, w_down, gain_one, shift_one, bias_query, bias_value, bias_out, gain_two, shift_two, bias_up, bias_down = params
    model_width = inputs.shape[1]
    row_count = inputs.shape[0]
    score_scale = 1.0 / math.sqrt(HEAD_DIM)
    normed_in = low(layer_norm(inputs, gain_one, shift_one))
    bias_row = jnp.concatenate([bias_query, jnp.zeros_like(bias_query), bias_value])
    projected = low_back(low(product(normed_in, w_qkv) + bias_row))
    queries = projected[:, :model_width].reshape(row_count, HEADS, HEAD_DIM)
    keys = projected[:, model_width:2 * model_width].reshape(row_count, HEADS, HEAD_DIM)
    values = projected[:, 2 * model_width:].reshape(row_count, HEADS, HEAD_DIM)
    key_pos = jnp.arange(row_count, dtype=jnp.int32)
    block_rows = math.gcd(row_count, 512)

    def attend(pieces):
        query_block, low_block, high_block = pieces
        scores = jnp.einsum('qhd,khd->hqk', query_block, keys, precision=lax.Precision.HIGHEST) * score_scale
        scores = low_back(scores)
        allowed = (key_pos[None, :] >= low_block[:, None]) & (key_pos[None, :] < high_block[:, None])
        scores = jnp.where(allowed[None], scores, NEG)
        top_score = lax.optimization_barrier(jnp.max(scores, axis=-1, keepdims=True))
        exponent = jnp.exp(scores - top_score)
        soft = exponent / lax.optimization_barrier(jnp.sum(exponent, axis=-1, keepdims=True))
        soft_low = low(soft)
        mixed = jnp.einsum('hqk,khd->qhd', soft_low, values, precision=lax.Precision.HIGHEST)
        return mixed.reshape(block_rows, model_width)
    attended = lax.map(jax.checkpoint(attend), (queries.reshape(row_count // block_rows, block_rows, HEADS, HEAD_DIM), table_low.reshape(row_count // block_rows, block_rows), table_high.reshape(row_count // block_rows, block_rows)))
    attended = attended.reshape(row_count, model_width) * live_rows[:, None]
    attended = low_back(low(attended))
    branch = low_back(product(attended, w_out))
    middle = inputs + branch + bias_out
    normed_mid = low(layer_norm(middle, gain_two, shift_two))
    pre_act = low_back(product(normed_mid, w_up) + bias_up)
    hidden = low(jax.nn.gelu(pre_act))
    return middle + product(hidden, w_down) + bias_down

def reference(tokens, w_qkv, w_out, w_up, w_down, norm1_gain, norm1_bias, query_bias, value_bias, out_bias, norm2_gain, norm2_bias, up_bias, down_bias, cotangent, table_start, support_count, query_count):
    params = tuple((member.astype(jnp.float32) for member in (w_qkv, w_out, w_up, w_down, norm1_gain, norm1_bias, query_bias, value_bias, out_bias, norm2_gain, norm2_bias, up_bias, down_bias)))
    positions = jnp.arange(GROUP_ROWS, dtype=jnp.int32)
    table_low, table_high, live_rows = jax.vmap(table_bounds, in_axes=(0, 0, 0, None))(table_start, support_count, query_count, positions)

    def forward(inputs, weights):
        return lax.map(lambda pieces: group_forward(pieces[0], pieces[1], pieces[2], pieces[3], weights), (inputs, table_low, table_high, live_rows))
    outputs, pullback = jax.vjp(forward, tokens.astype(jnp.float32), params)
    grad_inputs, grad_params = pullback(cotangent.astype(jnp.float32))
    g_qkv, g_out, g_up, g_down, g_gain_one, g_shift_one, g_query, g_value, g_bias_out, g_gain_two, g_shift_two, g_bias_up, g_bias_down = grad_params
    return (outputs.astype(jnp.bfloat16), grad_inputs.astype(jnp.bfloat16), g_qkv, g_out, g_up, g_down, g_gain_one, g_shift_one, g_query, g_value, g_bias_out, g_gain_two, g_shift_two, g_bias_up, g_bias_down)
```

```python
import functools
import math

import jax
import jax.numpy as jnp
import numpy as np
from jax import lax
from jax.experimental import pallas as pl
from jax.experimental.pallas import tpu as pltpu
from jax.sharding import PartitionSpec as P

HEADS = 4
HEAD_DIM = 128
EPS = 1e-05
NEG = -1e30
PLANE = 4
MIB = 1024 * 1024
BF = jnp.bfloat16
F32 = jnp.float32
I32 = jnp.int32
SCALE = 1.0 / math.sqrt(HEAD_DIM)
SCALE2 = SCALE * math.log2(math.e)
GELU_A = math.sqrt(2.0 / math.pi)
GELU_B = 0.044715

VMEM = pl.BlockSpec(memory_space=pltpu.VMEM)
SMEM = pl.BlockSpec(memory_space=pltpu.SMEM)
ANY = pl.BlockSpec(memory_space=pl.ANY)


def mm(left, right):
    return jnp.dot(left, right, preferred_element_type=F32)


def mm_nt(left, right):
    return lax.dot_general(left, right, (((1,), (1,)), ((), ())), preferred_element_type=F32)


def mm_tn(left, right):
    return lax.dot_general(left, right, (((0,), (0,)), ((), ())), preferred_element_type=F32)


def call(body, outs, ins, in_specs, out_specs, scratch=(), flops=0, moved=0, trans=0, vmem=40, name=None):
    return pl.pallas_call(
        body,
        out_shape=outs,
        in_specs=in_specs,
        out_specs=out_specs,
        scratch_shapes=scratch,
        compiler_params=pltpu.CompilerParams(vmem_limit_bytes=vmem * MIB),
        cost_estimate=pl.CostEstimate(
            flops=int(flops), bytes_accessed=int(moved), transcendentals=int(trans)
        ),
        name=name,
    )(*ins)


def normalize(values):
    centre = values - jnp.mean(values, axis=-1, keepdims=True)
    spread = jnp.mean(centre * centre, axis=-1, keepdims=True)
    inverse = lax.rsqrt(spread + EPS)
    return centre * inverse, inverse


def norm_back(grad_out, plain, inverse, gain):
    scaled = grad_out * gain
    return inverse * (
        scaled
        - jnp.mean(scaled, axis=-1, keepdims=True)
        - plain * jnp.mean(scaled * plain, axis=-1, keepdims=True)
    )


def table_of(tab, count, pos):
    low = jnp.zeros_like(pos) + tab[0]
    high = low + tab[count]
    finish = high + tab[2 * count]
    for t in range(1, count):
        here = pos >= tab[t]
        top = tab[t] + tab[count + t]
        low = jnp.where(here, tab[t], low)
        high = jnp.where(here, top, high)
        finish = jnp.where(here, top + tab[2 * count + t], finish)
    return low, high, finish


def chip_positions(start, core, rows, shape, dim):
    spot = lax.broadcasted_iota(I32, shape, dim) + core * rows
    return start + jnp.where(spot >= 2 * rows, spot - 2 * rows, spot)


def assemble_body(idx, *refs, rows, width):
    pieces, (w_ref, row_ref, col_ref) = refs[:-3], refs[-3:]
    k = 0
    for piece in pieces:
        for j in range(piece.shape[0]):
            at = pl.ds(pl.multiple_of(idx[k] * rows, rows), rows)
            w_ref[at, :] = piece[j, :, :width]
            col_ref[at, :] = piece[j, :, width:].astype(F32)
            k += 1
    row_ref[...] = jnp.transpose(col_ref[...])[: row_ref.shape[0]]


def project_body(sc, *refs, with_q, plane):
    pieces, (w_ref, row_ref) = refs[:PLANE], refs[PLANE : PLANE + 2]
    rest = refs[PLANE + 2 :]
    if with_q:
        q_ref, kv_hbm, n_ref, kv_ref, sem = rest
    else:
        unused, kv_hbm, n_ref, kv_ref, sem = rest
    local = pieces[0].shape[0]
    first = sc[0] == 0
    gain, shift = row_ref[0:1, :], row_ref[1:2, :]
    half = row_ref.shape[1] // 2
    q_bias = jnp.where(first, row_ref[2:3, :half], row_ref[2:3, half:])
    v_bias = jnp.where(first, row_ref[3:4, :half], row_ref[3:4, half:])
    kv_bias = jnp.concatenate([jnp.zeros_like(v_bias), v_bias], axis=1)
    for i, piece in enumerate(pieces):
        plain, unused_inverse = normalize(piece[...].astype(F32))
        n_ref[i * local : (i + 1) * local, :] = plain.astype(BF)
        normed = (plain * gain + shift).astype(BF)
        kv = (mm(normed, w_ref[:, half:]) + kv_bias).astype(BF)
        kv_ref[i // 2, (i % 2) * local : (i % 2 + 1) * local, :] = kv
        if with_q and i < 2:
            q_ref[i * local : (i + 1) * local, :] = (mm(normed, w_ref[:, :half]) + q_bias).astype(BF)
    copy = pltpu.make_async_copy(kv_ref, kv_hbm.at[pl.ds(2 * plane, 2)], sem)
    copy.start()
    copy.wait()


def attend_body(sc, tab, q_ref, kv_ref, o_ref, lse_ref, keep_ref, send_ref, s_scr, m_scr, acc_scr):
    count = tab.shape[0] // 3
    core, chip = sc[0], sc[1]
    units, rows, unused_width = kv_ref.shape
    local = rows // 2
    min_low, min_high, unused_f = table_of(tab, count, chip)
    max_low, max_high, unused_f = table_of(tab, count, chip + rows - 1)
    q_pos = chip_positions(chip, core, local, (rows, 1), 0)
    low, high, finish = table_of(tab, count, q_pos)
    live = (q_pos < finish).astype(F32)
    ones = jnp.ones((rows, HEAD_DIM), BF)
    for h in range(2):
        lanes = slice(h * HEAD_DIM, (h + 1) * HEAD_DIM)
        v_lanes = slice((2 + h) * HEAD_DIM, (3 + h) * HEAD_DIM)
        q = q_ref[:, lanes]
        m_scr[...] = jnp.full(m_scr.shape, NEG, F32)
        acc_scr[...] = jnp.zeros(acc_scr.shape, F32)

        def keep_scores(u, scores):
            s_scr[u] = scores
            top = m_scr[...]
            for j in range(rows // HEAD_DIM):
                top = jnp.maximum(top, scores[:, j * HEAD_DIM : (j + 1) * HEAD_DIM])
            m_scr[...] = top

        def score_step(u, carry):
            start = sc[2 + u]
            needed = (start < max_high) & (start + rows > min_low)
            whole = (start >= max_low) & (start + rows <= min_high)

            @pl.when(needed & whole)
            def _():
                keep_scores(u, mm_nt(q, kv_ref[u, :, lanes]))

            @pl.when(needed & jnp.logical_not(whole))
            def _():
                k_pos = chip_positions(start, core, local, (1, rows), 1)
                allowed = (k_pos >= low) & (k_pos < high)
                keep_scores(u, jnp.where(allowed, mm_nt(q, kv_ref[u, :, lanes]), NEG))

            return carry

        lax.fori_loop(0, units, score_step, 0)
        top = jnp.max(m_scr[...], axis=-1, keepdims=True) * SCALE2

        def value_step(u, carry):
            start = sc[2 + u]
            needed = (start < max_high) & (start + rows > min_low)

            @pl.when(needed)
            def _():
                soft = jnp.exp2(s_scr[u] * SCALE2 - top).astype(BF)
                wide = jnp.concatenate([kv_ref[u, :, v_lanes], ones], axis=1)
                acc_scr[...] += mm(soft, wide)

            return carry

        lax.fori_loop(0, units, value_step, 0)
        total = acc_scr[:, HEAD_DIM:]
        mixed = acc_scr[:, :HEAD_DIM] / total
        o_ref[:, lanes] = mixed
        masked = (mixed * live).astype(BF)
        keep_ref[:, lanes] = masked[:local]
        send_ref[:, lanes] = masked[local:]
        log_total = jnp.transpose(top + jnp.log2(total))
        lse_ref[h] = log_total[:8]


def middle_body(
    idx, sc, tab, *refs, rows, gather_count, grad_count
):
    m_refs = refs[:gather_count]
    tok_ref, own_ref, other_ref, cot_ref, row_ref, up_row_ref = refs[gather_count : gather_count + 6]
    outs = refs[gather_count + 6 :]
    out_ref, dmid_ref, dkeep_ref, dsend_ref, vec_ref = outs[:5]
    g_refs = outs[5 : 5 + grad_count]
    (w_out, w_up, w_down, g_out, g_up, g_down, sem, g_sem) = outs[5 + grad_count :]
    pieces = w_down.shape[0] // 4
    count = tab.shape[0] // 3
    core, chip = sc[0], sc[1]
    local = tok_ref.shape[0]
    k = 0
    for m_ref in m_refs:
        for j in range(m_ref.shape[0]):
            at = pl.ds(pl.multiple_of(idx[k] * rows, rows), rows)
            pltpu.make_async_copy(m_ref.at[j, 0], w_out.at[at, :], sem.at[0]).start()
            pltpu.make_async_copy(m_ref.at[j, pl.ds(1, 4)], w_up.at[:, at, :], sem.at[1]).start()
            pltpu.make_async_copy(
                m_ref.at[j, pl.ds(5, 4)], w_down.at[pl.ds(idx[k] * 4, 4)], sem.at[2]
            ).start()
            k += 1

    pos = chip + core * local + lax.broadcasted_iota(I32, (local, 1), 0)
    unused_low, unused_high, finish = table_of(tab, count, pos)
    live = (pos < finish).astype(F32)
    gain, shift = row_ref[5:6, :], row_ref[6:7, :]
    own, other = own_ref[...], other_ref[...]
    first = core == 0
    attended = jnp.concatenate([jnp.where(first, own, other), jnp.where(first, other, own)], axis=1)
    cot = cot_ref[...]
    pltpu.make_async_copy(w_out, w_out, sem.at[0]).wait()
    middle = tok_ref[...].astype(F32) + mm(attended, w_out[...]) + row_ref[4:5, :]
    plain, inverse = normalize(middle)
    normed = (plain * gain + shift).astype(BF)
    pltpu.make_async_copy(w_up, w_up, sem.at[1]).wait()
    pltpu.make_async_copy(w_down, w_down, sem.at[2]).wait()
    total = middle + row_ref[7:8, :]
    d_norm = jnp.zeros(middle.shape, F32)
    ones = jnp.ones((local, HEAD_DIM), BF)
    lane = lax.broadcasted_iota(I32, (1, 1, HEAD_DIM), 2)
    width = w_up.shape[2]
    per = pieces // 4 if pieces > 1 else 1
    vec_ref[...] = jnp.zeros(vec_ref.shape, F32)
    for j in range(4):
        up = w_up[j]
        down = w_down[j * pieces : (j + 1) * pieces].reshape(width, width)
        pre = mm(normed, up) + up_row_ref[:, j * width : (j + 1) * width]
        square = pre * pre
        t = jnp.tanh(GELU_A * pre * (1.0 + GELU_B * square))
        half = 0.5 * (1.0 + t)
        hidden = (pre * half).astype(BF)
        slope = half + 0.5 * pre * (1.0 - t * t) * (GELU_A * (1.0 + 3.0 * GELU_B * square))
        total = total + mm(hidden, down)
        d_pre = (mm_nt(cot, down) * slope).astype(BF)
        d_norm = d_norm + mm_nt(d_pre, up)
        g_down[j * pieces : (j + 1) * pieces] = mm_tn(hidden, cot).astype(BF).reshape(pieces, rows, width)
        g_up[j] = mm_tn(normed, d_pre).astype(BF)
        columns = mm_tn(d_pre, ones)
        if pieces > 1:
            split = columns.reshape(per, 4, rows, HEAD_DIM)
            placed = sum(jnp.where(lane == 4 + i, split[:, i], 0.0) for i in range(4))
            vec_ref[j * per * rows : (j + 1) * per * rows, :] = placed.reshape(per * rows, HEAD_DIM)
        else:
            vec_ref[...] += jnp.where(lane[0] == 4 + j, columns, 0.0)
    out_ref[...] = total.astype(BF)
    cot_f = cot.astype(F32)
    d_middle = cot_f + norm_back(d_norm, plain, inverse, gain)
    dmid_ref[...] = d_middle
    d_branch = d_middle.astype(BF)
    g_out[...] = mm_tn(attended, d_branch).astype(BF)
    d_att = mm_nt(d_branch, w_out[...]).astype(BF) * live.astype(BF)
    half_width = width // 2
    left, right = d_att[:, :half_width], d_att[:, half_width:]
    dkeep_ref[...] = jnp.where(first, left, right)
    dsend_ref[...] = jnp.where(first, right, left)

    g_pieces = g_refs[0].shape[0]
    for i in range(pieces):
        where = idx[k + i]
        at = pl.ds(pl.multiple_of(where * rows, rows), rows)
        g_ref, spot = g_refs[i // g_pieces], i % g_pieces
        pltpu.make_async_copy(g_out.at[at, :], g_ref.at[spot, 0], g_sem).start()
        pltpu.make_async_copy(g_up.at[:, at, :], g_ref.at[spot, pl.ds(1, 4)], g_sem).start()
        pltpu.make_async_copy(
            g_down.at[pl.ds(where * 4, 4)], g_ref.at[spot, pl.ds(5, 4)], g_sem
        ).start()

    lane = lane[0]
    for k_lane, column in enumerate((d_middle, d_norm * plain, d_norm, cot_f)):
        high = column.astype(BF)
        low = (column - high.astype(F32)).astype(BF)
        pick = jnp.where(lane == k_lane, ones, jnp.zeros_like(ones))
        vec_ref[...] += mm_tn(high, pick) + mm_tn(low, pick)
    for g_ref in g_refs:
        pltpu.make_async_copy(g_ref, g_ref, g_sem).wait()


def back_body(
    sc, tab, q_ref, keep_ref, recv_ref, o_ref, lse_ref, kv_ref, n_ref, w_ref, dq_in, nk_in, sum_in,
    d0_ref, d1_ref, dq_ref, nk_ref, sum_ref, do_scr, delta_scr, dkv_scr, *, plane,
):
    count = tab.shape[0] // 3
    core, chip = sc[0], sc[1]
    unused_units, rows, unused_width = kv_ref.shape
    local = rows // 2
    half = q_ref.shape[1]
    min_low, min_high, unused_f = table_of(tab, count, chip)
    max_low, max_high, unused_f = table_of(tab, count, chip + rows - 1)
    q_pos = chip_positions(chip, core, local, (1, rows), 1)
    low, high, unused_f = table_of(tab, count, q_pos)
    do_scr[:local] = keep_ref[...]
    do_scr[local:] = recv_ref[...]
    dq_ref[...] = dq_in[...]
    for h in range(2):
        lanes = slice(h * HEAD_DIM, (h + 1) * HEAD_DIM)
        product = jnp.transpose(do_scr[:, lanes].astype(F32) * o_ref[:, lanes])
        delta_scr[h] = jnp.broadcast_to(jnp.sum(product, axis=0, keepdims=True), (8, rows))

    def head(u, h, masked, start):
        lanes = slice(h * HEAD_DIM, (h + 1) * HEAD_DIM)
        v_lanes = slice((2 + h) * HEAD_DIM, (3 + h) * HEAD_DIM)
        q, do, key = q_ref[:, lanes], do_scr[:, lanes], kv_ref[u, :, lanes]
        soft = jnp.exp2(mm_nt(key, q) * SCALE2 - lse_ref[h, 0:1, :])
        if masked:
            k_pos = chip_positions(start, core, local, (rows, 1), 0)
            soft = jnp.where((k_pos >= low) & (k_pos < high), soft, 0.0)
        d_soft = mm_nt(kv_ref[u, :, v_lanes], do)
        d_scores = (soft * (d_soft - delta_scr[h, 0:1, :])).astype(BF)
        dkv_scr[u, :, v_lanes] = mm(soft.astype(BF), do).astype(BF)
        dkv_scr[u, :, lanes] = (mm(d_scores, q) * SCALE).astype(BF)
        dq_ref[:, lanes] += mm_tn(d_scores, key)

    def unit_step(u, carry):
        start = sc[2 + 2 * plane + u]
        needed = (start < max_high) & (start + rows > min_low)
        whole = (start >= max_low) & (start + rows <= min_high)

        @pl.when(needed & whole)
        def _():
            head(u, 0, False, start)
            head(u, 1, False, start)

        @pl.when(needed & jnp.logical_not(whole))
        def _():
            head(u, 0, True, start)
            head(u, 1, True, start)

        @pl.when(jnp.logical_not(needed))
        def _():
            dkv_scr[u] = jnp.zeros(dkv_scr.shape[1:], BF)

        return carry

    lax.fori_loop(0, 2, unit_step, 0)
    ones = jnp.ones((8, rows), BF)
    sums = sum_in[...]
    products = nk_in[...]
    for u in range(2):
        dkv = dkv_scr[u]
        d_normed = mm_nt(dkv, w_ref[:, half:])
        if plane == 0 and u == 0:
            d_normed += mm_nt((dq_ref[...] * SCALE).astype(BF), w_ref[:, :half])
        d_normed = d_normed.astype(BF)
        d0_ref[u] = d_normed[:local]
        d1_ref[u] = d_normed[local:]
        products += mm_tn(n_ref[u * rows : (u + 1) * rows, :], dkv)
        sums += mm(ones, dkv)
    nk_ref[...] = products
    sum_ref[...] = sums


def message_body(idx, sc, n_ref, dq_ref, nk_ref, sum_ref, w_ref, col_ref, vec_ref, msg_ref, full, vec, *, rows):
    half = dq_ref.shape[1]
    width = w_ref.shape[1]
    d_query = (dq_ref[...] * SCALE).astype(BF)
    q_sums = mm(jnp.ones((8, d_query.shape[0]), BF), d_query)
    q_product = mm_tn(n_ref[: d_query.shape[0], :], d_query)
    product = jnp.concatenate([q_product, nk_ref[...]], axis=1)
    sums = jnp.concatenate([q_sums[0:1], sum_ref[0:1]], axis=1)
    gain, shift = col_ref[:, 0:1], col_ref[:, 1:2]
    weight = w_ref[...].astype(F32)
    full[:, :width] = (product * gain + shift * sums).astype(BF)
    lane = lax.broadcasted_iota(I32, (1, HEAD_DIM), 1)
    gain_grad = jnp.sum(product * weight, axis=-1, keepdims=True)
    shift_grad = jnp.sum(weight * sums, axis=-1, keepdims=True)
    vec[...] = (
        vec_ref[...] + jnp.where(lane == 8, gain_grad, 0.0) + jnp.where(lane == 9, shift_grad, 0.0)
    )
    q_column = jnp.transpose(jnp.broadcast_to(sums[:, :half], (HEAD_DIM, half)))
    v_column = jnp.transpose(jnp.broadcast_to(sums[:, 2 * half :], (HEAD_DIM, half)))
    mine = pl.ds(pl.multiple_of(sc[0] * half, half), half)
    vec[mine, :] += jnp.where(lane == 10, q_column, 0.0) + jnp.where(lane == 11, v_column, 0.0)
    full[:, width:] = vec[...].astype(BF)
    for i in range(msg_ref.shape[0]):
        msg_ref[i] = full[pl.ds(pl.multiple_of(idx[i] * rows, rows), rows), :]


def finish_body(tok_ref, dmid_ref, row_ref, *refs):
    plain, inverse = normalize(tok_ref[...].astype(F32))
    total = refs[0][...].astype(F32)
    for ref in refs[1:-1]:
        total = total + ref[...].astype(F32)
    refs[-1][...] = (dmid_ref[...] + norm_back(total, plain, inverse, row_ref[0:1, :])).astype(BF)


def shards(
    tokens, w_qkv, w_out, w_up, w_down,
    norm1_gain, norm1_bias, query_bias, value_bias, out_bias, norm2_gain, norm2_bias, up_bias, down_bias,
    cotangent, table_start, support_count, query_count, *, R, F,
):
    A = R // PLANE
    count = R * F
    local, width = tokens.shape[1], tokens.shape[2]
    half = width // 2
    part = w_qkv.shape[0]
    hidden = w_up.shape[1]
    blocks = hidden // width
    aligned = part % 16 == 0
    rows = part if aligned else width
    sds = jax.ShapeDtypeStruct

    r, f = lax.axis_index("rows"), lax.axis_index("fsdp")
    a, x, c = r // PLANE, (r // 2) % 2, r % 2

    def swap_c(v):
        return lax.ppermute(v, "rows", [(i, i ^ 1) for i in range(R)])

    def swap_x(v):
        return lax.ppermute(v, "rows", [(i, i ^ 2) for i in range(R)])

    def turn_a(v, s):
        return lax.ppermute(
            v, "rows", [(i, ((i // PLANE + s) % A) * PLANE + i % PLANE) for i in range(R)]
        )

    def turn_f(v, t):
        return lax.ppermute(v, "fsdp", [(i, (i + t) % F) for i in range(F)])

    def owners(order):
        cr, t, xr, s = (np.array(list(z), np.int32) for z in zip(*order, strict=True))
        plane = lax.rem(a - s + A, A)
        return (((plane * 2 + (x ^ xr)) * 2 + (c ^ cr)) * F + lax.rem(f - t + F, F)).astype(I32)

    unit_s = np.repeat(np.arange(A), 2).astype(np.int32)
    unit_x = np.tile(np.arange(2), A).astype(np.int32)
    unit_start = (lax.rem(a - unit_s + A, A) * 2 + (x ^ unit_x)) * (2 * local)
    sc = jnp.concatenate([jnp.stack([c, (a * 2 + x) * 2 * local]), unit_start]).astype(I32)
    tab = jnp.concatenate([table_start[0], support_count[0], query_count[0]])

    vectors = jnp.stack(
        [norm1_gain, norm1_bias, query_bias, value_bias, out_bias, norm2_gain, norm2_bias, down_bias], axis=1
    )
    vectors = jnp.concatenate([vectors, up_bias.reshape(blocks, part).T], axis=1)
    vectors = jnp.pad(vectors, ((0, 0), (0, HEAD_DIM - vectors.shape[1])))
    by_core = w_qkv.reshape(part, 3, 2, half)
    pack = [
        jnp.concatenate(
            [lax.dynamic_index_in_dim(by_core, which, 2, keepdims=False).reshape(part, 3 * half), vectors], axis=1
        )
        for which in (c, 1 - c)
    ]
    q_mine = jnp.stack([pack[0], swap_c(pack[1])])
    q_z = jnp.stack([q_mine] + [turn_a(q_mine, s) for s in range(1, A)])
    q_zx = [q_z, swap_x(q_z)]
    q_all = [[q_zx[xr] if t == 0 else turn_f(q_zx[xr], t) for xr in range(2)] for t in range(F)]
    q_order = [(cr, t, xr, s) for t in range(F) for xr in range(2) for s in range(A) for cr in range(2)]
    q_idx = owners(q_order)
    wide = 3 * half + HEAD_DIM
    q_pieces = [q_all[t][xr].reshape(A * 2, part, wide) for t in range(F) for xr in range(2)]
    if not aligned:
        stacked = jnp.concatenate(q_pieces)
        q_pieces = [jnp.zeros_like(stacked).at[q_idx].set(stacked).reshape(1, width, wide)]
        q_idx = jnp.zeros((1,), I32)

    own = tokens[0]
    tok_z = [own] + [None] * (A - 1)
    near = sorted(range(1, A), key=lambda s: min(s, A - s))
    for s in near:
        tok_z[s] = turn_a(own, s)
    order = [0] + near
    tok_x = {s: swap_x(tok_z[s]) for s in order}
    tok = {s: [tok_z[s], swap_c(tok_z[s]), tok_x[s], swap_c(tok_x[s])] for s in order}

    w_mine, row_vec, col_vec = call(
        functools.partial(assemble_body, rows=rows, width=3 * half),
        [sds((width, 3 * half), BF), sds((16, width), F32), sds((width, HEAD_DIM), F32)],
        [q_idx, *q_pieces], [SMEM] + [VMEM] * len(q_pieces), [VMEM] * 3,
        flops=0, moved=4 * width * wide, name="assemble",
    )
    up_row = row_vec[8 : 8 + blocks].reshape(blocks, count, part).transpose(1, 0, 2).reshape(1, hidden)

    m_own = jnp.concatenate(
        [
            w_out[None],
            w_up.reshape(part, blocks, width).transpose(1, 0, 2),
            w_down.reshape(blocks, part, width),
        ]
    )
    m_z = {0: m_own}
    for s in near:
        m_z[s] = turn_a(m_own, s)
    m_arrays, m_order = [], []
    for s in order:
        pair = jnp.stack([m_z[s], swap_x(m_z[s])])
        for t in range(F):
            pair_t = pair if t == 0 else turn_f(pair, t)
            for cr in range(2):
                m_arrays.append(pair_t if cr == 0 else swap_c(pair_t))
                m_order += [(cr, t, xr, s) for xr in range(2)]
    m_idx = owners(m_order)
    if not aligned:
        stacked = jnp.concatenate(m_arrays)
        by_owner = jnp.zeros_like(stacked).at[m_idx].set(stacked)
        m_arrays = [
            jnp.concatenate(
                [
                    by_owner[:, 0].reshape(1, width, width),
                    by_owner[:, 1 : 1 + blocks].transpose(1, 0, 2, 3).reshape(blocks, width, width),
                    by_owner[:, 1 + blocks :].reshape(blocks, width, width),
                ]
            )[None]
        ]
        m_idx = jnp.zeros((1,), I32)
    g_order = [(cr, t, xr, s) for cr in range(2) for t in range(F) for xr in range(2) for s in range(A)]
    g_owner = owners(g_order)

    kv, n_rows, q = None, {}, None
    plane_rows = PLANE * local
    for s in order:
        with_q = s == 0
        outs = [sds((2 * A, 2 * local, width), BF), sds((plane_rows, width), BF)]
        out_specs = [ANY, VMEM]
        if with_q:
            outs, out_specs = [sds((2 * local, half), BF)] + outs, [VMEM] + out_specs
        ins = [sc, *tok[s], w_mine, row_vec] + ([] if with_q else [kv])
        got = pl.pallas_call(
            functools.partial(project_body, with_q=with_q, plane=s),
            out_shape=outs,
            in_specs=[SMEM] + [VMEM] * (PLANE + 2) + ([] if with_q else [ANY]),
            out_specs=out_specs,
            scratch_shapes=[pltpu.VMEM((2, 2 * local, width), BF), pltpu.SemaphoreType.DMA],
            input_output_aliases={} if with_q else {PLANE + 3: 0},
            compiler_params=pltpu.CompilerParams(vmem_limit_bytes=32 * MIB),
            cost_estimate=pl.CostEstimate(
                flops=2 * plane_rows * width * width, bytes_accessed=6 * plane_rows * width, transcendentals=0
            ),
            name="project",
        )(*ins)
        if with_q:
            q, kv, n_rows[s] = got
        else:
            kv, n_rows[s] = got

    unit = 2 * local
    work = 2 * unit * A * unit * HEAD_DIM * 2 * 2
    mixed, lse, att_keep, att_send = call(
        attend_body,
        [sds((unit, half), F32), sds((2, 8, unit), F32), sds((local, half), BF), sds((local, half), BF)],
        [sc, tab, q, kv], [SMEM, SMEM, VMEM, VMEM], [VMEM] * 4,
        scratch=[
            pltpu.VMEM((2 * A, unit, unit), F32), pltpu.VMEM((unit, HEAD_DIM), F32),
            pltpu.VMEM((unit, 2 * HEAD_DIM), F32),
        ],
        flops=2 * work, moved=2 * kv.size, trans=2 * unit * 2 * A * unit, name="attend",
    )
    att_other = swap_c(att_send)

    pieces = count if aligned else 1
    grad_count = 2 if aligned else 1
    g_shape = sds((pieces // grad_count, 1 + 2 * blocks, rows, width), BF)
    idx = jnp.concatenate([m_idx, g_owner if aligned else jnp.zeros((1,), I32)])
    got = call(
        functools.partial(middle_body, rows=rows, gather_count=len(m_arrays), grad_count=grad_count),
        [
            sds((local, width), BF), sds((local, width), F32), sds((local, half), BF), sds((local, half), BF),
            sds((width, HEAD_DIM), F32),
        ] + [g_shape] * grad_count,
        [idx, sc, tab, *m_arrays, own, att_keep, att_other, cotangent[0], row_vec, up_row],
        [SMEM] * 3 + [ANY] * len(m_arrays) + [VMEM] * 6,
        [VMEM] * 5 + [ANY] * grad_count,
        scratch=[
            pltpu.VMEM((width, width), BF), pltpu.VMEM((blocks, width, width), BF),
            pltpu.VMEM((pieces * blocks, rows, width), BF),
            pltpu.VMEM((width, width), BF), pltpu.VMEM((blocks, width, width), BF),
            pltpu.VMEM((pieces * blocks, rows, width), BF),
            pltpu.SemaphoreType.DMA((3,)), pltpu.SemaphoreType.DMA,
        ],
        flops=6 * local * width * width * (1 + 2 * blocks), moved=4 * width * width * (1 + 2 * blocks),
        trans=local * hidden, name="middle",
    )
    outputs, d_middle, d_keep, d_send, vec = got[:5]
    grads = got[5:]
    d_other = swap_c(d_send)

    lead = (F, 2, A, 1 + 2 * blocks, part, width)
    if aligned:
        g_near, g_far = grads[0].reshape(lead), swap_c(grads[1]).reshape(lead)
    else:
        whole = grads[0][0]
        by_owner = jnp.concatenate(
            [
                whole[0].reshape(count, 1, part, width),
                whole[1 : 1 + blocks].reshape(blocks, count, part, width).transpose(1, 0, 2, 3),
                whole[1 + blocks :].reshape(count, blocks, part, width),
            ],
            axis=1,
        )
        relative = by_owner[g_owner].reshape((2,) + lead)
        g_near, g_far = relative[0], swap_c(relative[1])

    def total(*terms):
        out = terms[0].astype(F32)
        for term in terms[1:]:
            out = out + term.astype(F32)
        return out

    g_y = {}
    for xr in (1, 0):
        g_y[xr] = [turn_f(total(g_near[t, xr], g_far[t, xr]).astype(BF), F - t) for t in range(1, F)]
    g_x = swap_x(total(g_near[0, 1], g_far[0, 1], *g_y[1]).astype(BF))
    g_own = [g_near[0, 0], g_far[0, 0], *g_y[0], g_x]
    g_z = [turn_a(total(*(v[s] for v in g_own)).astype(BF), A - s) for s in near]
    g_sum = total(*(v[0] for v in g_own), *g_z)

    d_query = jnp.zeros((unit, half), F32)
    n_product = jnp.zeros((width, width), F32)
    sums = jnp.zeros((8, width), F32)
    d_in_pieces = []
    for s in near[::-1] + [0]:
        d_near, d_far, d_query, n_product, sums = pl.pallas_call(
            functools.partial(back_body, plane=s),
            grid=(1,),
            out_shape=[
                sds((2, local, width), BF), sds((2, local, width), BF), sds((unit, half), F32),
                sds((width, width), F32), sds((8, width), F32),
            ],
            in_specs=[SMEM, SMEM] + [VMEM] * 5
            + [pl.BlockSpec((2, unit, width), lambda i, s=s: (s, 0, 0))] + [VMEM] * 5,
            out_specs=[VMEM] * 5,
            scratch_shapes=[
                pltpu.VMEM((unit, half), BF), pltpu.VMEM((2, 8, unit), F32), pltpu.VMEM((2, unit, width), BF),
            ],
            compiler_params=pltpu.CompilerParams(vmem_limit_bytes=40 * MIB),
            cost_estimate=pl.CostEstimate(
                flops=work // A * 5 // 2 + 4 * plane_rows * width * width,
                bytes_accessed=12 * plane_rows * width, transcendentals=4 * unit * unit,
            ),
            name="back",
        )(sc, tab, q, d_keep, d_other, mixed, lse, kv, n_rows[s], w_mine, d_query, n_product, sums)
        d_far = swap_c(d_far)
        d_x = swap_x(total(d_near[1], d_far[1]).astype(BF))
        d_sum = total(d_near[0], d_far[0], d_x).astype(BF)
        d_in_pieces.append(d_sum if s == 0 else turn_a(d_sum, A - s))

    if aligned:
        msg_idx = owners(q_order)
    else:
        msg_idx = jnp.zeros((1,), I32)
    message = call(
        functools.partial(message_body, rows=rows),
        sds((pieces, rows, wide), BF),
        [msg_idx, sc, n_rows[0], d_query, n_product, sums, w_mine, col_vec, vec],
        [SMEM, SMEM] + [VMEM] * 7, VMEM,
        scratch=[pltpu.VMEM((width, wide), BF), pltpu.VMEM((width, HEAD_DIM), F32)],
        flops=2 * unit * half * width, moved=8 * width * wide, name="message",
    )
    if not aligned:
        flat = message[0]
        up_part = flat[:, 3 * half + 4 : 3 * half + 4 + blocks].T.reshape(count, blocks, part)
        by_owner = flat.reshape(count, part, wide)
        by_owner = by_owner.at[:, :, 3 * half + 4 : 3 * half + 4 + blocks].set(up_part.transpose(0, 2, 1))
        message = by_owner[owners(q_order)]
    message = message.reshape(F, 2, A, 2, part, wide)
    w_y = [turn_f(message[t], F - t) for t in range(1, F)]
    w_x = swap_x(total(message[0, 1], *(v[1] for v in w_y)).astype(BF))
    w_own = [message[0, 0], *(v[0] for v in w_y), w_x]
    w_z = [turn_a(total(*(v[s] for v in w_own)).astype(BF), A - s) for s in near]
    w_sum = total(*(v[0] for v in w_own), *w_z)
    w_far = swap_c(w_sum[1])
    mine, theirs = (v[:, : 3 * half].reshape(part, 3, half) for v in (w_sum[0], w_far))
    grad_qkv = jnp.where(
        c == 0, jnp.concatenate([mine, theirs], axis=2), jnp.concatenate([theirs, mine], axis=2)
    ).reshape(part, 3 * width)
    last = w_sum[0][:, 3 * half :] + w_far[:, 3 * half :]

    grad_tokens = call(
        finish_body, sds((local, width), BF), [own, d_middle, row_vec, *d_in_pieces],
        [VMEM] * (3 + A), VMEM, flops=20 * local * width, moved=16 * local * width, name="finish",
    )
    return (
        outputs[None],
        grad_tokens[None],
        grad_qkv,
        g_sum[0],
        g_sum[1 : 1 + blocks].transpose(1, 0, 2).reshape(part, hidden),
        g_sum[1 + blocks :].reshape(blocks * part, width),
        last[:, 8],
        last[:, 9],
        last[:, 10],
        last[:, 11],
        last[:, 0],
        last[:, 1],
        last[:, 2],
        last[:, 4 : 4 + blocks].T.reshape(blocks * part),
        last[:, 3],
    )


def solution(mesh):
    both = ("rows", "fsdp")
    matrix, vector, act, table = P(both, None), P(both), P("fsdp", "rows", None), P("fsdp", None)
    return jax.shard_map(
        functools.partial(shards, R=mesh.shape["rows"], F=mesh.shape["fsdp"]),
        mesh=mesh,
        in_specs=(act,) + (matrix,) * 4 + (vector,) * 9 + (act,) + (table,) * 3,
        out_specs=(act, act) + (matrix,) * 4 + (vector,) * 9,
        check_vma=False,
    )
```

```python
import functools
import math

import jax
import jax.numpy as jnp
import numpy as np
from jax import lax
from jax.experimental import pallas as pl
from jax.experimental.pallas import tpu as pltpu
from jax.sharding import PartitionSpec as P

HEADS = 4
HEAD_DIM = 128
EPS = 1e-05
NEG = -1e30
PLANE = 4
MIB = 1024 * 1024
BF = jnp.bfloat16
F32 = jnp.float32
I32 = jnp.int32
SCALE = 1.0 / math.sqrt(HEAD_DIM)
SCALE2 = SCALE * math.log2(math.e)
GELU_A = math.sqrt(2.0 / math.pi)
GELU_B = 0.044715

VMEM = pl.BlockSpec(memory_space=pltpu.VMEM)
SMEM = pl.BlockSpec(memory_space=pltpu.SMEM)
HBM = pl.BlockSpec(memory_space=pltpu.HBM)


def after(value, *others):
    return lax.optimization_barrier((value, *others))[0]


def together(*values):
    return lax.optimization_barrier(values)


def mm(left, right):
    return jnp.dot(left, right, preferred_element_type=F32)


def mm_nt(left, right):
    return lax.dot_general(left, right, (((1,), (1,)), ((), ())), preferred_element_type=F32)


def mm_tn(left, right):
    return lax.dot_general(left, right, (((0,), (0,)), ((), ())), preferred_element_type=F32)


def call(body, outs, ins, in_specs, out_specs, scratch=(), flops=0, moved=0, trans=0, vmem=16, name=None):
    return pl.pallas_call(
        body,
        out_shape=outs,
        in_specs=in_specs,
        out_specs=out_specs,
        scratch_shapes=scratch,
        compiler_params=pltpu.CompilerParams(vmem_limit_bytes=vmem * MIB),
        cost_estimate=pl.CostEstimate(
            flops=int(flops), bytes_accessed=int(moved), transcendentals=int(trans)
        ),
        name=name,
    )(*ins)


def normalize(values):
    centre = values - jnp.mean(values, axis=-1, keepdims=True)
    spread = jnp.mean(centre * centre, axis=-1, keepdims=True)
    inverse = lax.rsqrt(spread + EPS)
    return centre * inverse, inverse


def norm_back(grad_out, plain, inverse, gain):
    scaled = grad_out * gain
    return inverse * (
        scaled
        - jnp.mean(scaled, axis=-1, keepdims=True)
        - plain * jnp.mean(scaled * plain, axis=-1, keepdims=True)
    )


def table_of(tab, count, pos):
    low = jnp.zeros_like(pos) + tab[0]
    high = low + tab[count]
    finish = high + tab[2 * count]
    for t in range(1, count):
        here = pos >= tab[t]
        top = tab[t] + tab[count + t]
        low = jnp.where(here, tab[t], low)
        high = jnp.where(here, top, high)
        finish = jnp.where(here, top + tab[2 * count + t], finish)
    return low, high, finish


def pack_body(qkv_ref, out_ref, up_ref, down_ref, *refs):
    vec_refs, (q_ref, m_ref, vec_scr) = refs[:-3], refs[-3:]
    part, width = out_ref.shape
    blocks = up_ref.shape[1] // width
    vec_scr[...] = jnp.zeros(vec_scr.shape, F32)
    for k, ref in enumerate(vec_refs[:-1]):
        vec_scr[k : k + 1, :part] = ref[...].astype(F32)
    for j in range(blocks):
        vec_scr[8 + j : 9 + j, :part] = vec_refs[-1][:, j * part : (j + 1) * part].astype(F32)
    for i in range(3):
        q_ref[i] = qkv_ref[:, i * width : (i + 1) * width]
    q_ref[3] = jnp.zeros((part, width), BF)
    q_ref[3, :, :HEAD_DIM] = jnp.transpose(vec_scr[...])[:part].astype(BF)
    m_ref[0] = out_ref[...]
    for j in range(blocks):
        m_ref[1 + j] = up_ref[:, j * width : (j + 1) * width]
        m_ref[1 + blocks + j] = down_ref[j * part : (j + 1) * part, :]


def sum_body(*refs, plan, count):
    for out_ref, terms in zip(refs[count:], plan, strict=True):
        total = None
        for which, spot in terms:
            term = refs[which][spot].astype(F32)
            total = term if total is None else total + term
        out_ref[...] = total.astype(out_ref.dtype)


def add_up(arrays, plan, dtype=BF):
    outs = []
    for terms in plan:
        which, spot = terms[0]
        outs.append(jax.ShapeDtypeStruct(jax.eval_shape(lambda v: v[spot], arrays[which]).shape, dtype))
    moved = sum(o.size for o in outs) * 4
    return call(
        functools.partial(sum_body, plan=plan, count=len(arrays)), outs, arrays,
        [VMEM] * len(arrays), [VMEM] * len(outs), flops=moved, moved=moved, vmem=16, name="add",
    )


def assemble_body(idx, *refs, rows, count):
    pieces, (w_ref, row_ref, col_ref, low_scr, sem) = refs[:count], refs[count:]
    k = 0
    for piece in pieces:
        for j in range(piece.shape[0]):
            at = pl.ds(pl.multiple_of(idx[k] * rows, rows), rows)
            pltpu.make_async_copy(piece.at[j, pl.ds(0, 3)], w_ref.at[:, at, :], sem.at[0]).start()
            pltpu.make_async_copy(piece.at[j, 3, :, pl.ds(0, HEAD_DIM)], low_scr.at[at, :], sem.at[1]).start()
            k += 1
    pltpu.make_async_copy(low_scr, low_scr, sem.at[1]).wait()
    columns = low_scr[...].astype(F32)
    col_ref[...] = columns
    row_ref[...] = jnp.transpose(columns)[: row_ref.shape[0]]
    pltpu.make_async_copy(w_ref, w_ref, sem.at[0]).wait()


def project_body(*refs, with_q, spots, count):
    pieces, (w_ref, row_ref), outs = refs[:count], refs[count : count + 2], refs[count + 2 :]
    gain, shift = row_ref[0:1, :], row_ref[1:2, :]
    for i, (which, lead) in enumerate(spots):
        kv_ref, n_ref = outs[2 * (i // 2)], outs[2 * (i // 2) + 1]
        plain, unused_inverse = normalize(pieces[which][lead].astype(F32))
        n_ref[i % 2] = plain.astype(BF)
        normed = (plain * gain + shift).astype(BF)
        keys = mm(normed, w_ref[1])
        values = mm(normed, w_ref[2]) + row_ref[3:4, :]
        for h in range(HEADS):
            lanes = slice(h * HEAD_DIM, (h + 1) * HEAD_DIM)
            kv_ref[i % 2, h] = keys[:, lanes].astype(BF)
            kv_ref[i % 2, HEADS + h] = values[:, lanes].astype(BF)
        if with_q and i == 0:
            queries = (mm(normed, w_ref[0]) + row_ref[2:3, :]) * SCALE2
            for h in range(HEADS):
                outs[2][h] = queries[:, h * HEAD_DIM : (h + 1) * HEAD_DIM].astype(BF)


def reach(sc, tab, rows):
    count = tab.shape[0] // 3
    min_low, min_high, unused = table_of(tab, count, sc[1])
    max_low, max_high, unused = table_of(tab, count, sc[1] + 2 * rows - 1)
    return min_low, max_high, max_low, min_high


def chip_rows(sc, rows, shape, dim):
    spot = lax.broadcasted_iota(I32, shape, dim) + sc[0] * rows
    return sc[1] + jnp.where(spot >= 2 * rows, spot - 2 * rows, spot)


def attend_body(sc, tab, q_own, q_other, *refs):
    kv_refs, (keep_ref, send_ref, q_scr, s_scr, m_scr, acc_scr, kv_ref, sem) = refs[:-8], refs[-8:]
    count = tab.shape[0] // 3
    units, unused, rows, unused = kv_ref.shape
    for i, ref in enumerate(kv_refs):
        pltpu.make_async_copy(ref, kv_ref.at[pl.ds(2 * i, 2)], sem.at[i]).start()
    min_low, max_high, max_low, min_high = reach(sc, tab, rows)
    q_pos = chip_rows(sc, rows, (2 * rows, 1), 0)
    low, high, unused = table_of(tab, count, q_pos)
    ones = jnp.ones((rows, HEAD_DIM), BF)
    q_scr[:, :rows] = q_own[...]
    q_scr[:, rows:] = q_other[...]
    m_scr[...] = jnp.full(m_scr.shape, NEG, F32)
    acc_scr[...] = jnp.zeros(acc_scr.shape, F32)

    def keep_scores(u, allowed):
        for h in range(HEADS):
            scores = mm_nt(q_scr[h], kv_ref[u, h])
            if allowed is not None:
                scores = jnp.where(allowed, scores, NEG)
            s_scr[u, h] = scores
            top = m_scr[h]
            for j in range(rows // HEAD_DIM):
                top = jnp.maximum(top, scores[:, j * HEAD_DIM : (j + 1) * HEAD_DIM])
            m_scr[h] = top

    def score_step(u, carry):
        start = sc[2 + u]

        @pl.when(u % 2 == 0)
        def _():
            pltpu.make_async_copy(kv_refs[0], kv_ref.at[pl.ds(u, 2)], sem.at[u // 2]).wait()

        needed = (start < max_high) & (start + rows > min_low)
        whole = (start >= max_low) & (start + rows <= min_high)

        @pl.when(needed & whole)
        def _():
            keep_scores(u, None)

        @pl.when(needed & jnp.logical_not(whole))
        def _():
            k_pos = start + lax.broadcasted_iota(I32, (1, rows), 1)
            keep_scores(u, (k_pos >= low) & (k_pos < high))

        return carry

    lax.fori_loop(0, units, score_step, 0)
    for h in range(HEADS):
        top = jnp.max(m_scr[h], axis=-1, keepdims=True)
        m_scr[h] = jnp.broadcast_to(jnp.where(top > 0.5 * NEG, top, 0.0), m_scr.shape[1:])

    def value_step(u, carry):
        start = sc[2 + u]
        needed = (start < max_high) & (start + rows > min_low)

        @pl.when(needed)
        def _():
            for h in range(HEADS):
                soft = jnp.exp2(s_scr[u, h] - m_scr[h][:, :1]).astype(BF)
                wide = jnp.concatenate([kv_ref[u, HEADS + h], ones], axis=1)
                acc_scr[h] += mm(soft, wide)

        return carry

    lax.fori_loop(0, units, value_step, 0)
    lane = lax.broadcasted_iota(I32, (1, HEAD_DIM), 1)
    width = HEADS * HEAD_DIM
    mine = jnp.zeros((rows, HEAD_DIM), F32)
    theirs = mine
    for h in range(HEADS):
        lanes = slice(h * HEAD_DIM, (h + 1) * HEAD_DIM)
        total = acc_scr[h, :, HEAD_DIM:]
        some = total > 0.0
        mixed = acc_scr[h, :, :HEAD_DIM] / jnp.where(some, total, 1.0)
        log_total = jnp.where(some, m_scr[h] + jnp.log2(jnp.where(some, total, 1.0)), NEG)
        keep_ref[:, lanes] = mixed[:rows]
        send_ref[:, lanes] = mixed[rows:]
        mine = jnp.where(lane == h, log_total[:rows], jnp.where(lane == HEADS + h, log_total[rows:], mine))
        theirs = jnp.where(lane == h, log_total[rows:], jnp.where(lane == HEADS + h, log_total[:rows], theirs))
    keep_ref[:, width:] = mine
    send_ref[:, width:] = theirs


def middle_body(idx, sc, tab, *refs, rows, m_count, grad_count):
    m_refs, (tok_ref, own_ref, other_ref, cot_ref, row_ref, up_row_ref) = refs[:m_count], refs[m_count : m_count + 6]
    outs = refs[m_count + 6 :]
    out_ref, dmid_ref, d_ref, lse_ref, vec_ref = outs[:5]
    g_refs = outs[5 : 5 + grad_count]
    (w_out, w_up, w_down, g_out, g_up, g_down, sem, g_sem) = outs[5 + grad_count :]
    blocks, width = w_up.shape[0], w_up.shape[2]
    pieces = w_down.shape[0] // blocks
    count = tab.shape[0] // 3
    local = tok_ref.shape[0]
    for k in range(pieces):
        m_ref, spot = m_refs[k // m_refs[0].shape[0]], k % m_refs[0].shape[0]
        at = pl.ds(pl.multiple_of(idx[k] * rows, rows), rows)
        pltpu.make_async_copy(m_ref.at[spot, 0], w_out.at[at, :], sem.at[0]).start()
        pltpu.make_async_copy(m_ref.at[spot, pl.ds(1, blocks)], w_up.at[:, at, :], sem.at[1]).start()
        pltpu.make_async_copy(
            m_ref.at[spot, pl.ds(1 + blocks, blocks)], w_down.at[pl.ds(idx[k] * blocks, blocks)], sem.at[2]
        ).start()

    pos = sc[1] + sc[0] * local + lax.broadcasted_iota(I32, (local, 1), 0)
    unused_low, unused_high, finish = table_of(tab, count, pos)
    live = (pos < finish).astype(F32)
    gain, shift = row_ref[5:6, :], row_ref[6:7, :]
    lane = lax.broadcasted_iota(I32, (1, HEAD_DIM), 1)
    lse_own, lse_other = own_ref[:, width:], other_ref[:, width:]
    top = jnp.maximum(lse_own, lse_other)
    share_own, share_other = jnp.exp2(lse_own - top), jnp.exp2(lse_other - top)
    share = share_own + share_other
    log_total = jnp.transpose(top + jnp.log2(share))
    lse_ref[...] = jnp.concatenate([log_total[:HEADS], log_total[HEADS : 2 * HEADS]], axis=1)
    share_own, share_other = share_own / share, share_other / share
    mixed = []
    for h in range(HEADS):
        lanes = slice(h * HEAD_DIM, (h + 1) * HEAD_DIM)
        mixed.append(own_ref[:, lanes] * share_own[:, h : h + 1] + other_ref[:, lanes] * share_other[:, h : h + 1])
    mixed = jnp.concatenate(mixed, axis=1)
    attended = (mixed * live).astype(BF)
    cot = cot_ref[...]
    pltpu.make_async_copy(w_out, w_out, sem.at[0]).wait()
    middle = tok_ref[...].astype(F32) + mm(attended, w_out[...]) + row_ref[4:5, :]
    plain, inverse = normalize(middle)
    normed = (plain * gain + shift).astype(BF)
    pltpu.make_async_copy(w_up, w_up, sem.at[1]).wait()
    pltpu.make_async_copy(w_down, w_down, sem.at[2]).wait()
    total = middle + row_ref[7:8, :]
    d_norm = jnp.zeros(middle.shape, F32)
    ones = jnp.ones((8, local), BF)
    up_sums = []
    for j in range(blocks):
        up = w_up[j]
        down = w_down[j * pieces : (j + 1) * pieces].reshape(width, width)
        pre = mm(normed, up) + up_row_ref[:, j * width : (j + 1) * width]
        square = pre * pre
        t = jnp.tanh(GELU_A * pre * (1.0 + GELU_B * square))
        half = 0.5 * (1.0 + t)
        hidden = (pre * half).astype(BF)
        slope = half + 0.5 * pre * (1.0 - t * t) * (GELU_A * (1.0 + 3.0 * GELU_B * square))
        total = total + mm(hidden, down)
        d_pre = (mm_nt(cot, down) * slope).astype(BF)
        d_norm = d_norm + mm_nt(d_pre, up)
        g_down[j * pieces : (j + 1) * pieces] = mm_tn(hidden, cot).astype(BF).reshape(pieces, rows, width)
        g_up[j] = mm_tn(normed, d_pre).astype(BF)
        up_sums.append(mm(ones, d_pre)[0:1])
    out_ref[...] = total.astype(BF)
    cot_f = cot.astype(F32)
    d_middle = cot_f + norm_back(d_norm, plain, inverse, gain)
    dmid_ref[...] = d_middle
    d_branch = d_middle.astype(BF)
    d_att = mm_nt(d_branch, w_out[...]).astype(BF) * live.astype(BF)
    d_ref[:, :width] = d_att
    product = d_att.astype(F32) * mixed
    tail = jnp.zeros((local, HEAD_DIM), F32)
    for h in range(HEADS):
        delta = jnp.sum(product[:, h * HEAD_DIM : (h + 1) * HEAD_DIM], axis=-1, keepdims=True)
        high = delta.astype(BF).astype(F32)
        tail = jnp.where(lane == h, high, jnp.where(lane == HEADS + h, delta - high, tail))
    d_ref[:, width:] = tail.astype(BF)
    g_out[...] = mm_tn(attended, d_branch).astype(BF)

    g_pieces = g_refs[0].shape[0]
    for i in range(pieces):
        where = idx[pieces + i]
        at = pl.ds(pl.multiple_of(where * rows, rows), rows)
        g_ref, spot = g_refs[i // g_pieces], i % g_pieces
        pltpu.make_async_copy(g_out.at[at, :], g_ref.at[spot, 0], g_sem).start()
        pltpu.make_async_copy(g_up.at[:, at, :], g_ref.at[spot, pl.ds(1, blocks)], g_sem).start()
        pltpu.make_async_copy(
            g_down.at[pl.ds(where * blocks, blocks)], g_ref.at[spot, pl.ds(1 + blocks, blocks)], g_sem
        ).start()

    sums = [jnp.sum(v, axis=0, keepdims=True) for v in (d_middle, d_norm * plain, d_norm, cot_f)]
    sums = jnp.concatenate(sums + up_sums + [jnp.zeros((HEAD_DIM - 4 - blocks, width), F32)], axis=0)
    columns = jnp.transpose(sums)
    if pieces > 1:
        per = pieces // blocks
        vec_ref[...] = jnp.where(lane < 4, columns, 0.0)
        for j in range(blocks):
            column = jnp.broadcast_to(columns[:, 4 + j : 5 + j], (width, HEAD_DIM)).reshape(
                per, blocks, rows, HEAD_DIM
            )
            wide_lane = lane.reshape(1, 1, HEAD_DIM)
            placed = sum(jnp.where(wide_lane == 4 + i, column[:, i], 0.0) for i in range(blocks))
            vec_ref[j * per * rows : (j + 1) * per * rows, :] += placed.reshape(per * rows, HEAD_DIM)
    else:
        vec_ref[...] = jnp.where(lane < 4 + blocks, columns, 0.0)
    for g_ref in g_refs:
        pltpu.make_async_copy(g_ref, g_ref, g_sem).wait()


def back_body(
    sc, tab, q_own, q_other, d_own, d_other, lse_ref, kv_ref, n_ref, w_ref, dq_in, nk_in, sum_in,
    keep_ref, send_ref, dq_ref, nk_ref, sum_ref, q_scr, do_scr, delta_scr, dkv_scr, *, plane,
):
    count = tab.shape[0] // 3
    unused, unused, rows, unused = kv_ref.shape
    width = w_ref.shape[1]
    min_low, max_high, max_low, min_high = reach(sc, tab, rows)
    q_pos = chip_rows(sc, rows, (1, 2 * rows), 1)
    low, high, unused = table_of(tab, count, q_pos)
    if dq_in is not None:
        dq_ref[...] = dq_in[...]
        nk_ref[...] = nk_in[...]
        sum_ref[...] = sum_in[...]
    q_scr[:, :rows] = q_own[...]
    q_scr[:, rows:] = q_other[...]
    for i, ref in enumerate((d_own, d_other)):
        for h in range(HEADS):
            do_scr[h, i * rows : (i + 1) * rows] = ref[:, h * HEAD_DIM : (h + 1) * HEAD_DIM]
        tail = jnp.transpose(ref[:, width:].astype(F32))
        delta_scr[:, i * rows : (i + 1) * rows] = tail[:HEADS] + tail[HEADS : 2 * HEADS]

    def unit(u, allowed):
        for h in range(HEADS):
            lanes = slice(h * HEAD_DIM, (h + 1) * HEAD_DIM)
            v_lanes = slice(width + h * HEAD_DIM, width + (h + 1) * HEAD_DIM)
            q, do, key = q_scr[h], do_scr[h], kv_ref[u, h]
            soft = jnp.exp2(mm_nt(key, q) - lse_ref[h : h + 1, :])
            if allowed is not None:
                soft = jnp.where(allowed, soft, 0.0)
            d_soft = mm_nt(kv_ref[u, HEADS + h], do)
            d_scores = (soft * (d_soft - delta_scr[h : h + 1, :])).astype(BF)
            dkv_scr[u, :, v_lanes] = mm(soft.astype(BF), do).astype(BF)
            dkv_scr[u, :, lanes] = (mm(d_scores, q) * (SCALE / SCALE2)).astype(BF)
            dq_ref[h] += mm_tn(d_scores, key)

    def unit_step(u, carry):
        start = sc[2 + 2 * plane + u]
        needed = (start < max_high) & (start + rows > min_low)
        whole = (start >= max_low) & (start + rows <= min_high)

        @pl.when(needed & whole)
        def _():
            unit(u, None)

        @pl.when(needed & jnp.logical_not(whole))
        def _():
            k_pos = start + lax.broadcasted_iota(I32, (rows, 1), 0)
            unit(u, (k_pos >= low) & (k_pos < high))

        @pl.when(jnp.logical_not(needed))
        def _():
            dkv_scr[u] = jnp.zeros(dkv_scr.shape[1:], BF)

        return carry

    lax.fori_loop(0, 2, unit_step, 0)
    ones = jnp.ones((8, rows), BF)
    for u, ref in enumerate((keep_ref, send_ref)):
        dkv = dkv_scr[u]
        ref[...] = (mm_nt(dkv[:, :width], w_ref[1]) + mm_nt(dkv[:, width:], w_ref[2])).astype(BF)
        nk_ref[...] += mm_tn(n_ref[u], dkv)
        sum_ref[...] += mm(ones, dkv)


def first_back_body(*refs, **options):
    ins, outs = refs[:10], refs[10:]
    for ref in outs[2:5]:
        ref[...] = jnp.zeros(ref.shape, ref.dtype)
    back_body(*ins, None, None, None, *outs, **options)


def message_body(idx, n_ref, dq_ref, dq_recv, nk_ref, sum_ref, w_ref, col_ref, vec_ref, *refs, rows):
    low_ref, msg_refs, (full, vec) = refs[0], refs[1:-2], refs[-2:]
    local = n_ref.shape[1]
    width = w_ref.shape[1]
    for h in range(HEADS):
        d_query = (dq_ref[h, :local] + dq_recv[h]) * SCALE
        low_ref[:, h * HEAD_DIM : (h + 1) * HEAD_DIM] = d_query.astype(BF)
    d_query = low_ref[...]
    q_sums = mm(jnp.ones((8, local), BF), d_query)
    gain, shift = col_ref[:, 0:1], col_ref[:, 1:2]
    lane = lax.broadcasted_iota(I32, (1, HEAD_DIM), 1)
    gain_grad = jnp.zeros((width, 1), F32)
    shift_grad = jnp.zeros((width, 1), F32)
    columns = []
    for i in range(3):
        lanes = slice(i * width, (i + 1) * width)
        if i == 0:
            product, sums = mm_tn(n_ref[0], d_query), q_sums[0:1]
        else:
            at = slice((i - 1) * width, i * width)
            product, sums = nk_ref[:, at], sum_ref[0:1, at]
        weight = w_ref[i].astype(F32)
        full[:, lanes] = (product * gain + shift * sums).astype(BF)
        gain_grad += jnp.sum(product * weight, axis=-1, keepdims=True)
        shift_grad += jnp.sum(weight * sums, axis=-1, keepdims=True)
        if i != 1:
            columns.append(jnp.transpose(jnp.broadcast_to(sums, (HEAD_DIM, width))))
    vec[...] = vec_ref[...]
    for at, column in ((8, gain_grad), (9, shift_grad), (10, columns[0]), (11, columns[1])):
        vec[...] += jnp.where(lane == at, column, 0.0)
    full[:, 3 * width :] = vec[...].astype(BF)
    k = 0
    for msg_ref in msg_refs:
        for i in range(msg_ref.shape[0]):
            msg_ref[i] = full[pl.ds(pl.multiple_of(idx[k] * rows, rows), rows), :]
            k += 1


def finish_body(tok_ref, dmid_ref, row_ref, dq_ref, w_ref, *refs):
    plain, inverse = normalize(tok_ref[...].astype(F32))
    total = mm_nt(dq_ref[...], w_ref[0])
    for ref in refs[:-1]:
        total = total + ref[...].astype(F32)
    refs[-1][...] = (dmid_ref[...] + norm_back(total, plain, inverse, row_ref[0:1, :])).astype(BF)


def matrices_body(*refs):
    terms, (out_ref, up_ref, down_ref) = refs[:-3], refs[-3:]
    width = out_ref.shape[1]
    part = out_ref.shape[0]
    blocks = up_ref.shape[1] // width

    def block(i):
        total = terms[0][i].astype(F32)
        for term in terms[1:]:
            total = total + term[i].astype(F32)
        return total

    out_ref[...] = block(0)
    for j in range(blocks):
        up_ref[:, j * width : (j + 1) * width] = block(1 + j)
        down_ref[j * part : (j + 1) * part, :] = block(1 + blocks + j)


def unpack_body(*refs):
    terms, (qkv_ref, vec_ref) = refs[:-2], refs[-2:]
    total = terms[0][...]
    for term in terms[1:]:
        total = total + term[...].astype(F32)
    width = qkv_ref.shape[1]
    qkv_ref[...] = total[:, :width]
    vec_ref[...] = total[:, width:]


def shards(
    tokens, w_qkv, w_out, w_up, w_down,
    norm1_gain, norm1_bias, query_bias, value_bias, out_bias, norm2_gain, norm2_bias, up_bias, down_bias,
    cotangent, table_start, support_count, query_count, *, R, F,
):
    A = R // PLANE
    count = R * F
    local, width = tokens.shape[1], tokens.shape[2]
    part = w_qkv.shape[0]
    hidden = w_up.shape[1]
    blocks = hidden // width
    aligned = part % 16 == 0
    rows = part if aligned else width
    pieces = count if aligned else 1
    sds = jax.ShapeDtypeStruct

    r, f = lax.axis_index("rows"), lax.axis_index("fsdp")
    a, x, c = r // PLANE, (r // 2) % 2, r % 2

    def swap_c(v):
        return lax.ppermute(v, "rows", [(i, i ^ 1) for i in range(R)])

    def swap_x(v):
        return lax.ppermute(v, "rows", [(i, i ^ 2) for i in range(R)])

    def turn_a(v, s):
        return lax.ppermute(
            v, "rows", [(i, ((i // PLANE + s) % A) * PLANE + i % PLANE) for i in range(R)]
        )

    def turn_f(v, t):
        return lax.ppermute(v, "fsdp", [(i, (i + t) % F) for i in range(F)])

    def turn_xf(v, t):
        return lax.ppermute(
            v, ("rows", "fsdp"),
            [(i * F + j, (i ^ 2) * F + (j + t) % F) for i in range(R) for j in range(F)],
        )

    def owners(order):
        cr, t, xr, s = (np.array(list(z), np.int32) for z in zip(*order, strict=True))
        plane = lax.rem(a - s + A, A)
        return (((plane * 2 + (x ^ xr)) * 2 + (c ^ cr)) * F + lax.rem(f - t + F, F)).astype(I32)

    unit_s = np.repeat(np.arange(A), 2).astype(np.int32)
    unit_x = np.tile(np.arange(2), A).astype(np.int32)
    unit_start = (lax.rem(a - unit_s + A, A) * 2 + (x ^ unit_x)) * (2 * local) + c * local
    sc = jnp.concatenate([jnp.stack([c, (a * 2 + x) * 2 * local]), unit_start]).astype(I32)
    tab = jnp.concatenate([table_start[0], support_count[0], query_count[0]])

    near = sorted(range(1, A), key=lambda s: min(s, A - s))
    order = [0] + near
    own = tokens[0]
    vectors = [
        v.reshape(1, -1)
        for v in (
            norm1_gain, norm1_bias, query_bias, value_bias, out_bias, norm2_gain, norm2_bias, down_bias, up_bias
        )
    ]
    wide = 3 * width + HEAD_DIM
    pack_in = [w_qkv, w_out, w_up, w_down, *vectors]
    q_own, m_own = pl.pallas_call(
        pack_body,
        grid=(1,),
        out_shape=[sds((4, part, width), BF), sds((1 + 2 * blocks, part, width), BF)],
        in_specs=[pl.BlockSpec(v.shape, lambda i: (0, 0)) for v in pack_in],
        out_specs=[VMEM] * 2,
        scratch_shapes=[pltpu.VMEM((HEAD_DIM, HEAD_DIM), F32)],
        compiler_params=pltpu.CompilerParams(vmem_limit_bytes=56 * MIB),
        cost_estimate=pl.CostEstimate(flops=0, bytes_accessed=16 * part * width, transcendentals=0),
        name="pack",
    )(*pack_in)
    far = near[-1]
    *q_z, own_x = together(*(turn_a(q_own, s) for s in range(1, A)), swap_x(own))
    q_z = jnp.stack([q_own] + q_z)
    moved = [swap_x(q_z)] + [v for t in range(1, F) for v in (turn_f(q_z, t), turn_xf(q_z, t))]
    moved += [turn_a(after(own, own_x), s) for s in near[:-1]]
    moved = together(*moved)
    q_far, tok_z = list(moved[: 2 * F - 1]), jnp.stack(moved[2 * F - 1 :])
    m_start = after(m_own, tok_z)
    *m_z, tok_x = together(*(turn_a(m_start, s) for s in range(1, A)), swap_x(tok_z))
    m_z = jnp.stack([m_own] + m_z)
    q_four = jnp.stack([q_z] + q_far)
    q_pieces = [q_four.reshape(count // 2, 4, part, width), swap_c(q_four).reshape(count // 2, 4, part, width)]
    q_order = [(cr, t, xr, s) for cr in range(2) for t in range(F) for xr in range(2) for s in range(A)]
    q_idx = owners(q_order)
    if not aligned:
        stacked = jnp.concatenate(q_pieces)
        by_owner = jnp.zeros_like(stacked).at[q_idx].set(stacked)
        q_pieces = [by_owner.transpose(1, 0, 2, 3).reshape(1, 4, width, width)]
        q_idx = jnp.zeros((1,), I32)
    w_all, row_vec, col_vec = call(
        functools.partial(assemble_body, rows=rows, count=len(q_pieces)),
        [sds((3, width, width), BF), sds((16, width), F32), sds((width, HEAD_DIM), F32)],
        [q_idx, *q_pieces], [SMEM] + [HBM] * len(q_pieces), [VMEM] * 3,
        scratch=[pltpu.VMEM((width, HEAD_DIM), BF), pltpu.SemaphoreType.DMA((2,))],
        moved=4 * width * wide, vmem=8, name="assemble",
    )
    up_row = row_vec[8 : 8 + blocks].reshape(blocks, count, part).transpose(1, 0, 2).reshape(1, hidden)

    kv, n_units = {}, {}

    def project(arrays, spots, planes, with_q=False):
        outs = [sds((2, 2 * HEADS, local, HEAD_DIM), BF), sds((2, local, width), BF)] * len(planes)
        if with_q:
            outs.append(sds((HEADS, local, HEAD_DIM), BF))
        ins = [*arrays, w_all, row_vec]
        got = call(
            functools.partial(project_body, with_q=with_q, spots=spots, count=len(arrays)),
            outs, ins, [VMEM] * len(ins), [VMEM] * len(outs),
            flops=4 * len(spots) * local * width * width, moved=8 * len(spots) * local * width,
            vmem=8, name="project",
        )
        for i, s in enumerate(planes):
            kv[s], n_units[s] = got[2 * i], got[2 * i + 1]
        return got[-1]

    every = slice(None)
    q = project([own, own_x], [(0, every), (1, every)], [0], True)
    q_other = swap_c(q)
    project([tok_z, tok_x], [(xr, i) for i in range(A - 2) for xr in range(2)], near[:-1])
    far_z, m_x, kv[near[0]], *m_f = together(
        turn_a(after(own, m_z), far), swap_x(m_z), kv[near[0]], *(turn_f(m_z, t) for t in range(1, F))
    )
    far_x, *m_c = together(swap_x(far_z), *(swap_c(v) for v in (m_z, m_x, *m_f)))
    m_xf = [turn_f(m_x, t) for t in range(1, F)]
    project([far_z, far_x], [(0, every), (1, every)], [far])

    unit = 2 * local
    work = 4 * unit * A * unit * width
    packet = width + HEAD_DIM
    att_keep, att_send = call(
        attend_body, [sds((local, packet), F32)] * 2,
        [sc, tab, q, q_other, *(kv[s] for s in range(A))], [SMEM, SMEM, VMEM, VMEM] + [HBM] * A, [VMEM] * 2,
        scratch=[
            pltpu.VMEM((HEADS, unit, HEAD_DIM), BF), pltpu.VMEM((2 * A, HEADS, unit, local), F32),
            pltpu.VMEM((HEADS, unit, HEAD_DIM), F32), pltpu.VMEM((HEADS, unit, 2 * HEAD_DIM), F32),
            pltpu.VMEM((2 * A, 2 * HEADS, local, HEAD_DIM), BF), pltpu.SemaphoreType.DMA((A,)),
        ],
        flops=work, moved=8 * A * unit * width, trans=HEADS * unit * A * unit, vmem=20 + 5 * A, name="attend",
    )
    att_keep, att_send, *m_xf = together(att_keep, att_send, *m_xf)
    att_other = swap_c(att_send)
    m_arrays = [m_z, m_x, *m_f, *m_c, *m_xf, *(swap_c(v) for v in m_xf)]
    m_order = [
        (cr, t, xr, s)
        for cr, t, xr in (
            [(cr, *spot) for cr in range(2) for spot in [(0, 0), (0, 1)] + [(t, 0) for t in range(1, F)]]
            + [(cr, t, 1) for cr in range(2) for t in range(1, F)]
        )
        for s in range(A)
    ]
    m_idx = owners(m_order)
    if not aligned:
        stacked = jnp.concatenate(m_arrays)
        by_owner = jnp.zeros_like(stacked).at[m_idx].set(stacked)
        m_arrays = [
            jnp.concatenate(
                [
                    by_owner[:, 0].reshape(1, width, width),
                    by_owner[:, 1 : 1 + blocks].transpose(1, 0, 2, 3).reshape(blocks, width, width),
                    by_owner[:, 1 + blocks :].reshape(blocks, width, width),
                ]
            )[None]
        ]
        m_idx = jnp.zeros((1,), I32)

    spots = [(t, xr) for t in range(F) for xr in range(2)]
    g_order = [(cr, t, xr, s) for cr in range(2) for t in range(F) for xr in range(2) for s in range(A)]
    g_owner = owners(g_order)
    grad_count = 4 * F if aligned else 1
    g_shape = sds((pieces // grad_count, 1 + 2 * blocks, rows, width), BF)
    idx = jnp.concatenate([m_idx, g_owner if aligned else jnp.zeros((1,), I32)])
    got = call(
        functools.partial(middle_body, rows=rows, m_count=len(m_arrays), grad_count=grad_count),
        [
            sds((local, width), BF), sds((local, width), F32), sds((local, packet), BF), sds((HEADS, unit), F32),
            sds((width, HEAD_DIM), F32),
        ] + [g_shape] * grad_count,
        [idx, sc, tab, *m_arrays, own, att_keep, att_other, cotangent[0], row_vec, up_row],
        [SMEM] * 3 + [HBM] * len(m_arrays) + [VMEM] * 6,
        [VMEM] * 5 + [HBM] * grad_count,
        scratch=[
            pltpu.VMEM((width, width), BF), pltpu.VMEM((blocks, width, width), BF),
            pltpu.VMEM((pieces * blocks, rows, width), BF),
            pltpu.VMEM((width, width), BF), pltpu.VMEM((blocks, width, width), BF),
            pltpu.VMEM((pieces * blocks, rows, width), BF),
            pltpu.SemaphoreType.DMA((3,)), pltpu.SemaphoreType.DMA,
        ],
        flops=6 * local * width * width * (1 + 2 * blocks), moved=4 * width * width * (1 + 2 * blocks),
        trans=local * hidden, vmem=56, name="middle",
    )
    outputs, d_middle, d_own, lse, vec = got[:5]
    grads = got[5:]
    d_other = swap_c(d_own)

    lead = (A, 1 + 2 * blocks, part, width)
    if aligned:
        relative = [g.reshape(lead) for g in grads]
    else:
        whole = grads[0][0]
        by_owner = jnp.concatenate(
            [
                whole[0].reshape(count, 1, part, width),
                whole[1 : 1 + blocks].reshape(blocks, count, part, width).transpose(1, 0, 2, 3),
                whole[1 + blocks :].reshape(count, blocks, part, width),
            ],
            axis=1,
        )
        by_owner = by_owner[g_owner].reshape((4 * F,) + lead)
        relative = [by_owner[i] for i in range(4 * F)]
    g_near = {spot: relative[i] for i, spot in enumerate(spots)}
    g_far = {spot: swap_c(after(relative[2 * F + i], d_other)) for i, spot in reversed(list(enumerate(spots)))}
    parts = [slice(0, A // 2), slice(A // 2, A)]

    def through_f(xr, half):
        return [
            turn_f(add_up([g_near[t, xr], g_far[t, xr]], [[(0, (half,)), (1, (half,))]])[0], F - t)
            for t in range(1, F)
        ]

    d_query = n_product = sums = None
    d_x, d_z, d_keep, d_send = {}, {}, {}, {}
    g_y = {}
    back_order = near[:-1][::-1] + near[-1:] + [0]
    q_now, in_flight = q, []
    steps = len(back_order)
    y_parts = [(xr, half) for xr in (1, 0) for half in parts]
    for step, s in enumerate(back_order):
        ins = [sc, tab, q_now, q_other, d_own, d_other, lse, kv[s], n_units[s], w_all]
        specs = [SMEM, SMEM] + [VMEM] * 8
        body = first_back_body
        if step:
            ins += [d_query, n_product, sums]
            specs += [VMEM] * 3
            body = back_body
        outs = pl.pallas_call(
            functools.partial(body, plane=s),
            out_shape=[
                sds((local, width), BF), sds((local, width), BF), sds((HEADS, unit, HEAD_DIM), F32),
                sds((width, 2 * width), F32), sds((8, 2 * width), F32),
            ],
            in_specs=specs,
            out_specs=[VMEM] * 5,
            scratch_shapes=[
                pltpu.VMEM((HEADS, unit, HEAD_DIM), BF), pltpu.VMEM((HEADS, unit, HEAD_DIM), BF),
                pltpu.VMEM((HEADS, unit), F32), pltpu.VMEM((2, local, 2 * width), BF),
            ],
            compiler_params=pltpu.CompilerParams(vmem_limit_bytes=16 * MIB),
            cost_estimate=pl.CostEstimate(
                flops=work // A * 5 // 2 + 8 * unit * width * width,
                bytes_accessed=16 * unit * width, transcendentals=HEADS * unit * unit,
            ),
            name="back",
        )(*ins)
        if step == 0:
            keys = list(g_far)
            got = together(*outs, *(g_far[k] for k in keys))
            outs = got[:5]
            g_far = dict(zip(keys, got[5:], strict=True))
        else:
            prev = back_order[step - 1]
            beside = {("x", prev): swap_x(d_send[prev])}
            if step >= 2:
                older = back_order[step - 2]
                beside["z", older] = turn_a(d_sum, A - older)
            if step - 1 < len(y_parts):
                for i, v in enumerate(through_f(y_parts[step - 1][0], y_parts[step - 1][1])):
                    beside["y", step - 1, i] = v
            keys = list(beside)
            got = together(*outs, *beside.values())
            outs = got[:5]
            beside = dict(zip(keys, got[5:], strict=True))
            for key, v in beside.items():
                if key[0] == "x":
                    d_x[key[1]] = v
                elif key[0] == "z":
                    d_z[key[1]] = v
                else:
                    g_y[y_parts[key[1]]] = g_y.get(y_parts[key[1]], []) + [v]
            (d_sum,) = add_up([d_keep[prev], d_x[prev]], [[(0, ()), (1, ())]])
        d_keep[s], d_send[s], d_query, n_product, sums = outs
        q_now = after(q, outs[2])
        if step:
            q_now = after(q_now, d_sum)

    last_plane = back_order[-2]
    for k in range(steps - 1, len(y_parts)):
        g_y[y_parts[k]] = through_f(*y_parts[k])
    d_x[0] = swap_x(d_send[0])
    d_z[last_plane] = turn_a(d_sum, A - last_plane)
    dq_recv = swap_c(d_query[:, local:])

    def g_kept(xr, half):
        arrays = [g_near[0, xr], g_far[0, xr], *g_y[xr, half]]
        return arrays, [(0, (half,)), (1, (half,))] + [(2 + i, ()) for i in range(F - 1)]

    half_count = 2 * F
    msg_lead = (A, part, wide)
    n_own = n_units[0]
    msg_idx = owners(q_order) if aligned else jnp.zeros((1,), I32)
    msg_shape = [sds((pieces // 2, rows, wide), BF)] * 2 if aligned else [sds((1, rows, wide), BF)]
    dq_low, *message = call(
        functools.partial(message_body, rows=rows),
        [sds((local, width), BF), *msg_shape],
        [msg_idx, n_own, d_query, dq_recv, n_product, sums, w_all, col_vec, vec],
        [SMEM] + [VMEM] * 8, [VMEM] * (1 + len(msg_shape)),
        scratch=[pltpu.VMEM((width, wide), BF), pltpu.VMEM((width, HEAD_DIM), F32)],
        flops=2 * local * width * width, moved=8 * width * wide, vmem=8, name="message",
    )
    if not aligned:
        flat = message[0][0]
        at = slice(3 * width + 4, 3 * width + 4 + blocks)
        up_part = flat[:, at].T.reshape(count, blocks, part)
        by_owner = flat.reshape(count, part, wide)
        by_owner = by_owner.at[:, :, at].set(up_part.transpose(0, 2, 1))
        by_owner = by_owner[owners(q_order)]
        message = [by_owner[: count // 2], by_owner[count // 2 :]]
    w_far = swap_c(message[1])
    g_x = []
    for half in parts:
        arrays, terms = g_kept(1, half)
        g_x.append(swap_x(add_up(arrays, [terms])[0]))
    w_far, g_last = together(w_far, g_y[y_parts[-1]][0])
    g_y[y_parts[-1]] = [g_last] + g_y[y_parts[-1]][1:]
    w_far = w_far.reshape((half_count,) + msg_lead)
    w_near = message[0].reshape((half_count,) + msg_lead)
    w_both = add_up([w_near, w_far], [[(0, (i,)), (1, (i,))] for i in range(half_count)])
    got = []
    for (t, xr), sent in zip(spots, w_both, strict=True):
        if xr:
            sent = turn_xf(sent, F - t) if t else swap_x(sent)
        elif t:
            sent = turn_f(sent, F - t)
        got.append(sent)
    got[0], d_x[0], d_z[last_plane] = together(got[0], d_x[0], d_z[last_plane])
    w_z = add_up(got, [[(i, (s,)) for i in range(len(got))] for s in near])
    (w_own,) = add_up(got, [[(i, (0,)) for i in range(len(got))]], F32)
    w_z = [turn_a(v, A - s) for s, v in zip(near, w_z, strict=True)]
    grad_qkv, last = call(
        unpack_body, [sds((part, 3 * width), F32), sds((part, HEAD_DIM), F32)], [w_own, *w_z],
        [VMEM] * A, [VMEM] * 2, moved=16 * part * width, vmem=8, name="unpack",
    )

    g_z_send, g_mine = {}, None
    for half, arrived in zip(parts, g_x, strict=True):
        arrays, terms = g_kept(0, half)
        arrays.append(arrived)
        planes = list(range(A))[half]

        def one(s, terms=terms, start=half.start, last=len(arrays) - 1):
            out = [(i, (start + s,) if spot else (s,)) for i, spot in terms]
            return out + [(last, (s,))]

        for s, v in zip(planes, add_up(arrays, [one(s - half.start) for s in planes]), strict=True):
            if s:
                g_z_send[s] = v
            else:
                g_mine = v
    g_z_send = [g_z_send[s] for s in near]
    g_z = [turn_a(v, A - s) for s, v in zip(near, g_z_send, strict=True)]
    grad_out, grad_up, grad_down = call(
        matrices_body,
        [sds((part, width), F32), sds((part, hidden), F32), sds((blocks * part, width), F32)],
        [g_mine, *g_z], [VMEM] * A, [VMEM] * 3, moved=6 * A * g_mine.size, vmem=8, name="matrices",
    )
    grad_tokens = call(
        finish_body, sds((local, width), BF),
        [own, d_middle, row_vec, dq_low, w_all, d_keep[0], d_x[0], *(d_z[s] for s in near)],
        [VMEM] * (6 + A), VMEM, flops=20 * local * width, moved=16 * local * width, vmem=8, name="finish",
    )
    return (
        outputs[None],
        grad_tokens[None],
        grad_qkv,
        grad_out,
        grad_up,
        grad_down,
        last[:, 8],
        last[:, 9],
        last[:, 10],
        last[:, 11],
        last[:, 0],
        last[:, 1],
        last[:, 2],
        last[:, 4 : 4 + blocks].T.reshape(blocks * part),
        last[:, 3],
    )


def solution(mesh):
    both = ("rows", "fsdp")
    matrix, vector, act, table = P(both, None), P(both), P("fsdp", "rows", None), P("fsdp", None)
    return jax.shard_map(
        functools.partial(shards, R=mesh.shape["rows"], F=mesh.shape["fsdp"]),
        mesh=mesh,
        in_specs=(act,) + (matrix,) * 4 + (vector,) * 9 + (act,) + (table,) * 3,
        out_specs=(act, act) + (matrix,) * 4 + (vector,) * 9,
        check_vma=False,
    )
```

```python
import functools
import math

import jax
import jax.numpy as jnp
import numpy as np
from jax import lax
from jax.experimental import pallas as pl
from jax.experimental.pallas import tpu as pltpu
from jax.sharding import PartitionSpec as P

HEADS = 4
HEAD_DIM = 128
EPS = 1e-05
NEG = -1e30
PLANE = 4
MIB = 1024 * 1024
BF = jnp.bfloat16
F32 = jnp.float32
I32 = jnp.int32
SCALE = 1.0 / math.sqrt(HEAD_DIM)
SCALE2 = SCALE * math.log2(math.e)
GELU_A = math.sqrt(2.0 / math.pi)
GELU_B = 0.044715

VMEM = pl.BlockSpec(memory_space=pltpu.VMEM)
SMEM = pl.BlockSpec(memory_space=pltpu.SMEM)
HBM = pl.BlockSpec(memory_space=pltpu.HBM)
ANY = pl.BlockSpec(memory_space=pl.ANY)


def after(value, *others):
    return lax.optimization_barrier((value, *others))[0]


def together(*values):
    return lax.optimization_barrier(values)


def mm(left, right):
    return jnp.dot(left, right, preferred_element_type=F32)


def mm_nt(left, right):
    return lax.dot_general(left, right, (((1,), (1,)), ((), ())), preferred_element_type=F32)


def mm_tn(left, right):
    return lax.dot_general(left, right, (((0,), (0,)), ((), ())), preferred_element_type=F32)


def call(body, outs, ins, in_specs, out_specs, scratch=(), flops=0, moved=0, trans=0, vmem=16, name=None):
    return pl.pallas_call(
        body,
        out_shape=outs,
        in_specs=in_specs,
        out_specs=out_specs,
        scratch_shapes=scratch,
        compiler_params=pltpu.CompilerParams(vmem_limit_bytes=vmem * MIB),
        cost_estimate=pl.CostEstimate(
            flops=int(flops), bytes_accessed=int(moved), transcendentals=int(trans)
        ),
        name=name,
    )(*ins)


def normalize(values):
    centre = values - jnp.mean(values, axis=-1, keepdims=True)
    spread = jnp.mean(centre * centre, axis=-1, keepdims=True)
    inverse = lax.rsqrt(spread + EPS)
    return centre * inverse, inverse


def norm_back(grad_out, plain, inverse, gain):
    scaled = grad_out * gain
    return inverse * (
        scaled
        - jnp.mean(scaled, axis=-1, keepdims=True)
        - plain * jnp.mean(scaled * plain, axis=-1, keepdims=True)
    )


def table_of(tab, count, pos):
    low = jnp.zeros_like(pos) + tab[0]
    high = low + tab[count]
    finish = high + tab[2 * count]
    for t in range(1, count):
        here = pos >= tab[t]
        top = tab[t] + tab[count + t]
        low = jnp.where(here, tab[t], low)
        high = jnp.where(here, top, high)
        finish = jnp.where(here, top + tab[2 * count + t], finish)
    return low, high, finish


def pack_body(qkv_ref, out_ref, up_ref, down_ref, *refs):
    vec_refs, (q_ref, m_ref, vec_scr) = refs[:-3], refs[-3:]
    part, width = out_ref.shape
    blocks = up_ref.shape[1] // width
    vec_scr[...] = jnp.zeros(vec_scr.shape, F32)
    for k, ref in enumerate(vec_refs[:-1]):
        vec_scr[k : k + 1, :part] = ref[...].astype(F32)
    for j in range(blocks):
        vec_scr[8 + j : 9 + j, :part] = vec_refs[-1][:, j * part : (j + 1) * part].astype(F32)
    for i in range(3):
        q_ref[i] = qkv_ref[:, i * width : (i + 1) * width]
    q_ref[3] = jnp.zeros((part, width), BF)
    q_ref[3, :, :HEAD_DIM] = jnp.transpose(vec_scr[...])[:part].astype(BF)
    m_ref[0] = out_ref[...]
    for j in range(blocks):
        m_ref[1 + j] = up_ref[:, j * width : (j + 1) * width]
        m_ref[1 + blocks + j] = down_ref[j * part : (j + 1) * part, :]


def sum_body(*refs, plan, count):
    for out_ref, terms in zip(refs[count:], plan, strict=True):
        total = None
        for which, spot in terms:
            term = refs[which][spot].astype(F32)
            total = term if total is None else total + term
        out_ref[...] = total.astype(out_ref.dtype)


def join_body(*refs, plan, count):
    out_ref, row = refs[count], 0
    for terms in plan:
        total = None
        for which, spot in terms:
            term = refs[which][spot].astype(F32)
            total = term if total is None else total + term
        out_ref[row : row + total.shape[0]] = total.astype(out_ref.dtype)
        row += total.shape[0]


def join_up(arrays, plan):
    shapes = [jax.eval_shape(lambda v: v[terms[0][1]], arrays[terms[0][0]]).shape for terms in plan]
    shape = (sum(v[0] for v in shapes),) + shapes[0][1:]
    moved = math.prod(shape) * 4
    return call(
        functools.partial(join_body, plan=plan, count=len(arrays)), [jax.ShapeDtypeStruct(shape, BF)], arrays,
        [VMEM] * len(arrays), [VMEM], flops=moved, moved=moved, vmem=16, name="join",
    )


def add_up(arrays, plan, dtype=BF):
    outs = []
    for terms in plan:
        which, spot = terms[0]
        outs.append(jax.ShapeDtypeStruct(jax.eval_shape(lambda v: v[spot], arrays[which]).shape, dtype))
    moved = sum(o.size for o in outs) * 4
    return call(
        functools.partial(sum_body, plan=plan, count=len(arrays)), outs, arrays,
        [VMEM] * len(arrays), [VMEM] * len(outs), flops=moved, moved=moved, vmem=16, name="add",
    )


def copy_body(*refs, plan, count):
    outs, sem = refs[count:-1], refs[-1]
    copies = []
    for k, (which, source, out, spot) in enumerate(plan):
        copies.append(pltpu.make_async_copy(refs[which].at[source], outs[out].at[spot], sem.at[k]))
        copies[-1].start()
    for copy in copies:
        copy.wait()


def copy_out(arrays, shapes, plan):
    moved = sum(math.prod(shape) for shape in shapes) * 4
    return call(
        functools.partial(copy_body, plan=plan, count=len(arrays)),
        [jax.ShapeDtypeStruct(shape, arrays[0].dtype) for shape in shapes], arrays,
        [HBM] * len(arrays), [VMEM] * len(shapes),
        scratch=[pltpu.SemaphoreType.DMA((len(plan),))], moved=moved, vmem=4, name="copy",
    )


def stack(arrays):
    shape = (len(arrays),) + arrays[0].shape
    every = (slice(None),)
    (out,) = copy_out(arrays, [shape], [(i, every, 0, (i,)) for i in range(len(arrays))])
    return out


def assemble_body(idx, *refs, rows, count):
    pieces, (w_ref, row_ref, col_ref, low_scr, sem) = refs[:count], refs[count:]
    k = 0
    for piece in pieces:
        for j in range(piece.shape[0]):
            at = pl.ds(pl.multiple_of(idx[k] * rows, rows), rows)
            pltpu.make_async_copy(piece.at[j, pl.ds(0, 3)], w_ref.at[:, at, :], sem.at[0]).start()
            pltpu.make_async_copy(piece.at[j, 3, :, pl.ds(0, HEAD_DIM)], low_scr.at[at, :], sem.at[1]).start()
            k += 1
    pltpu.make_async_copy(low_scr, low_scr, sem.at[1]).wait()
    columns = low_scr[...].astype(F32)
    col_ref[...] = columns
    row_ref[...] = jnp.transpose(columns)[: row_ref.shape[0]]
    pltpu.make_async_copy(w_ref, w_ref, sem.at[0]).wait()


def project_body(*refs, with_q, spots, count):
    pieces, (w_ref, row_ref), outs = refs[:count], refs[count : count + 2], refs[count + 2 :]
    kv_ref, n_ref = outs[:2]
    gain, shift = row_ref[0:1, :], row_ref[1:2, :]
    for i, (which, lead) in enumerate(spots):
        plain, unused_inverse = normalize(pieces[which][lead].astype(F32))
        n_ref[i] = plain.astype(BF)
        normed = (plain * gain + shift).astype(BF)
        keys = mm(normed, w_ref[1])
        values = mm(normed, w_ref[2]) + row_ref[3:4, :]
        for h in range(HEADS):
            lanes = slice(h * HEAD_DIM, (h + 1) * HEAD_DIM)
            kv_ref[i, h] = keys[:, lanes].astype(BF)
            kv_ref[i, HEADS + h] = values[:, lanes].astype(BF)
        if with_q and i == 0:
            queries = (mm(normed, w_ref[0]) + row_ref[2:3, :]) * SCALE2
            for h in range(HEADS):
                outs[2][h] = queries[:, h * HEAD_DIM : (h + 1) * HEAD_DIM].astype(BF)


def ready_body(idx, *refs, rows, count, part):
    pieces, (own_ref, own_x_ref, tok_ref) = refs[:count], refs[count : count + 3]
    w_ref, row_ref, col_ref, up_ref, kv_own, n_own, q_ref, kv_z, n_z, low_scr, sem = refs[count + 3 :]
    assemble_body(idx, *pieces, w_ref, row_ref, col_ref, low_scr, sem, rows=rows, count=count)
    width = up_ref.shape[1]
    blocks = up_ref.shape[0]
    per = width // blocks
    source = lax.broadcasted_iota(I32, (per, width), 0)
    target = lax.broadcasted_iota(I32, (per, width), 1)
    total = jnp.zeros((blocks, width), F32)
    for k in range(blocks):
        spread = jnp.where(
            target == (source // part) * (blocks * part) + k * part + lax.rem(source, part), 1.0, 0.0
        ).astype(BF)
        mine = [row_ref[8 + k : 9 + k, j * per : (j + 1) * per] for j in range(blocks)]
        total += mm(jnp.concatenate(mine, axis=0).astype(BF), spread)
    up_ref[...] = total
    every = slice(None)
    project_body(
        own_ref, own_x_ref, w_ref, row_ref, kv_own, n_own, q_ref, with_q=True, spots=[(0, every), (1, every)], count=2
    )
    spots = [(0, i) for i in range(tok_ref.shape[0])]
    project_body(tok_ref, w_ref, row_ref, kv_z, n_z, with_q=False, spots=spots, count=1)


def reach(sc, tab, rows):
    count = tab.shape[0] // 3
    min_low, min_high, unused = table_of(tab, count, sc[1])
    max_low, max_high, unused = table_of(tab, count, sc[1] + 2 * rows - 1)
    return min_low, max_high, max_low, min_high


def chip_rows(sc, rows, shape, dim):
    spot = lax.broadcasted_iota(I32, shape, dim) + sc[0] * rows
    return sc[1] + jnp.where(spot >= 2 * rows, spot - 2 * rows, spot)


def attend_body(sc, tab, q_own, q_other, *refs, kv_units):
    kv_refs, (keep_ref, send_ref, q_scr, s_scr, m_scr, acc_scr, kv_ref, sem) = refs[:-8], refs[-8:]
    count = tab.shape[0] // 3
    units, unused, rows, unused = kv_ref.shape
    k = 0
    for ref in kv_refs:
        for i in range(ref.shape[0]):
            pltpu.make_async_copy(ref.at[i], kv_ref.at[kv_units[k]], sem.at[kv_units[k]]).start()
            k += 1
    min_low, max_high, max_low, min_high = reach(sc, tab, rows)
    q_pos = chip_rows(sc, rows, (2 * rows, 1), 0)
    low, high, unused = table_of(tab, count, q_pos)
    ones = jnp.ones((rows, HEAD_DIM), BF)
    q_scr[:, :rows] = q_own[...]
    q_scr[:, rows:] = q_other[...]
    m_scr[...] = jnp.full(m_scr.shape, NEG, F32)
    acc_scr[...] = jnp.zeros(acc_scr.shape, F32)

    def keep_scores(u, allowed):
        for h in range(HEADS):
            scores = mm_nt(q_scr[h], kv_ref[u, h])
            if allowed is not None:
                scores = jnp.where(allowed, scores, NEG)
            s_scr[u, h] = scores
            top = m_scr[h]
            for j in range(rows // HEAD_DIM):
                top = jnp.maximum(top, scores[:, j * HEAD_DIM : (j + 1) * HEAD_DIM])
            m_scr[h] = top

    def score_step(u, carry):
        start = sc[2 + u]

        pltpu.make_async_copy(kv_refs[0].at[0], kv_ref.at[u], sem.at[u]).wait()
        needed = (start < max_high) & (start + rows > min_low)
        whole = (start >= max_low) & (start + rows <= min_high)

        @pl.when(needed & whole)
        def _():
            keep_scores(u, None)

        @pl.when(needed & jnp.logical_not(whole))
        def _():
            k_pos = start + lax.broadcasted_iota(I32, (1, rows), 1)
            keep_scores(u, (k_pos >= low) & (k_pos < high))

        return carry

    lax.fori_loop(0, units, score_step, 0)
    for h in range(HEADS):
        top = jnp.max(m_scr[h], axis=-1, keepdims=True)
        m_scr[h] = jnp.broadcast_to(jnp.where(top > 0.5 * NEG, top, 0.0), m_scr.shape[1:])

    def value_step(u, carry):
        start = sc[2 + u]
        needed = (start < max_high) & (start + rows > min_low)

        @pl.when(needed)
        def _():
            for h in range(HEADS):
                soft = jnp.exp2(s_scr[u, h] - m_scr[h][:, :1]).astype(BF)
                wide = jnp.concatenate([kv_ref[u, HEADS + h], ones], axis=1)
                acc_scr[h] += mm(soft, wide)

        return carry

    lax.fori_loop(0, units, value_step, 0)
    lane = lax.broadcasted_iota(I32, (1, HEAD_DIM), 1)
    width = HEADS * HEAD_DIM
    mine = jnp.zeros((rows, HEAD_DIM), F32)
    theirs = mine
    for h in range(HEADS):
        lanes = slice(h * HEAD_DIM, (h + 1) * HEAD_DIM)
        total = acc_scr[h, :, HEAD_DIM:]
        some = total > 0.0
        mixed = acc_scr[h, :, :HEAD_DIM] / jnp.where(some, total, 1.0)
        log_total = jnp.where(some, m_scr[h] + jnp.log2(jnp.where(some, total, 1.0)), NEG)
        keep_ref[:, lanes] = mixed[:rows]
        send_ref[:, lanes] = mixed[rows:]
        mine = jnp.where(lane == h, log_total[:rows], jnp.where(lane == HEADS + h, log_total[rows:], mine))
        theirs = jnp.where(lane == h, log_total[rows:], jnp.where(lane == HEADS + h, log_total[:rows], theirs))
    keep_ref[:, width:] = mine
    send_ref[:, width:] = theirs


def middle_body(idx, sc, tab, *refs, rows, m_count, grad_count):
    m_refs, (tok_ref, own_ref, other_ref, cot_ref, row_ref, up_row_ref) = refs[:m_count], refs[m_count : m_count + 6]
    outs = refs[m_count + 6 :]
    out_ref, dmid_ref, d_ref, lse_ref, vec_ref = outs[:5]
    g_refs = outs[5 : 5 + grad_count]
    (w_out, w_up, w_down, g_out, g_up, g_down, dh_scr, sem, g_sem) = outs[5 + grad_count :]
    blocks, width = w_up.shape[0], w_up.shape[2]
    pieces = w_down.shape[0] // blocks
    count = tab.shape[0] // 3
    local = tok_ref.shape[0]
    spots = []
    for m_ref in m_refs:
        for spot in range(m_ref.shape[0]):
            owner = idx[len(spots)]
            spots.append(
                (m_ref, spot, pl.ds(pl.multiple_of(owner * rows, rows), rows), pl.ds(owner * blocks, blocks))
            )
    for m_ref, spot, at, unused in spots:
        pltpu.make_async_copy(m_ref.at[spot, 0], w_out.at[at, :], sem.at[0]).start()
    for m_ref, spot, unused, at in spots:
        pltpu.make_async_copy(m_ref.at[spot, pl.ds(1 + blocks, blocks)], w_down.at[at], sem.at[2]).start()
    for m_ref, spot, at, unused in spots:
        pltpu.make_async_copy(m_ref.at[spot, pl.ds(1, blocks)], w_up.at[:, at, :], sem.at[1]).start()

    pos = sc[1] + sc[0] * local + lax.broadcasted_iota(I32, (local, 1), 0)
    unused_low, unused_high, finish = table_of(tab, count, pos)
    live = (pos < finish).astype(F32)
    gain, shift = row_ref[5:6, :], row_ref[6:7, :]
    lane = lax.broadcasted_iota(I32, (1, HEAD_DIM), 1)
    lse_own, lse_other = own_ref[:, width:], other_ref[:, width:]
    top = jnp.maximum(lse_own, lse_other)
    share_own, share_other = jnp.exp2(lse_own - top), jnp.exp2(lse_other - top)
    share = share_own + share_other
    log_total = jnp.transpose(top + jnp.log2(share))
    lse_ref[...] = jnp.concatenate([log_total[:HEADS], log_total[HEADS : 2 * HEADS]], axis=1)
    share_own, share_other = share_own / share, share_other / share
    mixed = []
    for h in range(HEADS):
        lanes = slice(h * HEAD_DIM, (h + 1) * HEAD_DIM)
        mixed.append(own_ref[:, lanes] * share_own[:, h : h + 1] + other_ref[:, lanes] * share_other[:, h : h + 1])
    mixed = jnp.concatenate(mixed, axis=1)
    attended = (mixed * live).astype(BF)
    cot = cot_ref[...]
    pltpu.make_async_copy(w_out, w_out, sem.at[0]).wait()
    middle = tok_ref[...].astype(F32) + mm(attended, w_out[...]) + row_ref[4:5, :]
    pltpu.make_async_copy(w_down, w_down, sem.at[2]).wait()
    for j in range(blocks):
        dh_scr[j] = mm_nt(cot, w_down[j * pieces : (j + 1) * pieces].reshape(width, width))
    plain, inverse = normalize(middle)
    normed = (plain * gain + shift).astype(BF)
    pltpu.make_async_copy(w_up, w_up, sem.at[1]).wait()
    total = middle + row_ref[7:8, :]
    d_norm = jnp.zeros(middle.shape, F32)
    ones = jnp.ones((8, local), BF)
    up_sums = []
    for j in range(blocks):
        up = w_up[j]
        down = w_down[j * pieces : (j + 1) * pieces].reshape(width, width)
        pre = mm(normed, up) + up_row_ref[j : j + 1, :]
        square = pre * pre
        t = jnp.tanh(GELU_A * pre * (1.0 + GELU_B * square))
        half = 0.5 * (1.0 + t)
        hidden = (pre * half).astype(BF)
        slope = half + 0.5 * pre * (1.0 - t * t) * (GELU_A * (1.0 + 3.0 * GELU_B * square))
        total = total + mm(hidden, down)
        d_pre = (dh_scr[j] * slope).astype(BF)
        d_norm = d_norm + mm_nt(d_pre, up)
        g_down[j * pieces : (j + 1) * pieces] = mm_tn(hidden, cot).astype(BF).reshape(pieces, rows, width)
        g_up[j] = mm_tn(normed, d_pre).astype(BF)
        up_sums.append(mm(ones, d_pre)[0:1])
    g_pieces = g_refs[0].shape[0]
    spots = []
    for i in range(pieces):
        g_ref, spot, where = g_refs[i // g_pieces], i % g_pieces, idx[pieces + i]
        spots.append((g_ref, spot, pl.ds(pl.multiple_of(where * rows, rows), rows)))
        at = pl.ds(where * blocks, blocks)
        pltpu.make_async_copy(g_down.at[at], g_ref.at[spot, pl.ds(1 + blocks, blocks)], g_sem).start()
    for g_ref, spot, at in spots:
        pltpu.make_async_copy(g_up.at[:, at, :], g_ref.at[spot, pl.ds(1, blocks)], g_sem).start()
    out_ref[...] = total.astype(BF)
    cot_f = cot.astype(F32)
    d_middle = cot_f + norm_back(d_norm, plain, inverse, gain)
    dmid_ref[...] = d_middle
    d_branch = d_middle.astype(BF)
    g_out[...] = mm_tn(attended, d_branch).astype(BF)
    for g_ref, spot, at in spots:
        pltpu.make_async_copy(g_out.at[at, :], g_ref.at[spot, 0], g_sem).start()
    d_att = mm_nt(d_branch, w_out[...]).astype(BF) * live.astype(BF)
    d_ref[:, :width] = d_att
    product = d_att.astype(F32) * mixed
    tail = jnp.zeros((local, HEAD_DIM), F32)
    for h in range(HEADS):
        delta = jnp.sum(product[:, h * HEAD_DIM : (h + 1) * HEAD_DIM], axis=-1, keepdims=True)
        high = delta.astype(BF).astype(F32)
        tail = jnp.where(lane == h, high, jnp.where(lane == HEADS + h, delta - high, tail))
    d_ref[:, width:] = tail.astype(BF)

    sums = [jnp.sum(v, axis=0, keepdims=True) for v in (d_middle, d_norm * plain, d_norm, cot_f)]
    sums = jnp.concatenate(sums + up_sums + [jnp.zeros((HEAD_DIM - 4 - blocks, width), F32)], axis=0)
    columns = jnp.transpose(sums)
    if pieces > 1:
        per = pieces // blocks
        vec_ref[...] = jnp.where(lane < 4, columns, 0.0)
        for j in range(blocks):
            column = jnp.broadcast_to(columns[:, 4 + j : 5 + j], (width, HEAD_DIM)).reshape(
                per, blocks, rows, HEAD_DIM
            )
            wide_lane = lane.reshape(1, 1, HEAD_DIM)
            placed = sum(jnp.where(wide_lane == 4 + i, column[:, i], 0.0) for i in range(blocks))
            vec_ref[j * per * rows : (j + 1) * per * rows, :] += placed.reshape(per * rows, HEAD_DIM)
    else:
        vec_ref[...] = jnp.where(lane < 4 + blocks, columns, 0.0)
    for g_ref in g_refs:
        pltpu.make_async_copy(g_ref, g_ref, g_sem).wait()


def back_body(
    sc, tab, q_ref, do_ref, delta_ref, lse_ref, kv_near, kv_far, n_near, n_far, w_ref, own_in, other_in, nk_in, sum_in,
    keep_ref, send_ref, own_ref, other_ref, nk_ref, sum_ref, dkv_scr, *, plane, spots,
):
    count = tab.shape[0] // 3
    unused, unused, rows, unused = kv_near.shape
    width = w_ref.shape[1]
    min_low, max_high, max_low, min_high = reach(sc, tab, rows)
    q_pos = chip_rows(sc, rows, (1, 2 * rows), 1)
    low, high, unused = table_of(tab, count, q_pos)
    if own_in is None:
        own_ref[...] = jnp.zeros(own_ref.shape, F32)
        other_ref[...] = jnp.zeros(other_ref.shape, F32)
    else:
        own_ref[...] = own_in[...]
        other_ref[...] = other_in[...]

    def unit(u, allowed):
        for h in range(HEADS):
            lanes = slice(h * HEAD_DIM, (h + 1) * HEAD_DIM)
            v_lanes = slice(width + h * HEAD_DIM, width + (h + 1) * HEAD_DIM)
            kv_ref, spot = (kv_near, kv_far)[u], spots[u]
            q, do, key = q_ref[h], do_ref[h], kv_ref[spot, h]
            soft = jnp.exp2(mm_nt(key, q) - lse_ref[h : h + 1, :])
            if allowed is not None:
                soft = jnp.where(allowed, soft, 0.0)
            d_soft = mm_nt(kv_ref[spot, HEADS + h], do)
            d_scores = (soft * (d_soft - delta_ref[h : h + 1, :])).astype(BF)
            dkv_scr[u, :, v_lanes] = mm(soft.astype(BF), do).astype(BF)
            dkv_scr[u, :, lanes] = (mm(d_scores, q) * (SCALE / SCALE2)).astype(BF)
            d_query = mm_tn(key, d_scores)
            own_ref[h] += d_query[:, :rows]
            other_ref[h] += d_query[:, rows:]

    for u in range(2):
        start = sc[2 + 2 * plane + u]
        needed = (start < max_high) & (start + rows > min_low)
        whole = (start >= max_low) & (start + rows <= min_high)

        @pl.when(needed & whole)
        def _(u=u):
            unit(u, None)

        @pl.when(needed & jnp.logical_not(whole))
        def _(u=u, start=start):
            k_pos = start + lax.broadcasted_iota(I32, (rows, 1), 0)
            unit(u, (k_pos >= low) & (k_pos < high))

        @pl.when(jnp.logical_not(needed))
        def _(u=u):
            dkv_scr[u] = jnp.zeros(dkv_scr.shape[1:], BF)

    ones = jnp.ones((8, rows), BF)
    for u, ref in enumerate((keep_ref, send_ref)):
        ref[...] = (mm_nt(dkv_scr[u, :, :width], w_ref[1]) + mm_nt(dkv_scr[u, :, width:], w_ref[2])).astype(BF)
    product = mm_tn(n_near[spots[0]], dkv_scr[0]) + mm_tn(n_far[spots[1]], dkv_scr[1])
    sums = mm(ones, dkv_scr[0]) + mm(ones, dkv_scr[1])
    nk_ref[...] = product if nk_in is None else nk_in[...] + product
    sum_ref[...] = sums if sum_in is None else sum_in[...] + sums


def first_back_body(sc, tab, q_ref, d_own, d_other, *refs, **options):
    ins, outs, do_ref, delta_ref, dkv_scr = refs[:6], refs[6:-3], refs[-3], refs[-2], refs[-1]
    rows, width = d_own.shape[0], HEADS * HEAD_DIM
    for i, ref in enumerate((d_own, d_other)):
        for h in range(HEADS):
            do_ref[h, i * rows : (i + 1) * rows] = ref[:, h * HEAD_DIM : (h + 1) * HEAD_DIM]
        tail = jnp.transpose(ref[:, width:].astype(F32))
        delta_ref[:, i * rows : (i + 1) * rows] = tail[:HEADS] + tail[HEADS : 2 * HEADS]
    nothing = [None] * 4
    back_body(sc, tab, q_ref, do_ref, delta_ref, *ins, *nothing, *outs, dkv_scr, **options)


def message_body(idx, n_ref, dq_own, dq_recv, nk_ref, sum_ref, w_ref, col_ref, vec_ref, *refs, rows):
    low_ref, msg_refs, (full, vec) = refs[0], refs[1:-2], refs[-2:]
    local = n_ref.shape[1]
    width = w_ref.shape[1]
    for h in range(HEADS):
        d_query = jnp.transpose(dq_own[h] + dq_recv[h]) * SCALE
        low_ref[:, h * HEAD_DIM : (h + 1) * HEAD_DIM] = d_query.astype(BF)
    d_query = low_ref[...]
    q_sums = mm(jnp.ones((8, local), BF), d_query)
    gain, shift = col_ref[:, 0:1], col_ref[:, 1:2]
    lane = lax.broadcasted_iota(I32, (1, HEAD_DIM), 1)
    gain_grad = jnp.zeros((width, 1), F32)
    shift_grad = jnp.zeros((width, 1), F32)
    columns = []
    for i in range(3):
        lanes = slice(i * width, (i + 1) * width)
        if i == 0:
            product, sums = mm_tn(n_ref[0], d_query), q_sums[0:1]
        else:
            at = slice((i - 1) * width, i * width)
            product, sums = nk_ref[:, at], sum_ref[0:1, at]
        weight = w_ref[i].astype(F32)
        full[:, lanes] = (product * gain + shift * sums).astype(BF)
        gain_grad += jnp.sum(product * weight, axis=-1, keepdims=True)
        shift_grad += jnp.sum(weight * sums, axis=-1, keepdims=True)
        if i != 1:
            columns.append(jnp.transpose(jnp.broadcast_to(sums, (HEAD_DIM, width))))
    vec[...] = vec_ref[...]
    for at, column in ((8, gain_grad), (9, shift_grad), (10, columns[0]), (11, columns[1])):
        vec[...] += jnp.where(lane == at, column, 0.0)
    full[:, 3 * width :] = vec[...].astype(BF)
    k = 0
    for msg_ref in msg_refs:
        for i in range(msg_ref.shape[0]):
            msg_ref[i] = full[pl.ds(pl.multiple_of(idx[k] * rows, rows), rows), :]
            k += 1


def finish_body(tok_ref, dmid_ref, row_ref, dq_ref, w_ref, *refs):
    plain, inverse = normalize(tok_ref[...].astype(F32))
    total = mm_nt(dq_ref[...], w_ref[0])
    for ref in refs[:-1]:
        total = total + ref[...].astype(F32)
    refs[-1][...] = (dmid_ref[...] + norm_back(total, plain, inverse, row_ref[0:1, :])).astype(BF)


def matrices_body(*refs):
    terms, (out_ref, up_ref, down_ref) = refs[:-3], refs[-3:]
    width = out_ref.shape[1]
    part = out_ref.shape[0]
    blocks = up_ref.shape[1] // width

    def block(i):
        total = terms[0][i].astype(F32)
        for term in terms[1:]:
            total = total + term[i].astype(F32)
        return total

    out_ref[...] = block(0)
    for j in range(blocks):
        up_ref[:, j * width : (j + 1) * width] = block(1 + j)
        down_ref[j * part : (j + 1) * part, :] = block(1 + blocks + j)


def unpack_body(*refs):
    terms, (qkv_ref, vec_ref) = refs[:-2], refs[-2:]
    total = terms[0][...]
    for term in terms[1:]:
        total = total + term[...].astype(F32)
    width = qkv_ref.shape[1]
    qkv_ref[...] = total[:, :width]
    vec_ref[...] = total[:, width:]


def shards(
    tokens, w_qkv, w_out, w_up, w_down,
    norm1_gain, norm1_bias, query_bias, value_bias, out_bias, norm2_gain, norm2_bias, up_bias, down_bias,
    cotangent, table_start, support_count, query_count, *, R, F,
):
    A = R // PLANE
    count = R * F
    local, width = tokens.shape[1], tokens.shape[2]
    part = w_qkv.shape[0]
    hidden = w_up.shape[1]
    blocks = hidden // width
    aligned = part % 16 == 0
    rows = part if aligned else width
    pieces = count if aligned else 1
    sds = jax.ShapeDtypeStruct

    r, f = lax.axis_index("rows"), lax.axis_index("fsdp")
    a, x, c = r // PLANE, (r // 2) % 2, r % 2

    def swap_c(v):
        return lax.ppermute(v, "rows", [(i, i ^ 1) for i in range(R)])

    def swap_x(v):
        return lax.ppermute(v, "rows", [(i, i ^ 2) for i in range(R)])

    def turn_a(v, s):
        return lax.ppermute(
            v, "rows", [(i, ((i // PLANE + s) % A) * PLANE + i % PLANE) for i in range(R)]
        )

    def turn_f(v, t):
        return lax.ppermute(v, "fsdp", [(i, (i + t) % F) for i in range(F)])

    def turn_xf(v, t):
        return lax.ppermute(
            v, ("rows", "fsdp"),
            [(i * F + j, (i ^ 2) * F + (j + t) % F) for i in range(R) for j in range(F)],
        )

    def owners(order):
        cr, t, xr, s = (np.array(list(z), np.int32) for z in zip(*order, strict=True))
        plane = lax.rem(a - s + A, A)
        return (((plane * 2 + (x ^ xr)) * 2 + (c ^ cr)) * F + lax.rem(f - t + F, F)).astype(I32)

    unit_s = np.repeat(np.arange(A), 2).astype(np.int32)
    unit_x = np.tile(np.arange(2), A).astype(np.int32)
    unit_start = (lax.rem(a - unit_s + A, A) * 2 + (x ^ unit_x)) * (2 * local) + c * local
    sc = jnp.concatenate([jnp.stack([c, (a * 2 + x) * 2 * local]), unit_start]).astype(I32)
    tab = jnp.concatenate([table_start[0], support_count[0], query_count[0]])
    q_order = [(cr, t, xr, s) for cr in range(2) for t in range(F) for xr in range(2) for s in range(A)]
    parts = [slice(0, A // 2), slice(A // 2, A)]
    m_order = [(cr, 0, xr, s) for xr in range(2) for cr in range(2) for s in range(A)]
    m_order += [(cr, t, 0, s) for cr in range(2) for t in range(1, F) for s in range(A)]
    m_order += [
        (cr, t, 1, s) for cr in range(2) for half in parts for t in range(1, F) for s in list(range(A))[half]
    ]
    every_owner = owners(q_order + m_order)
    q_owner, m_owner = every_owner[:count], every_owner[count:]
    if aligned:
        q_idx, idx = q_owner, jnp.concatenate([m_owner, q_owner])
    else:
        q_idx, idx = jnp.zeros((1,), I32), jnp.zeros((2,), I32)
    sc, tab, q_idx, idx = together(sc, tab, q_idx, idx)

    near = sorted(range(1, A), key=lambda s: min(s, A - s))
    order = [0] + near
    own = tokens[0]
    vectors = [
        v.reshape(1, -1)
        for v in (
            norm1_gain, norm1_bias, query_bias, value_bias, out_bias, norm2_gain, norm2_bias, down_bias, up_bias
        )
    ]
    wide = 3 * width + HEAD_DIM
    pack_in = [after(w_qkv, sc, tab, q_idx, idx), w_out, w_up, w_down, *vectors]
    q_own, m_own = pl.pallas_call(
        pack_body,
        grid=(1,),
        out_shape=[sds((4, part, width), BF), sds((1 + 2 * blocks, part, width), BF)],
        in_specs=[pl.BlockSpec(v.shape, lambda i: (0, 0)) for v in pack_in],
        out_specs=[VMEM] * 2,
        scratch_shapes=[pltpu.VMEM((HEAD_DIM, HEAD_DIM), F32)],
        compiler_params=pltpu.CompilerParams(vmem_limit_bytes=56 * MIB),
        cost_estimate=pl.CostEstimate(flops=0, bytes_accessed=16 * part * width, transcendentals=0),
        name="pack",
    )(*pack_in)
    *q_z, own_x, tok_first = together(
        *(turn_a(q_own, s) for s in range(1, A)), swap_x(own), turn_a(own, near[0])
    )
    q_z = jnp.stack([q_own] + q_z)
    moved = [swap_x(q_z)] + [v for t in range(1, F) for v in (turn_f(q_z, t), turn_xf(q_z, t))]
    moved += [turn_a(after(own, tok_first), s) for s in near[1:]]
    moved = together(*moved)
    q_far, tok_z = list(moved[: 2 * F - 1]), jnp.stack([tok_first, *moved[2 * F - 1 :]])
    m_start = after(m_own, tok_z)
    tok_x = swap_x(tok_z)
    m_z = [turn_a(m_start, s) for s in range(1, A)]
    q_four = jnp.stack([q_z] + q_far)
    q_other = swap_c(q_four)
    q_pieces = [q_four.reshape(count // 2, 4, part, width), q_other.reshape(count // 2, 4, part, width)]
    if not aligned:
        stacked = jnp.concatenate(q_pieces)
        by_owner = jnp.zeros_like(stacked).at[q_owner].set(stacked)
        q_pieces = [by_owner.transpose(1, 0, 2, 3).reshape(1, 4, width, width)]
    key_shape = (2 * HEADS, local, HEAD_DIM)
    w_all, row_vec, col_vec, up_row, kv_own, n_own, q, kv_z, n_z = call(
        functools.partial(ready_body, rows=rows, count=len(q_pieces), part=part),
        [
            sds((3, width, width), BF), sds((16, width), F32), sds((width, HEAD_DIM), F32), sds((blocks, width), F32),
            sds((2,) + key_shape, BF), sds((2, local, width), BF), sds((HEADS, local, HEAD_DIM), BF),
            sds((A - 1,) + key_shape, BF), sds((A - 1, local, width), BF),
        ],
        [q_idx, *q_pieces, own, own_x, tok_z], [SMEM] + [HBM] * len(q_pieces) + [VMEM] * 3, [VMEM] * 9,
        scratch=[pltpu.VMEM((width, HEAD_DIM), BF), pltpu.SemaphoreType.DMA((2,))],
        flops=4 * (A + 1) * local * width * width, moved=4 * width * wide, vmem=12, name="ready",
    )

    q_other = swap_c(q)
    *m_z, tok_x, kv_z = together(*m_z, tok_x, kv_z)
    m_z = stack([m_own] + m_z)
    m_x, m_f = swap_x(m_z), [turn_f(m_z, t) for t in range(1, F)]
    m_c = swap_c(m_z)
    kv_x, n_x = call(
        functools.partial(project_body, with_q=False, spots=[(0, i) for i in range(A - 1)], count=1),
        [sds((A - 1,) + key_shape, BF), sds((A - 1, local, width), BF)],
        [after(tok_x, m_z), w_all, row_vec], [VMEM] * 3, [VMEM] * 2,
        flops=4 * (A - 1) * local * width * width, moved=8 * (A - 1) * local * width, vmem=8, name="project",
    )
    where = {0: ((kv_own, kv_own, 0, 1), (n_own, n_own, 0, 1))}
    for i, s in enumerate(near):
        where[s] = ((kv_z, kv_x, i, i), (n_z, n_x, i, i))
    kv_pieces = [kv_own, kv_z, kv_x]
    kv_units = [0, 1] + [2 * s for s in near] + [2 * s + 1 for s in near]

    unit = 2 * local
    work = 4 * unit * A * unit * width
    packet = width + HEAD_DIM
    att_keep, att_send, q_chip = call(
        functools.partial(attend_body, kv_units=kv_units),
        [sds((local, packet), F32)] * 2 + [sds((HEADS, unit, HEAD_DIM), BF)],
        [sc, tab, q, q_other, *kv_pieces], [SMEM, SMEM, VMEM, VMEM] + [ANY] * 3, [VMEM] * 3,
        scratch=[
            pltpu.VMEM((2 * A, HEADS, unit, local), F32),
            pltpu.VMEM((HEADS, unit, HEAD_DIM), F32), pltpu.VMEM((HEADS, unit, 2 * HEAD_DIM), F32),
            pltpu.VMEM((2 * A, 2 * HEADS, local, HEAD_DIM), BF), pltpu.SemaphoreType.DMA((2 * A,)),
        ],
        flops=work, moved=8 * A * unit * width, trans=HEADS * unit * A * unit, vmem=4 + 6 * A, name="attend",
    )
    att_keep, att_send, m_x, m_c, *m_f = together(att_keep, att_send, m_x, m_c, *m_f)
    half_shape = (A // 2,) + m_z.shape[1:]
    halves = copy_out(
        [m_x, *m_f], [half_shape] * F, [(0, (parts[0],), 0, ())] + [(t, (parts[1],), t, ()) for t in range(1, F)]
    )
    crossed = [turn_f(halves[0], t) for t in range(1, F)] + [swap_x(v) for v in halves[1:]]
    att_other, *crossed = together(swap_c(att_send), *crossed)
    m_arrays = [m_z, m_c, m_x, swap_c(m_x), *m_f, *(swap_c(v) for v in m_f), *crossed, *(swap_c(v) for v in crossed)]
    if not aligned:
        stacked = jnp.concatenate(m_arrays)
        by_owner = jnp.zeros_like(stacked).at[m_owner].set(stacked)
        m_arrays = [
            jnp.concatenate(
                [
                    by_owner[:, 0].reshape(1, width, width),
                    by_owner[:, 1 : 1 + blocks].transpose(1, 0, 2, 3).reshape(blocks, width, width),
                    by_owner[:, 1 + blocks :].reshape(blocks, width, width),
                ]
            )[None]
        ]

    spots = [(t, xr) for t in range(F) for xr in range(2)]
    grad_count = 4 * F if aligned else 1
    g_shape = sds((pieces // grad_count, 1 + 2 * blocks, rows, width), BF)
    got = call(
        functools.partial(middle_body, rows=rows, m_count=len(m_arrays), grad_count=grad_count),
        [
            sds((local, width), BF), sds((local, width), F32), sds((local, packet), BF), sds((HEADS, unit), F32),
            sds((width, HEAD_DIM), F32),
        ] + [g_shape] * grad_count,
        [idx, sc, tab, *m_arrays, own, att_keep, att_other, cotangent[0], row_vec, up_row],
        [SMEM] * 3 + [HBM] * len(m_arrays) + [VMEM] * 6,
        [VMEM] * 5 + [HBM] * grad_count,
        scratch=[
            pltpu.VMEM((width, width), BF), pltpu.VMEM((blocks, width, width), BF),
            pltpu.VMEM((pieces * blocks, rows, width), BF),
            pltpu.VMEM((width, width), BF), pltpu.VMEM((blocks, width, width), BF),
            pltpu.VMEM((pieces * blocks, rows, width), BF), pltpu.VMEM((blocks, local, width), F32),
            pltpu.SemaphoreType.DMA((3,)), pltpu.SemaphoreType.DMA,
        ],
        flops=6 * local * width * width * (1 + 2 * blocks), moved=4 * width * width * (1 + 2 * blocks),
        trans=local * hidden, vmem=50, name="middle",
    )
    outputs, d_middle, d_own, lse, vec = got[:5]
    grads = got[5:]
    d_other = swap_c(d_own)

    lead = (A, 1 + 2 * blocks, part, width)
    if aligned:
        relative = [g.reshape(lead) for g in grads]
    else:
        whole = grads[0][0]
        by_owner = jnp.concatenate(
            [
                whole[0].reshape(count, 1, part, width),
                whole[1 : 1 + blocks].reshape(blocks, count, part, width).transpose(1, 0, 2, 3),
                whole[1 + blocks :].reshape(count, blocks, part, width),
            ],
            axis=1,
        )
        by_owner = by_owner[q_owner].reshape((4 * F,) + lead)
        relative = [by_owner[i] for i in range(4 * F)]
    g_near = {spot: relative[i] for i, spot in enumerate(spots)}
    g_far = {spot: swap_c(after(relative[2 * F + i], d_other)) for i, spot in reversed(list(enumerate(spots)))}

    def through_f(xr, half):
        return [
            turn_f(add_up([g_near[t, xr], g_far[t, xr]], [[(0, (half,)), (1, (half,))]])[0], F - t)
            for t in range(1, F)
        ]

    def g_kept(xr, half):
        arrays = [g_near[0, xr], g_far[0, xr], *g_y[xr, half]]
        return arrays, [(0, (half,)), (1, (half,))] + [(2 + i, ()) for i in range(F - 1)]

    carried, d_all = [], []
    d_x, d_z, d_keep, d_send = {}, {}, {}, {}
    g_y, g_x = {}, {}
    back_order = near[:-1][::-1] + near[-1:] + [0]
    q_now = q_chip
    steps = len(back_order)
    y_parts = [(xr, half) for xr in (1, 0) for half in parts]
    for step, s in enumerate(back_order):
        kv_at, n_at = where[s]
        if step:
            ins = [sc, tab, q_now, *d_all, lse, *kv_at[:2], *n_at[:2], w_all, *carried]
            body = back_body
        else:
            ins = [sc, tab, q_now, d_own, d_other, lse, *kv_at[:2], *n_at[:2], w_all]
            body = first_back_body
        dq_shape = sds((HEADS, HEAD_DIM, local), F32)
        shapes = [
            sds((local, width), BF), sds((local, width), BF), dq_shape, dq_shape,
            sds((width, 2 * width), F32), sds((8, 2 * width), F32),
        ]
        if not step:
            shapes += [sds((HEADS, unit, HEAD_DIM), BF), sds((HEADS, unit), F32)]
        outs = call(
            functools.partial(body, plane=s, spots=kv_at[2:]), shapes, ins,
            [SMEM, SMEM] + [VMEM] * (len(ins) - 2), [VMEM] * len(shapes),
            scratch=[pltpu.VMEM((2, local, 2 * width), BF)],
            flops=work // A * 5 // 2 + 8 * unit * width * width, moved=16 * unit * width,
            trans=HEADS * unit * unit, name="back",
        )
        if step == 0:
            keys = list(g_far)
            got = together(*outs, *(g_far[k] for k in keys))
            outs, d_all = got[:6], got[6:8]
            g_far = dict(zip(keys, got[8:], strict=True))
        else:
            prev = back_order[step - 1]
            beside = {("x", prev): swap_x(d_send[prev])}
            if step >= 2:
                older = back_order[step - 2]
                beside["z", older] = turn_a(d_sum, A - older)
            if step - 1 < len(y_parts):
                for i, v in enumerate(through_f(y_parts[step - 1][0], y_parts[step - 1][1])):
                    beside["y", step - 1, i] = v
            keys = list(beside)
            got = together(*outs, *beside.values())
            outs = got[:6]
            beside = dict(zip(keys, got[6:], strict=True))
            for key, v in beside.items():
                if key[0] == "x":
                    d_x[key[1]] = v
                elif key[0] == "z":
                    d_z[key[1]] = v
                else:
                    g_y[y_parts[key[1]]] = g_y.get(y_parts[key[1]], []) + [v]
            (d_sum,) = add_up([d_keep[prev], d_x[prev]], [[(0, ()), (1, ())]])
        d_keep[s], d_send[s], *carried = outs
        q_now = after(q_chip, outs[2])
        if step:
            q_now = after(q_now, d_sum)

    last_plane = back_order[-2]
    for k in range(steps - 1, len(y_parts)):
        g_y[y_parts[k]] = through_f(*y_parts[k])
    d_z[last_plane] = turn_a(d_sum, A - last_plane)
    dq_own, dq_other, n_product, sums = carried
    dq_recv = swap_c(dq_other)

    half_count = 2 * F
    msg_lead = (A, part, wide)
    msg_shape = [sds((pieces // 2, rows, wide), BF)] * 2 if aligned else [sds((1, rows, wide), BF)]
    dq_low, *message = call(
        functools.partial(message_body, rows=rows),
        [sds((local, width), BF), *msg_shape],
        [q_idx, n_own, dq_own, dq_recv, n_product, sums, w_all, col_vec, vec],
        [SMEM] + [VMEM] * 8, [VMEM] * (1 + len(msg_shape)),
        scratch=[pltpu.VMEM((width, wide), BF), pltpu.VMEM((width, HEAD_DIM), F32)],
        flops=2 * local * width * width, moved=8 * width * wide, vmem=8, name="message",
    )
    if not aligned:
        flat = message[0][0]
        at = slice(3 * width + 4, 3 * width + 4 + blocks)
        up_part = flat[:, at].T.reshape(count, blocks, part)
        by_owner = flat.reshape(count, part, wide)
        by_owner = by_owner.at[:, :, at].set(up_part.transpose(0, 2, 1))
        by_owner = by_owner[q_owner]
        message = [by_owner[: count // 2], by_owner[count // 2 :]]
    w_far = swap_c(message[1])
    arrays = [g_near[0, 1], g_far[0, 1], *g_y[1, parts[0]], *g_y[1, parts[1]]]
    lows = [(0, (parts[0],)), (1, (parts[0],))] + [(2 + i, ()) for i in range(F - 1)]
    highs = [(0, (parts[1],)), (1, (parts[1],))] + [(1 + F + i, ()) for i in range(F - 1)]
    (g_x_send,) = join_up(arrays, [lows, highs])
    g_x_all = swap_x(g_x_send)
    w_far = w_far.reshape((half_count,) + msg_lead)
    w_near = message[0].reshape((half_count,) + msg_lead)
    w_both = add_up([w_near, w_far], [[(0, (i,)), (1, (i,))] for i in range(half_count)])
    got = []
    for (t, xr), sent in zip(spots, w_both, strict=True):
        if xr:
            sent = turn_xf(sent, F - t) if t else swap_x(sent)
        elif t:
            sent = turn_f(sent, F - t)
        got.append(sent)
    got[0], d_z[last_plane] = together(got[0], d_z[last_plane])
    d_x[0] = swap_x(after(d_send[0], got[0]))
    w_z = add_up(got, [[(i, (s,)) for i in range(len(got))] for s in near])
    (w_own,) = add_up(got, [[(i, (0,)) for i in range(len(got))]], F32)
    w_z = [turn_a(v, A - s) for s, v in zip(near, w_z, strict=True)]
    grad_qkv, last = call(
        unpack_body, [sds((part, 3 * width), F32), sds((part, HEAD_DIM), F32)], [w_own, *w_z],
        [VMEM] * A, [VMEM] * 2, moved=16 * part * width, vmem=8, name="unpack",
    )

    g_z_send, g_mine = {}, None
    for half in parts:
        arrays, terms = g_kept(0, half)
        arrays.append(g_x_all)
        planes = list(range(A))[half]

        def one(s, terms=terms, start=half.start, last=len(arrays) - 1):
            out = [(i, (start + s,) if spot else (s,)) for i, spot in terms]
            return out + [(last, (start + s,))]

        for s, v in zip(planes, add_up(arrays, [one(s - half.start) for s in planes]), strict=True):
            if s:
                g_z_send[s] = v
            else:
                g_mine = v
    g_z_send = [g_z_send[s] for s in near]
    g_z = [turn_a(v, A - s) for s, v in zip(near, g_z_send, strict=True)]
    grad_out, grad_up, grad_down = call(
        matrices_body,
        [sds((part, width), F32), sds((part, hidden), F32), sds((blocks * part, width), F32)],
        [g_mine, *g_z], [VMEM] * A, [VMEM] * 3, moved=6 * A * g_mine.size, vmem=8, name="matrices",
    )
    grad_tokens = call(
        finish_body, sds((local, width), BF),
        [own, d_middle, row_vec, dq_low, w_all, d_keep[0], d_x[0], *(d_z[s] for s in near)],
        [VMEM] * (6 + A), VMEM, flops=20 * local * width, moved=16 * local * width, vmem=8, name="finish",
    )
    return (
        outputs[None],
        grad_tokens[None],
        grad_qkv,
        grad_out,
        grad_up,
        grad_down,
        last[:, 8],
        last[:, 9],
        last[:, 10],
        last[:, 11],
        last[:, 0],
        last[:, 1],
        last[:, 2],
        last[:, 4 : 4 + blocks].T.reshape(blocks * part),
        last[:, 3],
    )


def solution(mesh):
    both = ("rows", "fsdp")
    matrix, vector, act, table = P(both, None), P(both), P("fsdp", "rows", None), P("fsdp", None)
    return jax.shard_map(
        functools.partial(shards, R=mesh.shape["rows"], F=mesh.shape["fsdp"]),
        mesh=mesh,
        in_specs=(act,) + (matrix,) * 4 + (vector,) * 9 + (act,) + (table,) * 3,
        out_specs=(act, act) + (matrix,) * 4 + (vector,) * 9,
        check_vma=False,
    )
```

```python
import functools
import math

import jax
import jax.numpy as jnp
import numpy as np
from jax import lax
from jax.experimental import pallas as pl
from jax.experimental.pallas import tpu as pltpu
from jax.sharding import PartitionSpec as P

HEADS = 4
HEAD_DIM = 128
EPS = 1e-05
NEG = -1e30
PLANE = 4
MIB = 1024 * 1024
BF = jnp.bfloat16
F32 = jnp.float32
I32 = jnp.int32
SCALE = 1.0 / math.sqrt(HEAD_DIM)
SCALE2 = SCALE * math.log2(math.e)
GELU_A = math.sqrt(2.0 / math.pi)
GELU_B = 0.044715

VMEM = pl.BlockSpec(memory_space=pltpu.VMEM)
SMEM = pl.BlockSpec(memory_space=pltpu.SMEM)
HBM = pl.BlockSpec(memory_space=pltpu.HBM)
ANY = pl.BlockSpec(memory_space=pl.ANY)


def after(value, *others):
    return lax.optimization_barrier((value, *others))[0]


def together(*values):
    return lax.optimization_barrier(values)


def mm(left, right):
    return jnp.dot(left, right, preferred_element_type=F32)


def mm_nt(left, right):
    return lax.dot_general(left, right, (((1,), (1,)), ((), ())), preferred_element_type=F32)


def mm_tn(left, right):
    return lax.dot_general(left, right, (((0,), (0,)), ((), ())), preferred_element_type=F32)


def call(body, outs, ins, in_specs, out_specs, scratch=(), flops=0, moved=0, trans=0, vmem=16, name=None):
    return pl.pallas_call(
        body,
        out_shape=outs,
        in_specs=in_specs,
        out_specs=out_specs,
        scratch_shapes=scratch,
        compiler_params=pltpu.CompilerParams(vmem_limit_bytes=vmem * MIB),
        cost_estimate=pl.CostEstimate(
            flops=int(flops), bytes_accessed=int(moved), transcendentals=int(trans)
        ),
        name=name,
    )(*ins)


def normalize(values):
    centre = values - jnp.mean(values, axis=-1, keepdims=True)
    spread = jnp.mean(centre * centre, axis=-1, keepdims=True)
    inverse = lax.rsqrt(spread + EPS)
    return centre * inverse, inverse


def norm_back(grad_out, plain, inverse, gain):
    scaled = grad_out * gain
    return inverse * (
        scaled
        - jnp.mean(scaled, axis=-1, keepdims=True)
        - plain * jnp.mean(scaled * plain, axis=-1, keepdims=True)
    )


def table_of(tab, count, pos):
    low = jnp.zeros_like(pos) + tab[0]
    high = low + tab[count]
    finish = high + tab[2 * count]
    for t in range(1, count):
        here = pos >= tab[t]
        top = tab[t] + tab[count + t]
        low = jnp.where(here, tab[t], low)
        high = jnp.where(here, top, high)
        finish = jnp.where(here, top + tab[2 * count + t], finish)
    return low, high, finish


def pack_body(qkv_ref, out_ref, up_ref, down_ref, *refs):
    vec_refs, (q_ref, m_ref, vec_scr) = refs[:-3], refs[-3:]
    part, width = out_ref.shape
    blocks = up_ref.shape[1] // width
    vec_scr[...] = jnp.zeros(vec_scr.shape, F32)
    for k, ref in enumerate(vec_refs[:-1]):
        vec_scr[k : k + 1, :part] = ref[...].astype(F32)
    for j in range(blocks):
        vec_scr[8 + j : 9 + j, :part] = vec_refs[-1][:, j * part : (j + 1) * part].astype(F32)
    for i in range(3):
        q_ref[i] = qkv_ref[:, i * width : (i + 1) * width]
    q_ref[3] = jnp.zeros((part, width), BF)
    q_ref[3, :, :HEAD_DIM] = jnp.transpose(vec_scr[...])[:part].astype(BF)
    m_ref[0] = out_ref[...]
    for j in range(blocks):
        m_ref[1 + j] = up_ref[:, j * width : (j + 1) * width]
        m_ref[1 + blocks + j] = down_ref[j * part : (j + 1) * part, :]


def sum_body(*refs, plan, count):
    for out_ref, terms in zip(refs[count:], plan, strict=True):
        total = None
        for which, spot in terms:
            term = refs[which][spot].astype(F32)
            total = term if total is None else total + term
        out_ref[...] = total.astype(out_ref.dtype)


def join_body(*refs, plan, count):
    out_ref, row = refs[count], 0
    for terms in plan:
        total = None
        for which, spot in terms:
            term = refs[which][spot].astype(F32)
            total = term if total is None else total + term
        out_ref[row : row + total.shape[0]] = total.astype(out_ref.dtype)
        row += total.shape[0]


def join_up(arrays, plan):
    shapes = [jax.eval_shape(lambda v: v[terms[0][1]], arrays[terms[0][0]]).shape for terms in plan]
    shape = (sum(v[0] for v in shapes),) + shapes[0][1:]
    moved = math.prod(shape) * 4
    return call(
        functools.partial(join_body, plan=plan, count=len(arrays)), [jax.ShapeDtypeStruct(shape, BF)], arrays,
        [VMEM] * len(arrays), [VMEM], flops=moved, moved=moved, vmem=16, name="join",
    )


def add_up(arrays, plan, dtype=BF):
    outs = []
    for terms in plan:
        which, spot = terms[0]
        outs.append(jax.ShapeDtypeStruct(jax.eval_shape(lambda v: v[spot], arrays[which]).shape, dtype))
    moved = sum(o.size for o in outs) * 4
    return call(
        functools.partial(sum_body, plan=plan, count=len(arrays)), outs, arrays,
        [VMEM] * len(arrays), [VMEM] * len(outs), flops=moved, moved=moved, vmem=16, name="add",
    )


def copy_body(*refs, plan, count):
    outs, sem = refs[count:-1], refs[-1]
    copies = []
    for k, (which, source, out, spot) in enumerate(plan):
        copies.append(pltpu.make_async_copy(refs[which].at[source], outs[out].at[spot], sem.at[k]))
        copies[-1].start()
    for copy in copies:
        copy.wait()


def copy_out(arrays, shapes, plan):
    moved = sum(math.prod(shape) for shape in shapes) * 4
    return call(
        functools.partial(copy_body, plan=plan, count=len(arrays)),
        [jax.ShapeDtypeStruct(shape, arrays[0].dtype) for shape in shapes], arrays,
        [HBM] * len(arrays), [VMEM] * len(shapes),
        scratch=[pltpu.SemaphoreType.DMA((len(plan),))], moved=moved, vmem=4, name="copy",
    )


def stack(arrays):
    shape = (len(arrays),) + arrays[0].shape
    every = (slice(None),)
    (out,) = copy_out(arrays, [shape], [(i, every, 0, (i,)) for i in range(len(arrays))])
    return out


def assemble_body(idx, *refs, rows, count):
    pieces, (w_ref, row_ref, col_ref, low_scr, sem) = refs[:count], refs[count:]
    k = 0
    for piece in pieces:
        for j in range(piece.shape[0]):
            at = pl.ds(pl.multiple_of(idx[k] * rows, rows), rows)
            pltpu.make_async_copy(piece.at[j, pl.ds(0, 3)], w_ref.at[:, at, :], sem.at[0]).start()
            pltpu.make_async_copy(piece.at[j, 3, :, pl.ds(0, HEAD_DIM)], low_scr.at[at, :], sem.at[1]).start()
            k += 1
    pltpu.make_async_copy(low_scr, low_scr, sem.at[1]).wait()
    columns = low_scr[...].astype(F32)
    col_ref[...] = columns
    row_ref[...] = jnp.transpose(columns)[: row_ref.shape[0]]
    pltpu.make_async_copy(w_ref, w_ref, sem.at[0]).wait()


def project_body(*refs, with_q, spots, count):
    pieces, (w_ref, row_ref), outs = refs[:count], refs[count : count + 2], refs[count + 2 :]
    kv_ref, n_ref = outs[:2]
    gain, shift = row_ref[0:1, :], row_ref[1:2, :]
    for i, (which, lead) in enumerate(spots):
        plain, unused_inverse = normalize(pieces[which][lead].astype(F32))
        n_ref[i] = plain.astype(BF)
        normed = (plain * gain + shift).astype(BF)
        keys = mm(normed, w_ref[1])
        values = mm(normed, w_ref[2]) + row_ref[3:4, :]
        for h in range(HEADS):
            lanes = slice(h * HEAD_DIM, (h + 1) * HEAD_DIM)
            kv_ref[i, h] = keys[:, lanes].astype(BF)
            kv_ref[i, HEADS + h] = values[:, lanes].astype(BF)
        if with_q and i == 0:
            queries = (mm(normed, w_ref[0]) + row_ref[2:3, :]) * SCALE2
            for h in range(HEADS):
                outs[2][h] = queries[:, h * HEAD_DIM : (h + 1) * HEAD_DIM].astype(BF)


def ready_body(idx, *refs, rows, count, part):
    pieces, (own_ref, own_x_ref, tok_ref) = refs[:count], refs[count : count + 3]
    w_ref, row_ref, col_ref, up_ref, kv_own, n_own, q_ref, kv_z, n_z, n_first, low_scr, sem = refs[count + 3 :]
    assemble_body(idx, *pieces, w_ref, row_ref, col_ref, low_scr, sem, rows=rows, count=count)
    width = up_ref.shape[1]
    blocks = up_ref.shape[0]
    per = width // blocks
    source = lax.broadcasted_iota(I32, (per, width), 0)
    target = lax.broadcasted_iota(I32, (per, width), 1)
    total = jnp.zeros((blocks, width), F32)
    for k in range(blocks):
        spread = jnp.where(
            target == (source // part) * (blocks * part) + k * part + lax.rem(source, part), 1.0, 0.0
        ).astype(BF)
        mine = [row_ref[8 + k : 9 + k, j * per : (j + 1) * per] for j in range(blocks)]
        total += mm(jnp.concatenate(mine, axis=0).astype(BF), spread)
    up_ref[...] = total
    every = slice(None)
    project_body(
        own_ref, own_x_ref, w_ref, row_ref, kv_own, n_own, q_ref, with_q=True, spots=[(0, every), (1, every)], count=2
    )
    n_first[0] = n_own[0]
    spots = [(0, i) for i in range(tok_ref.shape[0])]
    project_body(tok_ref, w_ref, row_ref, kv_z, n_z, with_q=False, spots=spots, count=1)


def reach(sc, tab, rows):
    count = tab.shape[0] // 3
    min_low, min_high, unused = table_of(tab, count, sc[1])
    max_low, max_high, unused = table_of(tab, count, sc[1] + 2 * rows - 1)
    return min_low, max_high, max_low, min_high


def chip_rows(sc, rows, shape, dim):
    spot = lax.broadcasted_iota(I32, shape, dim) + sc[0] * rows
    return sc[1] + jnp.where(spot >= 2 * rows, spot - 2 * rows, spot)


def attend_body(sc, tab, q_own, q_other, *refs, kv_units):
    kv_refs, (keep_ref, send_ref, q_scr, s_scr, m_scr, acc_scr, kv_ref, sem) = refs[:-8], refs[-8:]
    count = tab.shape[0] // 3
    units, unused, rows, unused = kv_ref.shape
    k = 0
    for ref in kv_refs:
        for i in range(ref.shape[0]):
            pltpu.make_async_copy(ref.at[i], kv_ref.at[kv_units[k]], sem.at[kv_units[k]]).start()
            k += 1
    min_low, max_high, max_low, min_high = reach(sc, tab, rows)
    q_pos = chip_rows(sc, rows, (2 * rows, 1), 0)
    low, high, unused = table_of(tab, count, q_pos)
    ones = jnp.ones((rows, HEAD_DIM), BF)
    q_scr[:, :rows] = q_own[...]
    q_scr[:, rows:] = q_other[...]
    m_scr[...] = jnp.full(m_scr.shape, NEG, F32)
    acc_scr[...] = jnp.zeros(acc_scr.shape, F32)

    def keep_scores(u, allowed):
        for h in range(HEADS):
            scores = mm_nt(q_scr[h], kv_ref[u, h])
            if allowed is not None:
                scores = jnp.where(allowed, scores, NEG)
            s_scr[u, h] = scores
            top = m_scr[h]
            for j in range(rows // HEAD_DIM):
                top = jnp.maximum(top, scores[:, j * HEAD_DIM : (j + 1) * HEAD_DIM])
            m_scr[h] = top

    def score_step(u, carry):
        start = sc[2 + u]

        pltpu.make_async_copy(kv_refs[0].at[0], kv_ref.at[u], sem.at[u]).wait()
        needed = (start < max_high) & (start + rows > min_low)
        whole = (start >= max_low) & (start + rows <= min_high)

        @pl.when(needed & whole)
        def _():
            keep_scores(u, None)

        @pl.when(needed & jnp.logical_not(whole))
        def _():
            k_pos = start + lax.broadcasted_iota(I32, (1, rows), 1)
            keep_scores(u, (k_pos >= low) & (k_pos < high))

        return carry

    lax.fori_loop(0, units, score_step, 0)
    for h in range(HEADS):
        top = jnp.max(m_scr[h], axis=-1, keepdims=True)
        m_scr[h] = jnp.broadcast_to(jnp.where(top > 0.5 * NEG, top, 0.0), m_scr.shape[1:])

    def value_step(u, carry):
        start = sc[2 + u]
        needed = (start < max_high) & (start + rows > min_low)

        @pl.when(needed)
        def _():
            for h in range(HEADS):
                soft = jnp.exp2(s_scr[u, h] - m_scr[h][:, :1]).astype(BF)
                wide = jnp.concatenate([kv_ref[u, HEADS + h], ones], axis=1)
                acc_scr[h] += mm(soft, wide)

        return carry

    lax.fori_loop(0, units, value_step, 0)
    lane = lax.broadcasted_iota(I32, (1, HEAD_DIM), 1)
    width = HEADS * HEAD_DIM
    mine = jnp.zeros((rows, HEAD_DIM), F32)
    theirs = mine
    for h in range(HEADS):
        lanes = slice(h * HEAD_DIM, (h + 1) * HEAD_DIM)
        total = acc_scr[h, :, HEAD_DIM:]
        some = total > 0.0
        mixed = acc_scr[h, :, :HEAD_DIM] / jnp.where(some, total, 1.0)
        log_total = jnp.where(some, m_scr[h] + jnp.log2(jnp.where(some, total, 1.0)), NEG)
        keep_ref[:, lanes] = mixed[:rows]
        send_ref[:, lanes] = mixed[rows:]
        mine = jnp.where(lane == h, log_total[:rows], jnp.where(lane == HEADS + h, log_total[rows:], mine))
        theirs = jnp.where(lane == h, log_total[rows:], jnp.where(lane == HEADS + h, log_total[:rows], theirs))
    keep_ref[:, width:] = mine
    send_ref[:, width:] = theirs


def middle_body(idx, sc, tab, *refs, rows, m_count, grad_count):
    m_refs, (tok_ref, own_ref, other_ref, cot_ref, row_ref, up_row_ref) = refs[:m_count], refs[m_count : m_count + 6]
    outs = refs[m_count + 6 :]
    out_ref, dmid_ref, d_ref, lse_ref, vec_ref = outs[:5]
    g_refs = outs[5 : 5 + grad_count]
    (w_out, w_up, w_down, g_out, g_up, g_down, dh_scr, sem, g_sem) = outs[5 + grad_count :]
    blocks, width = w_up.shape[0], w_up.shape[2]
    pieces = w_down.shape[0] // blocks
    count = tab.shape[0] // 3
    local = tok_ref.shape[0]
    spots = []
    for m_ref in m_refs:
        for spot in range(m_ref.shape[0]):
            owner = idx[len(spots)]
            spots.append(
                (m_ref, spot, pl.ds(pl.multiple_of(owner * rows, rows), rows), pl.ds(owner * blocks, blocks))
            )
    for m_ref, spot, at, unused in spots:
        pltpu.make_async_copy(m_ref.at[spot, 0], w_out.at[at, :], sem.at[0]).start()
    for m_ref, spot, unused, at in spots:
        pltpu.make_async_copy(m_ref.at[spot, pl.ds(1 + blocks, blocks)], w_down.at[at], sem.at[2]).start()
    for m_ref, spot, at, unused in spots:
        pltpu.make_async_copy(m_ref.at[spot, pl.ds(1, blocks)], w_up.at[:, at, :], sem.at[1]).start()

    pos = sc[1] + sc[0] * local + lax.broadcasted_iota(I32, (local, 1), 0)
    unused_low, unused_high, finish = table_of(tab, count, pos)
    live = (pos < finish).astype(F32)
    gain, shift = row_ref[5:6, :], row_ref[6:7, :]
    lane = lax.broadcasted_iota(I32, (1, HEAD_DIM), 1)
    lse_own, lse_other = own_ref[:, width:], other_ref[:, width:]
    top = jnp.maximum(lse_own, lse_other)
    share_own, share_other = jnp.exp2(lse_own - top), jnp.exp2(lse_other - top)
    share = share_own + share_other
    log_total = jnp.transpose(top + jnp.log2(share))
    lse_ref[...] = jnp.concatenate([log_total[:HEADS], log_total[HEADS : 2 * HEADS]], axis=1)
    share_own, share_other = share_own / share, share_other / share
    mixed = []
    for h in range(HEADS):
        lanes = slice(h * HEAD_DIM, (h + 1) * HEAD_DIM)
        mixed.append(own_ref[:, lanes] * share_own[:, h : h + 1] + other_ref[:, lanes] * share_other[:, h : h + 1])
    mixed = jnp.concatenate(mixed, axis=1)
    attended = (mixed * live).astype(BF)
    cot = cot_ref[...]
    pltpu.make_async_copy(w_out, w_out, sem.at[0]).wait()
    middle = tok_ref[...].astype(F32) + mm(attended, w_out[...]) + row_ref[4:5, :]
    pltpu.make_async_copy(w_down, w_down, sem.at[2]).wait()
    for j in range(blocks):
        dh_scr[j] = mm_nt(cot, w_down[j * pieces : (j + 1) * pieces].reshape(width, width))
    plain, inverse = normalize(middle)
    normed = (plain * gain + shift).astype(BF)
    pltpu.make_async_copy(w_up, w_up, sem.at[1]).wait()
    total = middle + row_ref[7:8, :]
    d_norm = jnp.zeros(middle.shape, F32)
    ones = jnp.ones((8, local), BF)
    up_sums = []
    for j in range(blocks):
        up = w_up[j]
        down = w_down[j * pieces : (j + 1) * pieces].reshape(width, width)
        pre = mm(normed, up) + up_row_ref[j : j + 1, :]
        square = pre * pre
        t = jnp.tanh(GELU_A * pre * (1.0 + GELU_B * square))
        half = 0.5 * (1.0 + t)
        hidden = (pre * half).astype(BF)
        slope = half + 0.5 * pre * (1.0 - t * t) * (GELU_A * (1.0 + 3.0 * GELU_B * square))
        total = total + mm(hidden, down)
        d_pre = (dh_scr[j] * slope).astype(BF)
        d_norm = d_norm + mm_nt(d_pre, up)
        g_down[j * pieces : (j + 1) * pieces] = mm_tn(hidden, cot).astype(BF).reshape(pieces, rows, width)
        g_up[j] = mm_tn(normed, d_pre).astype(BF)
        up_sums.append(mm(ones, d_pre)[0:1])
    g_pieces = g_refs[0].shape[0]
    spots = []
    for i in range(pieces):
        g_ref, spot, where = g_refs[i // g_pieces], i % g_pieces, idx[pieces + i]
        spots.append((g_ref, spot, pl.ds(pl.multiple_of(where * rows, rows), rows)))
        at = pl.ds(where * blocks, blocks)
        pltpu.make_async_copy(g_down.at[at], g_ref.at[spot, pl.ds(1 + blocks, blocks)], g_sem).start()
    for g_ref, spot, at in spots:
        pltpu.make_async_copy(g_up.at[:, at, :], g_ref.at[spot, pl.ds(1, blocks)], g_sem).start()
    out_ref[...] = total.astype(BF)
    cot_f = cot.astype(F32)
    d_middle = cot_f + norm_back(d_norm, plain, inverse, gain)
    dmid_ref[...] = d_middle
    d_branch = d_middle.astype(BF)
    g_out[...] = mm_tn(attended, d_branch).astype(BF)
    for g_ref, spot, at in spots:
        pltpu.make_async_copy(g_out.at[at, :], g_ref.at[spot, 0], g_sem).start()
    d_att = mm_nt(d_branch, w_out[...]).astype(BF) * live.astype(BF)
    d_ref[:, :width] = d_att
    product = d_att.astype(F32) * mixed
    tail = jnp.zeros((local, HEAD_DIM), F32)
    for h in range(HEADS):
        delta = jnp.sum(product[:, h * HEAD_DIM : (h + 1) * HEAD_DIM], axis=-1, keepdims=True)
        high = delta.astype(BF).astype(F32)
        tail = jnp.where(lane == h, high, jnp.where(lane == HEADS + h, delta - high, tail))
    d_ref[:, width:] = tail.astype(BF)

    sums = [jnp.sum(v, axis=0, keepdims=True) for v in (d_middle, d_norm * plain, d_norm, cot_f)]
    sums = jnp.concatenate(sums + up_sums + [jnp.zeros((HEAD_DIM - 4 - blocks, width), F32)], axis=0)
    columns = jnp.transpose(sums)
    if pieces > 1:
        per = pieces // blocks
        vec_ref[...] = jnp.where(lane < 4, columns, 0.0)
        for j in range(blocks):
            column = jnp.broadcast_to(columns[:, 4 + j : 5 + j], (width, HEAD_DIM)).reshape(
                per, blocks, rows, HEAD_DIM
            )
            wide_lane = lane.reshape(1, 1, HEAD_DIM)
            placed = sum(jnp.where(wide_lane == 4 + i, column[:, i], 0.0) for i in range(blocks))
            vec_ref[j * per * rows : (j + 1) * per * rows, :] += placed.reshape(per * rows, HEAD_DIM)
    else:
        vec_ref[...] = jnp.where(lane < 4 + blocks, columns, 0.0)
    for g_ref in g_refs:
        pltpu.make_async_copy(g_ref, g_ref, g_sem).wait()


def back_body(
    sc, tab, q_ref, do_ref, delta_ref, lse_ref, kv_near, kv_far, n_near, n_far, w_ref, own_in, other_in, nk_in, sum_in,
    keep_ref, send_ref, own_ref, other_ref, nk_ref, sum_ref, dkv_scr, *, plane, spots,
):
    count = tab.shape[0] // 3
    unused, unused, rows, unused = kv_near.shape
    width = w_ref.shape[1]
    min_low, max_high, max_low, min_high = reach(sc, tab, rows)
    q_pos = chip_rows(sc, rows, (1, 2 * rows), 1)
    low, high, unused = table_of(tab, count, q_pos)
    if own_in is None:
        own_ref[...] = jnp.zeros(own_ref.shape, F32)
        other_ref[...] = jnp.zeros(other_ref.shape, F32)
    else:
        own_ref[...] = own_in[...]
        other_ref[...] = other_in[...]

    def unit(u, allowed):
        for h in range(HEADS):
            lanes = slice(h * HEAD_DIM, (h + 1) * HEAD_DIM)
            v_lanes = slice(width + h * HEAD_DIM, width + (h + 1) * HEAD_DIM)
            kv_ref, spot = (kv_near, kv_far)[u], spots[u]
            q, do, key = q_ref[h], do_ref[h], kv_ref[spot, h]
            soft = jnp.exp2(mm_nt(key, q) - lse_ref[h : h + 1, :])
            if allowed is not None:
                soft = jnp.where(allowed, soft, 0.0)
            d_soft = mm_nt(kv_ref[spot, HEADS + h], do)
            d_scores = (soft * (d_soft - delta_ref[h : h + 1, :])).astype(BF)
            dkv_scr[u, :, v_lanes] = mm(soft.astype(BF), do).astype(BF)
            dkv_scr[u, :, lanes] = (mm(d_scores, q) * (SCALE / SCALE2)).astype(BF)
            d_query = mm_tn(key, d_scores)
            own_ref[h] += d_query[:, :rows]
            other_ref[h] += d_query[:, rows:]

    for u in range(2):
        start = sc[2 + 2 * plane + u]
        needed = (start < max_high) & (start + rows > min_low)
        whole = (start >= max_low) & (start + rows <= min_high)

        @pl.when(needed & whole)
        def _(u=u):
            unit(u, None)

        @pl.when(needed & jnp.logical_not(whole))
        def _(u=u, start=start):
            k_pos = start + lax.broadcasted_iota(I32, (rows, 1), 0)
            unit(u, (k_pos >= low) & (k_pos < high))

        @pl.when(jnp.logical_not(needed))
        def _(u=u):
            dkv_scr[u] = jnp.zeros(dkv_scr.shape[1:], BF)

    ones = jnp.ones((8, rows), BF)
    for u, ref in enumerate((keep_ref, send_ref)):
        ref[...] = (mm_nt(dkv_scr[u, :, :width], w_ref[1]) + mm_nt(dkv_scr[u, :, width:], w_ref[2])).astype(BF)
    product = mm_tn(n_near[spots[0]], dkv_scr[0]) + mm_tn(n_far[spots[1]], dkv_scr[1])
    sums = mm(ones, dkv_scr[0]) + mm(ones, dkv_scr[1])
    nk_ref[...] = product if nk_in is None else nk_in[...] + product
    sum_ref[...] = sums if sum_in is None else sum_in[...] + sums


def first_back_body(sc, tab, q_ref, d_own, d_other, *refs, **options):
    ins, outs, do_ref, delta_ref, dkv_scr = refs[:6], refs[6:-3], refs[-3], refs[-2], refs[-1]
    rows, width = d_own.shape[0], HEADS * HEAD_DIM
    for i, ref in enumerate((d_own, d_other)):
        for h in range(HEADS):
            do_ref[h, i * rows : (i + 1) * rows] = ref[:, h * HEAD_DIM : (h + 1) * HEAD_DIM]
        tail = jnp.transpose(ref[:, width:].astype(F32))
        delta_ref[:, i * rows : (i + 1) * rows] = tail[:HEADS] + tail[HEADS : 2 * HEADS]
    nothing = [None] * 4
    back_body(sc, tab, q_ref, do_ref, delta_ref, *ins, *nothing, *outs, dkv_scr, **options)


def message_body(idx, n_own, n_other, dq_own, dq_other, nk_ref, sum_ref, w_ref, col_ref, vec_ref, *refs, rows):
    msg_refs, (full, vec) = refs[:-2], refs[-2:]
    local = n_own.shape[1]
    width = w_ref.shape[1]
    q_product = jnp.zeros((width, width), F32)
    q_sums = jnp.zeros((8, width), F32)
    ones = jnp.ones((8, local), BF)
    for n_ref, dq_ref in ((n_own, dq_own), (n_other, dq_other)):
        d_query = jnp.concatenate([dq_ref[h] * SCALE for h in range(HEADS)], axis=0).astype(BF)
        q_product += lax.dot_general(n_ref[0], d_query, (((0,), (1,)), ((), ())), preferred_element_type=F32)
        q_sums += mm_nt(ones, d_query)
    gain, shift = col_ref[:, 0:1], col_ref[:, 1:2]
    lane = lax.broadcasted_iota(I32, (1, HEAD_DIM), 1)
    gain_grad = jnp.zeros((width, 1), F32)
    shift_grad = jnp.zeros((width, 1), F32)
    columns = []
    for i in range(3):
        lanes = slice(i * width, (i + 1) * width)
        if i == 0:
            product, sums = q_product, q_sums[0:1]
        else:
            at = slice((i - 1) * width, i * width)
            product, sums = nk_ref[:, at], sum_ref[0:1, at]
        weight = w_ref[i].astype(F32)
        full[:, lanes] = (product * gain + shift * sums).astype(BF)
        gain_grad += jnp.sum(product * weight, axis=-1, keepdims=True)
        shift_grad += jnp.sum(weight * sums, axis=-1, keepdims=True)
        if i != 1:
            columns.append(jnp.transpose(jnp.broadcast_to(sums, (HEAD_DIM, width))))
    vec[...] = vec_ref[...]
    for at, column in ((8, gain_grad), (9, shift_grad), (10, columns[0]), (11, columns[1])):
        vec[...] += jnp.where(lane == at, column, 0.0)
    full[:, 3 * width :] = vec[...].astype(BF)
    k = 0
    for msg_ref in msg_refs:
        for i in range(msg_ref.shape[0]):
            msg_ref[i] = full[pl.ds(pl.multiple_of(idx[k] * rows, rows), rows), :]
            k += 1


def query_body(dq_own, dq_other, w_ref, keep_ref, send_ref):
    for dq_ref, out_ref in ((dq_own, keep_ref), (dq_other, send_ref)):
        d_query = jnp.concatenate([dq_ref[h] * SCALE for h in range(HEADS)], axis=0).astype(BF)
        out = lax.dot_general(d_query, w_ref[0], (((0,), (1,)), ((), ())), preferred_element_type=F32)
        out_ref[...] = out.astype(BF)


def finish_body(tok_ref, dmid_ref, row_ref, *refs):
    plain, inverse = normalize(tok_ref[...].astype(F32))
    total = refs[0][...].astype(F32)
    for ref in refs[1:-1]:
        total = total + ref[...].astype(F32)
    refs[-1][...] = (dmid_ref[...] + norm_back(total, plain, inverse, row_ref[0:1, :])).astype(BF)


def matrices_body(*refs):
    terms, (out_ref, up_ref, down_ref) = refs[:-3], refs[-3:]
    width = out_ref.shape[1]
    part = out_ref.shape[0]
    blocks = up_ref.shape[1] // width

    def block(i):
        total = terms[0][i].astype(F32)
        for term in terms[1:]:
            total = total + term[i].astype(F32)
        return total

    out_ref[...] = block(0)
    for j in range(blocks):
        up_ref[:, j * width : (j + 1) * width] = block(1 + j)
        down_ref[j * part : (j + 1) * part, :] = block(1 + blocks + j)


def unpack_body(*refs):
    terms, (qkv_ref, *vec_refs, up_ref, pad_ref) = refs[:-11], refs[-11:]
    total = terms[0][...]
    for term in terms[1:]:
        total = total + term[...].astype(F32)
    width = qkv_ref.shape[1]
    part = qkv_ref.shape[0]
    qkv_ref[...] = total[:, :width]
    pad_ref[...] = jnp.zeros(pad_ref.shape, F32)
    pad_ref[:part] = total[:, width:]
    rows = jnp.transpose(pad_ref[...])
    for ref, row in zip(vec_refs, (8, 9, 10, 11, 0, 1, 2, 3), strict=True):
        ref[...] = rows[row : row + 1, :part]
    up_ref[...] = rows[4 : 4 + up_ref.shape[0], :part]


def shards(
    tokens, w_qkv, w_out, w_up, w_down,
    norm1_gain, norm1_bias, query_bias, value_bias, out_bias, norm2_gain, norm2_bias, up_bias, down_bias,
    cotangent, table_start, support_count, query_count, *, R, F,
):
    A = R // PLANE
    count = R * F
    local, width = tokens.shape[1], tokens.shape[2]
    part = w_qkv.shape[0]
    hidden = w_up.shape[1]
    blocks = hidden // width
    aligned = part % 16 == 0
    rows = part if aligned else width
    pieces = count if aligned else 1
    sds = jax.ShapeDtypeStruct

    r, f = lax.axis_index("rows"), lax.axis_index("fsdp")
    a, x, c = r // PLANE, (r // 2) % 2, r % 2

    def swap_c(v):
        return lax.ppermute(v, "rows", [(i, i ^ 1) for i in range(R)])

    def swap_x(v):
        return lax.ppermute(v, "rows", [(i, i ^ 2) for i in range(R)])

    def turn_a(v, s):
        return lax.ppermute(
            v, "rows", [(i, ((i // PLANE + s) % A) * PLANE + i % PLANE) for i in range(R)]
        )

    def turn_f(v, t):
        return lax.ppermute(v, "fsdp", [(i, (i + t) % F) for i in range(F)])

    def turn_xf(v, t):
        return lax.ppermute(
            v, ("rows", "fsdp"),
            [(i * F + j, (i ^ 2) * F + (j + t) % F) for i in range(R) for j in range(F)],
        )

    def owners(order):
        cr, t, xr, s = (np.array(list(z), np.int32) for z in zip(*order, strict=True))
        plane = lax.rem(a - s + A, A)
        return (((plane * 2 + (x ^ xr)) * 2 + (c ^ cr)) * F + lax.rem(f - t + F, F)).astype(I32)

    unit_s = np.repeat(np.arange(A), 2).astype(np.int32)
    unit_x = np.tile(np.arange(2), A).astype(np.int32)
    unit_start = (lax.rem(a - unit_s + A, A) * 2 + (x ^ unit_x)) * (2 * local) + c * local
    sc = jnp.concatenate([jnp.stack([c, (a * 2 + x) * 2 * local]), unit_start]).astype(I32)
    tab = jnp.concatenate([table_start[0], support_count[0], query_count[0]])
    q_order = [(cr, t, xr, s) for cr in range(2) for t in range(F) for xr in range(2) for s in range(A)]
    parts = [slice(0, A // 2), slice(A // 2, A)]
    m_order = [(cr, 0, xr, s) for xr in range(2) for cr in range(2) for s in range(A)]
    m_order += [(cr, t, 0, s) for cr in range(2) for t in range(1, F) for s in range(A)]
    m_order += [
        (cr, t, 1, s) for cr in range(2) for half in parts for t in range(1, F) for s in list(range(A))[half]
    ]
    every_owner = owners(q_order + m_order)
    q_owner, m_owner = every_owner[:count], every_owner[count:]
    if aligned:
        q_idx, idx = q_owner, jnp.concatenate([m_owner, q_owner])
    else:
        q_idx, idx = jnp.zeros((1,), I32), jnp.zeros((2,), I32)

    near = list(range(1, A))
    early, late = near[:2], near[2:]
    own = tokens[0]
    vectors = [
        v.reshape(1, -1)
        for v in (
            norm1_gain, norm1_bias, query_bias, value_bias, out_bias, norm2_gain, norm2_bias, down_bias, up_bias
        )
    ]
    wide = 3 * width + HEAD_DIM
    pack_in = [w_qkv, w_out, w_up, w_down, *vectors]
    q_own, m_own = pl.pallas_call(
        pack_body,
        grid=(1,),
        out_shape=[sds((4, part, width), BF), sds((1 + 2 * blocks, part, width), BF)],
        in_specs=[pl.BlockSpec(v.shape, lambda i: (0, 0)) for v in pack_in],
        out_specs=[VMEM] * 2,
        scratch_shapes=[pltpu.VMEM((HEAD_DIM, HEAD_DIM), F32)],
        compiler_params=pltpu.CompilerParams(vmem_limit_bytes=56 * MIB),
        cost_estimate=pl.CostEstimate(flops=0, bytes_accessed=16 * part * width, transcendentals=0),
        name="pack",
    )(*pack_in)
    *q_z, own_x, tok_first, sc, tab, q_idx, idx = together(
        *(turn_a(q_own, s) for s in range(1, A)), swap_x(own), turn_a(own, 1), sc, tab, q_idx, idx
    )
    q_z = jnp.stack([q_own] + q_z)
    tok_z, m_z = {1: tok_first}, {0: m_own}
    moved = [swap_x(q_z)] + [v for t in range(1, F) for v in (turn_f(q_z, t), turn_xf(q_z, t))]
    *q_far, tok_z[2], m_z[1] = together(*moved, turn_a(tok_z[1], 1), turn_a(after(m_own, tok_first), 1))
    tok_early = jnp.stack([tok_z[s] for s in early])
    x_early = swap_x(tok_early)
    tok_z[3], m_z[2] = turn_a(tok_z[2], 1), turn_a(m_z[1], 1)
    q_four = jnp.stack([q_z] + q_far)
    q_other = swap_c(q_four)
    q_pieces = [q_four.reshape(count // 2, 4, part, width), q_other.reshape(count // 2, 4, part, width)]
    if not aligned:
        stacked = jnp.concatenate(q_pieces)
        by_owner = jnp.zeros_like(stacked).at[q_owner].set(stacked)
        q_pieces = [by_owner.transpose(1, 0, 2, 3).reshape(1, 4, width, width)]
    key_shape = (2 * HEADS, local, HEAD_DIM)
    w_all, row_vec, col_vec, up_row, kv_own, n_own, q, kv_z, n_z, n_first = call(
        functools.partial(ready_body, rows=rows, count=len(q_pieces), part=part),
        [
            sds((3, width, width), BF), sds((16, width), F32), sds((width, HEAD_DIM), F32), sds((blocks, width), F32),
            sds((2,) + key_shape, BF), sds((2, local, width), BF), sds((HEADS, local, HEAD_DIM), BF),
            sds((2,) + key_shape, BF), sds((2, local, width), BF), sds((1, local, width), BF),
        ],
        [q_idx, *q_pieces, own, own_x, tok_early], [SMEM] + [HBM] * len(q_pieces) + [VMEM] * 3, [VMEM] * 10,
        scratch=[pltpu.VMEM((width, HEAD_DIM), BF), pltpu.SemaphoreType.DMA((2,))],
        flops=4 * (A + 1) * local * width * width, moved=4 * width * wide, vmem=12, name="ready",
    )

    q_other, n_other = swap_c(q), swap_c(n_first)
    tok_z[3], m_z[2], x_early, kv_z = together(tok_z[3], m_z[2], x_early, kv_z)
    for s in range(4, A):
        tok_z[s], m_z[s - 1] = together(turn_a(tok_z[s - 1], 1), turn_a(m_z[s - 2], 1))
    tok_late = tok_z[3][None] if A == 4 else jnp.stack([tok_z[s] for s in late])
    x_late, m_z[A - 1] = together(swap_x(tok_late), turn_a(m_z[A - 2], 1))
    m_z = stack([m_z[s] for s in range(A)])
    m_x, m_f = swap_x(m_z), [turn_f(m_z, t) for t in range(1, F)]
    m_c = swap_c(m_z)
    spots = [(0, i) for i in range(A - 3)] + [(1, i) for i in range(2)] + [(2, i) for i in range(A - 3)]
    kv_x, n_x = call(
        functools.partial(project_body, with_q=False, spots=spots, count=3),
        [sds((len(spots),) + key_shape, BF), sds((len(spots), local, width), BF)],
        [tok_late, x_early, after(x_late, m_z), w_all, row_vec], [VMEM] * 5, [VMEM] * 2,
        flops=4 * len(spots) * local * width * width, moved=8 * len(spots) * local * width, vmem=8, name="project",
    )
    where = {0: ((kv_own, kv_own, 0, 1), (n_own, n_own, 0, 1))}
    for i, s in enumerate(early):
        where[s] = ((kv_z, kv_x, i, A - 3 + i), (n_z, n_x, i, A - 3 + i))
    for i, s in enumerate(late):
        where[s] = ((kv_x, kv_x, i, A - 1 + i), (n_x, n_x, i, A - 1 + i))
    kv_pieces = [kv_own, kv_z, kv_x]
    kv_units = [0, 1] + [2 * s for s in near] + [2 * s + 1 for s in near]

    unit = 2 * local
    work = 4 * unit * A * unit * width
    packet = width + HEAD_DIM
    att_keep, att_send, q_chip = call(
        functools.partial(attend_body, kv_units=kv_units),
        [sds((local, packet), F32)] * 2 + [sds((HEADS, unit, HEAD_DIM), BF)],
        [sc, tab, q, q_other, *kv_pieces], [SMEM, SMEM, VMEM, VMEM] + [ANY] * 3, [VMEM] * 3,
        scratch=[
            pltpu.VMEM((2 * A, HEADS, unit, local), F32),
            pltpu.VMEM((HEADS, unit, HEAD_DIM), F32), pltpu.VMEM((HEADS, unit, 2 * HEAD_DIM), F32),
            pltpu.VMEM((2 * A, 2 * HEADS, local, HEAD_DIM), BF), pltpu.SemaphoreType.DMA((2 * A,)),
        ],
        flops=work, moved=8 * A * unit * width, trans=HEADS * unit * A * unit, vmem=4 + 6 * A, name="attend",
    )
    att_keep, att_send, m_x, m_c, *m_f = together(att_keep, att_send, m_x, m_c, *m_f)
    half_shape = (A // 2,) + m_z.shape[1:]
    halves = copy_out(
        [m_x, *m_f], [half_shape] * F, [(0, (parts[0],), 0, ())] + [(t, (parts[1],), t, ()) for t in range(1, F)]
    )
    crossed = [turn_f(halves[0], t) for t in range(1, F)] + [swap_x(v) for v in halves[1:]]
    att_other, *crossed = together(swap_c(att_send), *crossed)
    m_arrays = [m_z, m_c, m_x, swap_c(m_x), *m_f, *(swap_c(v) for v in m_f), *crossed, *(swap_c(v) for v in crossed)]
    if not aligned:
        stacked = jnp.concatenate(m_arrays)
        by_owner = jnp.zeros_like(stacked).at[m_owner].set(stacked)
        m_arrays = [
            jnp.concatenate(
                [
                    by_owner[:, 0].reshape(1, width, width),
                    by_owner[:, 1 : 1 + blocks].transpose(1, 0, 2, 3).reshape(blocks, width, width),
                    by_owner[:, 1 + blocks :].reshape(blocks, width, width),
                ]
            )[None]
        ]

    spots = [(t, xr) for t in range(F) for xr in range(2)]
    grad_count = 4 * F if aligned else 1
    g_shape = sds((pieces // grad_count, 1 + 2 * blocks, rows, width), BF)
    got = call(
        functools.partial(middle_body, rows=rows, m_count=len(m_arrays), grad_count=grad_count),
        [
            sds((local, width), BF), sds((local, width), F32), sds((local, packet), BF), sds((HEADS, unit), F32),
            sds((width, HEAD_DIM), F32),
        ] + [g_shape] * grad_count,
        [idx, sc, tab, *m_arrays, own, att_keep, att_other, cotangent[0], row_vec, up_row],
        [SMEM] * 3 + [HBM] * len(m_arrays) + [VMEM] * 6,
        [VMEM] * 5 + [HBM] * grad_count,
        scratch=[
            pltpu.VMEM((width, width), BF), pltpu.VMEM((blocks, width, width), BF),
            pltpu.VMEM((pieces * blocks, rows, width), BF),
            pltpu.VMEM((width, width), BF), pltpu.VMEM((blocks, width, width), BF),
            pltpu.VMEM((pieces * blocks, rows, width), BF), pltpu.VMEM((blocks, local, width), F32),
            pltpu.SemaphoreType.DMA((3,)), pltpu.SemaphoreType.DMA,
        ],
        flops=6 * local * width * width * (1 + 2 * blocks), moved=4 * width * width * (1 + 2 * blocks),
        trans=local * hidden, vmem=50, name="middle",
    )
    outputs, d_middle, d_own, lse, vec = got[:5]
    grads = got[5:]
    d_other = swap_c(d_own)

    lead = (A, 1 + 2 * blocks, part, width)
    if aligned:
        relative = [g.reshape(lead) for g in grads]
    else:
        whole = grads[0][0]
        by_owner = jnp.concatenate(
            [
                whole[0].reshape(count, 1, part, width),
                whole[1 : 1 + blocks].reshape(blocks, count, part, width).transpose(1, 0, 2, 3),
                whole[1 + blocks :].reshape(count, blocks, part, width),
            ],
            axis=1,
        )
        by_owner = by_owner[q_owner].reshape((4 * F,) + lead)
        relative = [by_owner[i] for i in range(4 * F)]
    g_near = {spot: relative[i] for i, spot in enumerate(spots)}
    g_far = {spot: swap_c(after(relative[2 * F + i], d_other)) for i, spot in reversed(list(enumerate(spots)))}

    def through_f(xr, half):
        return [
            turn_f(add_up([g_near[t, xr], g_far[t, xr]], [[(0, (half,)), (1, (half,))]])[0], F - t)
            for t in range(1, F)
        ]

    def g_kept(xr, half):
        arrays = [g_near[0, xr], g_far[0, xr], *g_y[xr, half]]
        return arrays, [(0, (half,)), (1, (half,))] + [(2 + i, ()) for i in range(F - 1)]

    carried, d_all = [], []
    d_x, d_z, d_keep, d_send = {}, {}, {}, {}
    g_y, g_x = {}, {}
    back_order = near + [0]
    q_now = q_chip
    steps = len(back_order)
    y_parts = [(xr, half) for xr in (1, 0) for half in parts]
    for step, s in enumerate(back_order):
        kv_at, n_at = where[s]
        if step:
            ins = [sc, tab, q_now, *d_all, lse, *kv_at[:2], *n_at[:2], w_all, *carried]
            body = back_body
        else:
            ins = [sc, tab, q_now, d_own, d_other, lse, *kv_at[:2], *n_at[:2], w_all]
            body = first_back_body
        dq_shape = sds((HEADS, HEAD_DIM, local), F32)
        shapes = [
            sds((local, width), BF), sds((local, width), BF), dq_shape, dq_shape,
            sds((width, 2 * width), F32), sds((8, 2 * width), F32),
        ]
        if not step:
            shapes += [sds((HEADS, unit, HEAD_DIM), BF), sds((HEADS, unit), F32)]
        outs = call(
            functools.partial(body, plane=s, spots=kv_at[2:]), shapes, ins,
            [SMEM, SMEM] + [VMEM] * (len(ins) - 2), [VMEM] * len(shapes),
            scratch=[pltpu.VMEM((2, local, 2 * width), BF)],
            flops=work // A * 5 // 2 + 8 * unit * width * width, moved=16 * unit * width,
            trans=HEADS * unit * unit, name="back",
        )
        if step == 0:
            keys = list(g_far)
            got = together(*outs, *(g_far[k] for k in keys))
            outs, d_all = got[:6], got[6:8]
            g_far = dict(zip(keys, got[8:], strict=True))
        else:
            prev = back_order[step - 1]
            beside = {("x", prev): swap_x(d_send[prev])}
            if step >= 2:
                beside["z", step] = turn_a(d_sum, 1)
            if step - 1 < len(y_parts):
                for i, v in enumerate(through_f(y_parts[step - 1][0], y_parts[step - 1][1])):
                    beside["y", step - 1, i] = v
            keys = list(beside)
            got = together(*outs, *beside.values())
            outs = got[:6]
            beside = dict(zip(keys, got[6:], strict=True))
            for key, v in beside.items():
                if key[0] == "x":
                    d_x[key[1]] = v
                elif key[0] == "z":
                    d_z[key[1]] = v
                else:
                    g_y[y_parts[key[1]]] = g_y.get(y_parts[key[1]], []) + [v]
            arrived = [d_keep[prev], d_x[prev]] + ([d_z[step]] if step in d_z else [])
            (d_sum,) = add_up(arrived, [[(i, ()) for i in range(len(arrived))]])
        d_keep[s], d_send[s], *carried = outs
        q_now = after(q_chip, outs[2])
        if step:
            q_now = after(q_now, d_sum)

    for k in range(steps - 1, len(y_parts)):
        g_y[y_parts[k]] = through_f(*y_parts[k])
    d_last = turn_a(d_sum, 1)
    dq_own, dq_other, n_product, sums = carried

    half_count = 2 * F
    msg_lead = (A, part, wide)
    msg_shape = [sds((pieces // 2, rows, wide), BF)] * 2 if aligned else [sds((1, rows, wide), BF)]
    message = call(
        functools.partial(message_body, rows=rows),
        msg_shape,
        [q_idx, n_own, n_other, dq_own, dq_other, n_product, sums, w_all, col_vec, vec],
        [SMEM] + [VMEM] * 9, [VMEM] * len(msg_shape),
        scratch=[pltpu.VMEM((width, wide), BF), pltpu.VMEM((width, HEAD_DIM), F32)],
        flops=2 * local * width * width, moved=8 * width * wide, vmem=8, name="message",
    )
    if not aligned:
        flat = message[0][0]
        at = slice(3 * width + 4, 3 * width + 4 + blocks)
        up_part = flat[:, at].T.reshape(count, blocks, part)
        by_owner = flat.reshape(count, part, wide)
        by_owner = by_owner.at[:, :, at].set(up_part.transpose(0, 2, 1))
        by_owner = by_owner[q_owner]
        message = [by_owner[: count // 2], by_owner[count // 2 :]]
    w_far = swap_c(message[1])
    arrays = [g_near[0, 1], g_far[0, 1], *g_y[1, parts[0]], *g_y[1, parts[1]]]
    lows = [(0, (parts[0],)), (1, (parts[0],))] + [(2 + i, ()) for i in range(F - 1)]
    highs = [(0, (parts[1],)), (1, (parts[1],))] + [(1 + F + i, ()) for i in range(F - 1)]
    (g_x_send,) = join_up(arrays, [lows, highs])
    g_x_all = swap_x(g_x_send)
    w_far = w_far.reshape((half_count,) + msg_lead)
    w_near = message[0].reshape((half_count,) + msg_lead)
    w_both = add_up([w_near, w_far], [[(0, (i,)), (1, (i,))] for i in range(half_count)])
    got = []
    for (t, xr), sent in zip(spots, w_both, strict=True):
        if xr:
            sent = turn_xf(sent, F - t) if t else swap_x(sent)
        elif t:
            sent = turn_f(sent, F - t)
        got.append(sent)
    got[0], d_last = together(got[0], d_last)
    d_x[0] = swap_x(after(d_send[0], got[0]))
    w_z = add_up(got, [[(i, (s,)) for i in range(len(got))] for s in near])
    (w_own,) = add_up(got, [[(i, (0,)) for i in range(len(got))]], F32)
    w_z = [turn_a(v, A - s) for s, v in zip(near, w_z, strict=True)]
    grad_qkv, *vector_grads, up_grad = call(
        unpack_body, [sds((part, 3 * width), F32)] + [sds((1, part), F32)] * 8 + [sds((blocks, part), F32)],
        [w_own, *w_z], [VMEM] * A, [VMEM] * 10, scratch=[pltpu.VMEM((HEAD_DIM, HEAD_DIM), F32)], moved=16 * part * width, vmem=8, name="unpack",
    )

    g_z_send, g_mine = {}, None
    for half in parts:
        arrays, terms = g_kept(0, half)
        arrays.append(g_x_all)
        planes = list(range(A))[half]

        def one(s, terms=terms, start=half.start, last=len(arrays) - 1):
            out = [(i, (start + s,) if spot else (s,)) for i, spot in terms]
            return out + [(last, (start + s,))]

        for s, v in zip(planes, add_up(arrays, [one(s - half.start) for s in planes]), strict=True):
            if s:
                g_z_send[s] = v
            else:
                g_mine = v
    g_z_send = [g_z_send[s] for s in near]
    g_z = [turn_a(v, A - s) for s, v in zip(near, g_z_send, strict=True)]
    grad_out, grad_up, grad_down = call(
        matrices_body,
        [sds((part, width), F32), sds((part, hidden), F32), sds((blocks * part, width), F32)],
        [g_mine, *g_z], [VMEM] * A, [VMEM] * 3, moved=6 * A * g_mine.size, vmem=8, name="matrices",
    )
    query_keep, query_send = call(
        query_body, [sds((local, width), BF)] * 2, [after(dq_own, got[0]), dq_other, w_all], [VMEM] * 3, [VMEM] * 2,
        flops=4 * local * width * width, moved=4 * local * width, vmem=8, name="query",
    )
    grad_tokens = call(
        finish_body, sds((local, width), BF),
        [own, d_middle, row_vec, query_keep, swap_c(query_send), d_keep[0], d_x[0], d_last],
        [VMEM] * 8, VMEM, flops=20 * local * width, moved=16 * local * width, vmem=8, name="finish",
    )
    return (
        outputs[None],
        grad_tokens[None],
        grad_qkv,
        grad_out,
        grad_up,
        grad_down,
        *(v.reshape(part) for v in vector_grads[:7]),
        up_grad.reshape(blocks * part),
        vector_grads[7].reshape(part),
    )


def solution(mesh):
    both = ("rows", "fsdp")
    matrix, vector, act, table = P(both, None), P(both), P("fsdp", "rows", None), P("fsdp", None)
    return jax.shard_map(
        functools.partial(shards, R=mesh.shape["rows"], F=mesh.shape["fsdp"]),
        mesh=mesh,
        in_specs=(act,) + (matrix,) * 4 + (vector,) * 9 + (act,) + (table,) * 3,
        out_specs=(act, act) + (matrix,) * 4 + (vector,) * 9,
        check_vma=False,
    )
```

```python
import functools
import math

import jax
import jax.numpy as jnp
import numpy as np
from jax import lax
from jax.experimental import pallas as pl
from jax.experimental.pallas import tpu as pltpu
from jax.sharding import PartitionSpec as P

HEADS = 4
HEAD_DIM = 128
EPS = 1e-05
NEG = -1e30
PLANE = 4
MIB = 1024 * 1024
BF = jnp.bfloat16
F32 = jnp.float32
I32 = jnp.int32
SCALE = 1.0 / math.sqrt(HEAD_DIM)
SCALE2 = SCALE * math.log2(math.e)
GELU_A = math.sqrt(2.0 / math.pi)
GELU_B = 0.044715

VMEM = pl.BlockSpec(memory_space=pltpu.VMEM)
SMEM = pl.BlockSpec(memory_space=pltpu.SMEM)
HBM = pl.BlockSpec(memory_space=pltpu.HBM)
ANY = pl.BlockSpec(memory_space=pl.ANY)


def after(value, *others):
    return lax.optimization_barrier((value, *others))[0]


def together(*values):
    return lax.optimization_barrier(values)


def mm(left, right):
    return jnp.dot(left, right, preferred_element_type=F32)


def mm_nt(left, right):
    return lax.dot_general(left, right, (((1,), (1,)), ((), ())), preferred_element_type=F32)


def mm_tn(left, right):
    return lax.dot_general(left, right, (((0,), (0,)), ((), ())), preferred_element_type=F32)


def call(body, outs, ins, in_specs, out_specs, scratch=(), flops=0, moved=0, trans=0, vmem=16, name=None):
    return pl.pallas_call(
        body,
        out_shape=outs,
        in_specs=in_specs,
        out_specs=out_specs,
        scratch_shapes=scratch,
        compiler_params=pltpu.CompilerParams(vmem_limit_bytes=vmem * MIB),
        cost_estimate=pl.CostEstimate(
            flops=int(flops), bytes_accessed=int(moved), transcendentals=int(trans)
        ),
        name=name,
    )(*ins)


def normalize(values):
    centre = values - jnp.mean(values, axis=-1, keepdims=True)
    spread = jnp.mean(centre * centre, axis=-1, keepdims=True)
    inverse = lax.rsqrt(spread + EPS)
    return centre * inverse, inverse


def norm_back(grad_out, plain, inverse, gain):
    scaled = grad_out * gain
    return inverse * (
        scaled
        - jnp.mean(scaled, axis=-1, keepdims=True)
        - plain * jnp.mean(scaled * plain, axis=-1, keepdims=True)
    )


def table_of(tab, count, pos):
    low = jnp.zeros_like(pos) + tab[0]
    high = low + tab[count]
    finish = high + tab[2 * count]
    for t in range(1, count):
        here = pos >= tab[t]
        top = tab[t] + tab[count + t]
        low = jnp.where(here, tab[t], low)
        high = jnp.where(here, top, high)
        finish = jnp.where(here, top + tab[2 * count + t], finish)
    return low, high, finish


def pack_body(qkv_ref, out_ref, up_ref, down_ref, *refs):
    vec_refs, (q_ref, m_ref, vec_scr) = refs[:-3], refs[-3:]
    part, width = out_ref.shape
    blocks = up_ref.shape[1] // width
    vec_scr[...] = jnp.zeros(vec_scr.shape, F32)
    for k, ref in enumerate(vec_refs[:-1]):
        vec_scr[k : k + 1, :part] = ref[...].astype(F32)
    for j in range(blocks):
        vec_scr[8 + j : 9 + j, :part] = vec_refs[-1][:, j * part : (j + 1) * part].astype(F32)
    for i in range(3):
        q_ref[i] = qkv_ref[:, i * width : (i + 1) * width]
    q_ref[3] = jnp.zeros((part, width), BF)
    q_ref[3, :, :HEAD_DIM] = jnp.transpose(vec_scr[...])[:part].astype(BF)
    m_ref[0] = out_ref[...]
    for j in range(blocks):
        m_ref[1 + j] = up_ref[:, j * width : (j + 1) * width]
        m_ref[1 + blocks + j] = down_ref[j * part : (j + 1) * part, :]


def sum_body(*refs, plan, count):
    for out_ref, terms in zip(refs[count:], plan, strict=True):
        total = None
        for which, spot in terms:
            term = refs[which][spot].astype(F32)
            total = term if total is None else total + term
        out_ref[...] = total.astype(out_ref.dtype)


def join_body(*refs, plan, count):
    out_ref, row = refs[count], 0
    for terms in plan:
        total = None
        for which, spot in terms:
            term = refs[which][spot].astype(F32)
            total = term if total is None else total + term
        out_ref[row : row + total.shape[0]] = total.astype(out_ref.dtype)
        row += total.shape[0]


def join_up(arrays, plan):
    shapes = [jax.eval_shape(lambda v: v[terms[0][1]], arrays[terms[0][0]]).shape for terms in plan]
    shape = (sum(v[0] for v in shapes),) + shapes[0][1:]
    moved = math.prod(shape) * 4
    return call(
        functools.partial(join_body, plan=plan, count=len(arrays)), [jax.ShapeDtypeStruct(shape, BF)], arrays,
        [VMEM] * len(arrays), [VMEM], flops=moved, moved=moved, vmem=16, name="join",
    )


def lay_body(*refs, plan, count):
    out_ref, row = refs[count], 0
    width = out_ref.shape[2]
    for wide, terms in plan:
        total = None
        for which, spot in terms:
            term = refs[which][spot].astype(F32)
            total = term if total is None else total + term
        total = total.astype(out_ref.dtype)
        if wide:
            for j in range(-(-total.shape[1] // width)):
                piece = total[:, j * width : (j + 1) * width]
                if piece.shape[1] < width:
                    out_ref[row] = jnp.zeros(out_ref.shape[1:], out_ref.dtype)
                out_ref[row, :, : piece.shape[1]] = piece
                row += 1
        else:
            out_ref[row : row + total.shape[0]] = total
            row += total.shape[0]


def lay_out(arrays, plan, part, width):
    blocks = 0
    for wide, terms in plan:
        shape = jax.eval_shape(lambda v: v[terms[0][1]], arrays[terms[0][0]]).shape
        blocks += -(-shape[1] // width) if wide else shape[0]
    moved = blocks * part * width * 4
    return call(
        functools.partial(lay_body, plan=plan, count=len(arrays)), [jax.ShapeDtypeStruct((blocks, part, width), BF)],
        arrays, [VMEM] * len(arrays), [VMEM], flops=moved, moved=moved, vmem=8, name="lay",
    )[0]


def add_up(arrays, plan, dtype=BF):
    outs = []
    for terms in plan:
        which, spot = terms[0]
        outs.append(jax.ShapeDtypeStruct(jax.eval_shape(lambda v: v[spot], arrays[which]).shape, dtype))
    moved = sum(o.size for o in outs) * 4
    return call(
        functools.partial(sum_body, plan=plan, count=len(arrays)), outs, arrays,
        [VMEM] * len(arrays), [VMEM] * len(outs), flops=moved, moved=moved, vmem=16, name="add",
    )


def copy_body(*refs, plan, count):
    outs, sem = refs[count:-1], refs[-1]
    copies = []
    for k, (which, source, out, spot) in enumerate(plan):
        copies.append(pltpu.make_async_copy(refs[which].at[source], outs[out].at[spot], sem.at[k]))
        copies[-1].start()
    for copy in copies:
        copy.wait()


def copy_out(arrays, shapes, plan):
    moved = sum(math.prod(shape) for shape in shapes) * 4
    return call(
        functools.partial(copy_body, plan=plan, count=len(arrays)),
        [jax.ShapeDtypeStruct(shape, arrays[0].dtype) for shape in shapes], arrays,
        [HBM] * len(arrays), [VMEM] * len(shapes),
        scratch=[pltpu.SemaphoreType.DMA((len(plan),))], moved=moved, vmem=4, name="copy",
    )


def stack(arrays):
    shape = (len(arrays),) + arrays[0].shape
    every = (slice(None),)
    (out,) = copy_out(arrays, [shape], [(i, every, 0, (i,)) for i in range(len(arrays))])
    return out


def assemble_body(idx, *refs, rows, count):
    pieces, (w_ref, row_ref, col_ref, low_scr, sem) = refs[:count], refs[count:]
    k = 0
    for piece in pieces:
        for j in range(piece.shape[0]):
            at = pl.ds(pl.multiple_of(idx[k] * rows, rows), rows)
            pltpu.make_async_copy(piece.at[j, pl.ds(0, 3)], w_ref.at[:, at, :], sem.at[0]).start()
            pltpu.make_async_copy(piece.at[j, 3, :, pl.ds(0, HEAD_DIM)], low_scr.at[at, :], sem.at[1]).start()
            k += 1
    pltpu.make_async_copy(low_scr, low_scr, sem.at[1]).wait()
    columns = low_scr[...].astype(F32)
    col_ref[...] = columns
    row_ref[...] = jnp.transpose(columns)[: row_ref.shape[0]]
    pltpu.make_async_copy(w_ref, w_ref, sem.at[0]).wait()


def project_body(*refs, with_q, spots, count):
    pieces, (w_ref, row_ref), outs = refs[:count], refs[count : count + 2], refs[count + 2 :]
    kv_ref, n_ref = outs[:2]
    gain, shift = row_ref[0:1, :], row_ref[1:2, :]
    for i, (which, lead) in enumerate(spots):
        plain, unused_inverse = normalize(pieces[which][lead].astype(F32))
        n_ref[i] = plain.astype(BF)
        normed = (plain * gain + shift).astype(BF)
        keys = mm(normed, w_ref[1])
        values = mm(normed, w_ref[2]) + row_ref[3:4, :]
        for h in range(HEADS):
            lanes = slice(h * HEAD_DIM, (h + 1) * HEAD_DIM)
            kv_ref[i, h] = keys[:, lanes].astype(BF)
            kv_ref[i, HEADS + h] = values[:, lanes].astype(BF)
        if with_q and i == 0:
            queries = (mm(normed, w_ref[0]) + row_ref[2:3, :]) * SCALE2
            for h in range(HEADS):
                outs[2][h] = queries[:, h * HEAD_DIM : (h + 1) * HEAD_DIM].astype(BF)


def ready_body(idx, *refs, rows, count, part):
    pieces, (own_ref, tok_ref) = refs[:count], refs[count : count + 2]
    w_ref, row_ref, col_ref, up_ref, kv_ref, n_ref, q_ref, n_first, low_scr, sem = refs[count + 2 :]
    assemble_body(idx, *pieces, w_ref, row_ref, col_ref, low_scr, sem, rows=rows, count=count)
    width = up_ref.shape[1]
    blocks = up_ref.shape[0]
    per = width // blocks
    source = lax.broadcasted_iota(I32, (per, width), 0)
    target = lax.broadcasted_iota(I32, (per, width), 1)
    total = jnp.zeros((blocks, width), F32)
    for k in range(blocks):
        spread = jnp.where(
            target == (source // part) * (blocks * part) + k * part + lax.rem(source, part), 1.0, 0.0
        ).astype(BF)
        mine = [row_ref[8 + k : 9 + k, j * per : (j + 1) * per] for j in range(blocks)]
        total += mm(jnp.concatenate(mine, axis=0).astype(BF), spread)
    up_ref[...] = total
    spots = [(0, slice(None))] + [(1, i) for i in range(tok_ref.shape[0])]
    project_body(own_ref, tok_ref, w_ref, row_ref, kv_ref, n_ref, q_ref, with_q=True, spots=spots, count=2)
    n_first[0] = n_ref[0]


def reach(sc, tab, rows):
    count = tab.shape[0] // 3
    min_low, min_high, unused = table_of(tab, count, sc[0])
    max_low, max_high, unused = table_of(tab, count, sc[0] + PLANE * rows - 1)
    return min_low, max_high, max_low, min_high


def plane_rows(sc, rows, shape, dim):
    spot = lax.broadcasted_iota(I32, shape, dim)
    place = spot + sc[1]
    for b in range(1, PLANE):
        place = jnp.where(spot >= b * rows, spot + (sc[1 + b] - b * rows), place)
    return place


def attend_body(sc, tab, *refs, kv_units):
    q_refs, kv_refs = refs[:PLANE], refs[PLANE:-8]
    keep_ref, send_ref, q_scr, s_scr, m_scr, acc_scr, kv_ref, sem = refs[-8:]
    count = tab.shape[0] // 3
    units, unused, rows, unused = kv_ref.shape
    k = 0
    for ref in kv_refs:
        for i in range(ref.shape[0]):
            pltpu.make_async_copy(ref.at[i], kv_ref.at[kv_units[k]], sem.at[kv_units[k]]).start()
            k += 1
    min_low, max_high, max_low, min_high = reach(sc, tab, rows)
    q_pos = plane_rows(sc, rows, (PLANE * rows, 1), 0)
    low, high, unused = table_of(tab, count, q_pos)
    ones = jnp.ones((rows, HEAD_DIM), BF)
    for b, ref in enumerate(q_refs):
        q_scr[:, b * rows : (b + 1) * rows] = ref[...]
    m_scr[...] = jnp.full(m_scr.shape, NEG, F32)
    acc_scr[...] = jnp.zeros(acc_scr.shape, F32)

    def keep_scores(u, allowed):
        for h in range(HEADS):
            scores = mm_nt(q_scr[h], kv_ref[u, h])
            if allowed is not None:
                scores = jnp.where(allowed, scores, NEG)
            s_scr[u, h] = scores
            top = m_scr[h]
            for j in range(rows // HEAD_DIM):
                top = jnp.maximum(top, scores[:, j * HEAD_DIM : (j + 1) * HEAD_DIM])
            m_scr[h] = top

    def score_step(u, carry):
        start = sc[1 + PLANE + u]
        pltpu.make_async_copy(kv_refs[0].at[0], kv_ref.at[u], sem.at[u]).wait()
        needed = (start < max_high) & (start + rows > min_low)
        whole = (start >= max_low) & (start + rows <= min_high)

        @pl.when(needed & whole)
        def _():
            keep_scores(u, None)

        @pl.when(needed & jnp.logical_not(whole))
        def _():
            k_pos = start + lax.broadcasted_iota(I32, (1, rows), 1)
            keep_scores(u, (k_pos >= low) & (k_pos < high))

        return carry

    lax.fori_loop(0, units, score_step, 0)
    for h in range(HEADS):
        top = jnp.max(m_scr[h], axis=-1, keepdims=True)
        m_scr[h] = jnp.broadcast_to(jnp.where(top > 0.5 * NEG, top, 0.0), m_scr.shape[1:])

    def value_step(u, carry):
        start = sc[1 + PLANE + u]
        needed = (start < max_high) & (start + rows > min_low)

        @pl.when(needed)
        def _():
            for h in range(HEADS):
                soft = jnp.exp2(s_scr[u, h] - m_scr[h][:, :1]).astype(BF)
                wide = jnp.concatenate([kv_ref[u, HEADS + h], ones], axis=1)
                acc_scr[h] += mm(soft, wide)

        return carry

    lax.fori_loop(0, units, value_step, 0)
    lane = lax.broadcasted_iota(I32, (1, HEAD_DIM), 1)
    width = HEADS * HEAD_DIM
    for b in range(PLANE):
        ref, spot = (keep_ref, send_ref)[b % 2], b // 2
        at = slice(b * rows, (b + 1) * rows)
        logs = jnp.zeros((rows, HEAD_DIM), F32)
        for h in range(HEADS):
            total = acc_scr[h, at, HEAD_DIM:]
            some = total > 0.0
            safe = jnp.where(some, total, 1.0)
            ref[spot, :, h * HEAD_DIM : (h + 1) * HEAD_DIM] = acc_scr[h, at, :HEAD_DIM] / safe
            logs = jnp.where(lane == h, jnp.where(some, m_scr[h, at] + jnp.log2(safe), NEG), logs)
        ref[spot, :, width:] = logs


def in_parts(value, lane, first):
    out = jnp.zeros((value[0].shape[0], HEAD_DIM), F32)
    for h, column in enumerate(value):
        high = column.astype(BF).astype(F32)
        rest = column - high
        middle = rest.astype(BF).astype(F32)
        for i, part in enumerate((high, middle, rest - middle)):
            out = jnp.where(lane == first + i * HEADS + h, part, out)
    return out


def merge_body(mine_ref, other_ref, own_ref, far_ref):
    width = HEADS * HEAD_DIM
    lane = lax.broadcasted_iota(I32, (1, HEAD_DIM), 1)
    for b in range(2):
        lse_mine, lse_other = mine_ref[b, :, width:], other_ref[b, :, width:]
        top = jnp.maximum(lse_mine, lse_other)
        share_mine, share_other = jnp.exp2(lse_mine - top), jnp.exp2(lse_other - top)
        share = share_mine + share_other
        log_total = top + jnp.log2(share)
        share_mine, share_other = share_mine / share, share_other / share
        for h in range(HEADS):
            lanes = slice(h * HEAD_DIM, (h + 1) * HEAD_DIM)
            mixed = mine_ref[b, :, lanes] * share_mine[:, h : h + 1] + other_ref[b, :, lanes] * share_other[:, h : h + 1]
            if b == 0:
                own_ref[:, lanes] = mixed
            else:
                far_ref[:, lanes] = mixed.astype(BF)
        if b == 0:
            own_ref[:, width:] = log_total
        else:
            columns = [log_total[:, h : h + 1] for h in range(HEADS)]
            far_ref[:, width:] = in_parts(columns, lane, 0).astype(BF)


def middle_body(idx, sc, tab, *refs, rows, m_count, grad_count):
    m_refs, (tok_ref, own_ref, other_ref, cot_ref, row_ref, up_row_ref) = refs[:m_count], refs[m_count : m_count + 6]
    outs = refs[m_count + 6 :]
    out_ref, dmid_ref, d_ref, vec_ref = outs[:4]
    g_refs = outs[4 : 4 + grad_count]
    (w_out, w_up, w_down, g_out, g_up, g_down, dh_scr, sem, g_sem) = outs[4 + grad_count :]
    blocks, width = w_up.shape[0], w_up.shape[2]
    pieces = w_down.shape[0] // blocks
    count = tab.shape[0] // 3
    local = tok_ref.shape[0]
    spots = []
    for m_ref in m_refs:
        for spot in range(m_ref.shape[0]):
            owner = idx[len(spots)]
            spots.append(
                (m_ref, spot, pl.ds(pl.multiple_of(owner * rows, rows), rows), pl.ds(owner * blocks, blocks))
            )
    for m_ref, spot, at, unused in spots:
        pltpu.make_async_copy(m_ref.at[spot, 0], w_out.at[at, :], sem.at[0]).start()
    for m_ref, spot, unused, at in spots:
        pltpu.make_async_copy(m_ref.at[spot, pl.ds(1 + blocks, blocks)], w_down.at[at], sem.at[2]).start()
    for m_ref, spot, at, unused in spots:
        pltpu.make_async_copy(m_ref.at[spot, pl.ds(1, blocks)], w_up.at[:, at, :], sem.at[1]).start()

    pos = sc[1] + lax.broadcasted_iota(I32, (local, 1), 0)
    unused_low, unused_high, finish = table_of(tab, count, pos)
    live = (pos < finish).astype(F32)
    gain, shift = row_ref[5:6, :], row_ref[6:7, :]
    lane = lax.broadcasted_iota(I32, (1, HEAD_DIM), 1)
    logs, mixed = [], []
    for h in range(HEADS):
        lanes = slice(h * HEAD_DIM, (h + 1) * HEAD_DIM)
        lse_own = own_ref[:, width + h : width + h + 1]
        lse_other = sum(
            other_ref[:, width + i * HEADS + h : width + i * HEADS + h + 1].astype(F32) for i in range(3)
        )
        top = jnp.maximum(lse_own, lse_other)
        share_own, share_other = jnp.exp2(lse_own - top), jnp.exp2(lse_other - top)
        share = share_own + share_other
        logs.append(top + jnp.log2(share))
        mixed.append(
            own_ref[:, lanes] * (share_own / share) + other_ref[:, lanes].astype(F32) * (share_other / share)
        )
    mixed = jnp.concatenate(mixed, axis=1)
    attended = (mixed * live).astype(BF)
    cot = cot_ref[...]
    pltpu.make_async_copy(w_out, w_out, sem.at[0]).wait()
    middle = tok_ref[...].astype(F32) + mm(attended, w_out[...]) + row_ref[4:5, :]
    pltpu.make_async_copy(w_down, w_down, sem.at[2]).wait()
    for j in range(blocks):
        dh_scr[j] = mm_nt(cot, w_down[j * pieces : (j + 1) * pieces].reshape(width, width))
    plain, inverse = normalize(middle)
    normed = (plain * gain + shift).astype(BF)
    pltpu.make_async_copy(w_up, w_up, sem.at[1]).wait()
    total = middle + row_ref[7:8, :]
    d_norm = jnp.zeros(middle.shape, F32)
    ones = jnp.ones((8, local), BF)
    up_sums = []
    for j in range(blocks):
        up = w_up[j]
        down = w_down[j * pieces : (j + 1) * pieces].reshape(width, width)
        pre = mm(normed, up) + up_row_ref[j : j + 1, :]
        square = pre * pre
        t = jnp.tanh(GELU_A * pre * (1.0 + GELU_B * square))
        half = 0.5 * (1.0 + t)
        hidden = (pre * half).astype(BF)
        slope = half + 0.5 * pre * (1.0 - t * t) * (GELU_A * (1.0 + 3.0 * GELU_B * square))
        total = total + mm(hidden, down)
        d_pre = (dh_scr[j] * slope).astype(BF)
        d_norm = d_norm + mm_nt(d_pre, up)
        g_down[j * pieces : (j + 1) * pieces] = mm_tn(hidden, cot).astype(BF).reshape(pieces, rows, width)
        g_up[j] = mm_tn(normed, d_pre).astype(BF)
        up_sums.append(mm(ones, d_pre)[0:1])
    g_pieces = g_refs[0].shape[0]
    spots = []
    for i in range(pieces):
        g_ref, spot, where = g_refs[i // g_pieces], i % g_pieces, idx[pieces + i]
        spots.append((g_ref, spot, pl.ds(pl.multiple_of(where * rows, rows), rows)))
        at = pl.ds(where * blocks, blocks)
        pltpu.make_async_copy(g_down.at[at], g_ref.at[spot, pl.ds(1 + blocks, blocks)], g_sem).start()
    for g_ref, spot, at in spots:
        pltpu.make_async_copy(g_up.at[:, at, :], g_ref.at[spot, pl.ds(1, blocks)], g_sem).start()
    out_ref[...] = total.astype(BF)
    cot_f = cot.astype(F32)
    d_middle = cot_f + norm_back(d_norm, plain, inverse, gain)
    dmid_ref[...] = d_middle
    d_branch = d_middle.astype(BF)
    g_out[...] = mm_tn(attended, d_branch).astype(BF)
    for g_ref, spot, at in spots:
        pltpu.make_async_copy(g_out.at[at, :], g_ref.at[spot, 0], g_sem).start()
    d_att = mm_nt(d_branch, w_out[...]).astype(BF) * live.astype(BF)
    d_ref[:, :width] = d_att
    product = d_att.astype(F32) * mixed
    deltas = [
        jnp.sum(product[:, h * HEAD_DIM : (h + 1) * HEAD_DIM], axis=-1, keepdims=True) for h in range(HEADS)
    ]
    d_ref[:, width:] = (in_parts(deltas, lane, 0) + in_parts(logs, lane, 3 * HEADS)).astype(BF)

    sums = [jnp.sum(v, axis=0, keepdims=True) for v in (d_middle, d_norm * plain, d_norm, cot_f)]
    sums = jnp.concatenate(sums + up_sums + [jnp.zeros((HEAD_DIM - 4 - blocks, width), F32)], axis=0)
    columns = jnp.transpose(sums)
    if pieces > 1:
        per = pieces // blocks
        vec_ref[...] = jnp.where(lane < 4, columns, 0.0)
        for j in range(blocks):
            column = jnp.broadcast_to(columns[:, 4 + j : 5 + j], (width, HEAD_DIM)).reshape(
                per, blocks, rows, HEAD_DIM
            )
            wide_lane = lane.reshape(1, 1, HEAD_DIM)
            placed = sum(jnp.where(wide_lane == 4 + i, column[:, i], 0.0) for i in range(blocks))
            vec_ref[j * per * rows : (j + 1) * per * rows, :] += placed.reshape(per * rows, HEAD_DIM)
    else:
        vec_ref[...] = jnp.where(lane < 4 + blocks, columns, 0.0)
    for g_ref in g_refs:
        pltpu.make_async_copy(g_ref, g_ref, g_sem).wait()


def back_unit(sc, tab, plane, kv_ref, spot, q_ref, do_refs, stat_refs, dq_refs, put, none):
    count = tab.shape[0] // 3
    rows = kv_ref.shape[2]
    min_low, max_high, max_low, min_high = reach(sc, tab, rows)
    low, high, unused = table_of(tab, count, plane_rows(sc, rows, (1, PLANE * rows), 1))
    start = sc[1 + PLANE + plane]
    needed = (start < max_high) & (start + rows > min_low)
    whole = (start >= max_low) & (start + rows <= min_high)

    def unit(masked):
        k_pos = start + lax.broadcasted_iota(I32, (rows, 1), 0)
        for h in range(HEADS):
            key, value = kv_ref[spot, h], kv_ref[spot, HEADS + h]
            d_key, d_value = 0.0, 0.0
            for half in do_refs:
                at = slice(2 * half * rows, 2 * (half + 1) * rows)
                q, do, stat_ref = q_ref[h, at], do_refs[half][h], stat_refs[half]
                soft = jnp.exp2(mm_nt(key, q) - stat_ref[HEADS + h : HEADS + h + 1, :])
                if masked:
                    soft = jnp.where((k_pos >= low[:, at]) & (k_pos < high[:, at]), soft, 0.0)
                d_soft = mm_nt(value, do)
                d_scores = (soft * (d_soft - stat_ref[h : h + 1, :])).astype(BF)
                d_value = d_value + mm(soft.astype(BF), do)
                d_key = d_key + mm(d_scores, q)
                dq_refs[half][h] += mm_tn(key, d_scores)
            put(slice(h * HEAD_DIM, (h + 1) * HEAD_DIM), d_key * (SCALE / SCALE2))
            put(slice((HEADS + h) * HEAD_DIM, (HEADS + h + 1) * HEAD_DIM), d_value)

    @pl.when(needed & whole)
    def _():
        unit(False)

    @pl.when(needed & jnp.logical_not(whole))
    def _():
        unit(True)

    @pl.when(jnp.logical_not(needed))
    def _():
        none()


def unpack_rows(packets, do_ref, stat_ref):
    rows, width = packets[0].shape[0], HEADS * HEAD_DIM
    for b, ref in enumerate(packets):
        at = slice(b * rows, (b + 1) * rows)
        for h in range(HEADS):
            do_ref[h, at] = ref[:, h * HEAD_DIM : (h + 1) * HEAD_DIM]
        tail = jnp.transpose(ref[:, width:].astype(F32))
        parts = [tail[i * HEADS : (i + 1) * HEADS] for i in range(6)]
        stat_ref[:, at] = jnp.concatenate([parts[0] + parts[1] + parts[2], parts[3] + parts[4] + parts[5]], axis=0)


def open_body(sc, tab, q_ref, d_own, d_c, kv_ref, do_ref, stat_ref, dq_ref, part_ref, *, units):
    unpack_rows((d_own, d_c), do_ref, stat_ref)
    dq_ref[...] = jnp.zeros(dq_ref.shape, F32)
    for j, (plane, spot) in enumerate(units):

        def put(lanes, value, j=j):
            part_ref[j, :, lanes] = value

        def none(j=j):
            part_ref[j] = jnp.zeros(part_ref.shape[1:], F32)

        back_unit(sc, tab, plane, kv_ref, spot, q_ref, {0: do_ref}, {0: stat_ref}, {0: dq_ref}, put, none)


def keep_planes(units, n_ref, w_ref, d_refs, nk_ref, sum_ref, nk_in, sum_in, dkv_scr):
    width = w_ref.shape[1]
    ones = jnp.ones((8, dkv_scr.shape[1]), BF)
    product = 0.0 if nk_in is None else nk_in[...]
    sums = 0.0 if sum_in is None else sum_in[...]
    for j, (unused, spot) in enumerate(units):
        d_refs[j][...] = (mm_nt(dkv_scr[j, :, :width], w_ref[1]) + mm_nt(dkv_scr[j, :, width:], w_ref[2])).astype(BF)
        product = product + mm_tn(n_ref[spot], dkv_scr[j])
        sums = sums + mm(ones, dkv_scr[j])
    nk_ref[...] = product
    sum_ref[...] = sums


def close_body(
    sc, tab, q_ref, d_x, d_xc, kv_ref, n_ref, w_ref, part_ref, do_ref, stat_ref, dq_ref, nk_ref, sum_ref, *refs, units
):
    d_refs, dkv_scr = refs[:-1], refs[-1]
    unpack_rows((d_x, d_xc), do_ref, stat_ref)
    dq_ref[...] = jnp.zeros(dq_ref.shape, F32)
    for j, (plane, spot) in enumerate(units):

        def put(lanes, value, j=j):
            dkv_scr[j, :, lanes] = (part_ref[j, :, lanes] + value).astype(BF)

        def none(j=j):
            dkv_scr[j] = jnp.zeros(dkv_scr.shape[1:], BF)

        back_unit(sc, tab, plane, kv_ref, spot, q_ref, {1: do_ref}, {1: stat_ref}, {1: dq_ref}, put, none)
    keep_planes(units, n_ref, w_ref, d_refs, nk_ref, sum_ref, None, None, dkv_scr)


def back_body(
    sc, tab, q_ref, do_one, do_two, stat_one, stat_two, kv_ref, n_ref, w_ref, one_in, two_in, nk_in, sum_in,
    d_ref, one_ref, two_ref, nk_ref, sum_ref, dkv_scr, *, unit,
):
    one_ref[...] = one_in[...]
    two_ref[...] = two_in[...]

    def put(lanes, value):
        dkv_scr[0, :, lanes] = value.astype(BF)

    def none():
        dkv_scr[0] = jnp.zeros(dkv_scr.shape[1:], BF)

    halves = {0: do_one, 1: do_two}, {0: stat_one, 1: stat_two}, {0: one_ref, 1: two_ref}
    back_unit(sc, tab, unit[0], kv_ref, unit[1], q_ref, *halves, put, none)
    keep_planes([unit], n_ref, w_ref, [d_ref], nk_ref, sum_ref, nk_in, sum_in, dkv_scr)


def query_block(dq_refs, b, rows):
    ref, at = dq_refs[b // 2], slice((b % 2) * rows, (b % 2 + 1) * rows)
    return jnp.concatenate([ref[h, :, at] * SCALE for h in range(HEADS)], axis=0).astype(BF)


def message_body(idx, *refs, rows):
    n_refs, dq_refs = refs[:PLANE], refs[PLANE : PLANE + 2]
    (nk_ref, sum_ref, w_ref, col_ref, vec_ref), (full, vec) = refs[PLANE + 2 : PLANE + 7], refs[-2:]
    msg_refs = refs[PLANE + 7 : -2]
    local = n_refs[0].shape[1]
    width = w_ref.shape[1]
    q_product = jnp.zeros((width, width), F32)
    q_sums = jnp.zeros((8, width), F32)
    ones = jnp.ones((8, local), BF)
    for b, n_ref in enumerate(n_refs):
        d_query = query_block(dq_refs, b, local)
        q_product += lax.dot_general(n_ref[0], d_query, (((0,), (1,)), ((), ())), preferred_element_type=F32)
        q_sums += mm_nt(ones, d_query)
    gain, shift = col_ref[:, 0:1], col_ref[:, 1:2]
    lane = lax.broadcasted_iota(I32, (1, HEAD_DIM), 1)
    gain_grad = jnp.zeros((width, 1), F32)
    shift_grad = jnp.zeros((width, 1), F32)
    columns = []
    for i in range(3):
        lanes = slice(i * width, (i + 1) * width)
        if i == 0:
            product, sums = q_product, q_sums[0:1]
        else:
            at = slice((i - 1) * width, i * width)
            product, sums = nk_ref[:, at], sum_ref[0:1, at]
        weight = w_ref[i].astype(F32)
        full[:, lanes] = (product * gain + shift * sums).astype(BF)
        gain_grad += jnp.sum(product * weight, axis=-1, keepdims=True)
        shift_grad += jnp.sum(weight * sums, axis=-1, keepdims=True)
        if i != 1:
            columns.append(jnp.transpose(jnp.broadcast_to(sums, (HEAD_DIM, width))))
    vec[...] = vec_ref[...]
    for at, column in ((8, gain_grad), (9, shift_grad), (10, columns[0]), (11, columns[1])):
        vec[...] += jnp.where(lane == at, column, 0.0)
    full[:, 3 * width :] = vec[...].astype(BF)
    k = 0
    for msg_ref in msg_refs:
        for i in range(msg_ref.shape[0]):
            msg_ref[i] = full[pl.ds(pl.multiple_of(idx[k] * rows, rows), rows), :]
            k += 1


def query_body(dq_one, dq_two, w_ref, keep_ref, send_ref):
    rows = keep_ref.shape[1]
    for b in range(PLANE):
        d_query = query_block((dq_one, dq_two), b, rows)
        out = lax.dot_general(d_query, w_ref[0], (((0,), (1,)), ((), ())), preferred_element_type=F32)
        (keep_ref, send_ref)[b % 2][b // 2] = out.astype(BF)


def finish_body(tok_ref, dmid_ref, row_ref, last_ref, *refs):
    plain, inverse = normalize(tok_ref[...].astype(F32))
    lines = 0 if len(last_ref.shape) == 2 else tok_ref.shape[0] // last_ref.shape[1]
    last = last_ref[:lines].reshape(tok_ref.shape) if lines else last_ref[...]
    total = last.astype(F32)
    for ref in refs[:-1]:
        total = total + ref[...].astype(F32)
    refs[-1][...] = (dmid_ref[...] + norm_back(total, plain, inverse, row_ref[0:1, :])).astype(BF)


def matrices_body(*refs, starts):
    terms, (out_ref, up_ref, down_ref) = refs[:-3], refs[-3:]
    width = out_ref.shape[1]
    part = out_ref.shape[0]
    blocks = up_ref.shape[1] // width

    def block(i):
        total = terms[0][starts[0] + i].astype(F32)
        for term, start in zip(terms[1:], starts[1:], strict=True):
            total = total + term[start + i].astype(F32)
        return total

    out_ref[...] = block(0)
    for j in range(blocks):
        up_ref[:, j * width : (j + 1) * width] = block(1 + j)
        down_ref[j * part : (j + 1) * part, :] = block(1 + blocks + j)


def unpack_body(*refs, w_blocks):
    terms, (qkv_ref, *vec_refs, up_ref, pad_ref) = refs[:-11], refs[-11:]
    total = terms[0][...]
    for term in terms[1:]:
        line = jnp.concatenate([term[j] for j in range(w_blocks)], axis=1)
        total = total + line[:, : total.shape[1]].astype(F32)
    width = qkv_ref.shape[1]
    part = qkv_ref.shape[0]
    qkv_ref[...] = total[:, :width]
    pad_ref[...] = jnp.zeros(pad_ref.shape, F32)
    pad_ref[:part] = total[:, width:]
    rows = jnp.transpose(pad_ref[...])
    for ref, row in zip(vec_refs, (8, 9, 10, 11, 0, 1, 2, 3), strict=True):
        ref[...] = rows[row : row + 1, :part]
    up_ref[...] = rows[4 : 4 + up_ref.shape[0], :part]


def shards(
    tokens, w_qkv, w_out, w_up, w_down,
    norm1_gain, norm1_bias, query_bias, value_bias, out_bias, norm2_gain, norm2_bias, up_bias, down_bias,
    cotangent, table_start, support_count, query_count, *, R, F,
):
    A = R // PLANE
    count = R * F
    local, width = tokens.shape[1], tokens.shape[2]
    part = w_qkv.shape[0]
    hidden = w_up.shape[1]
    blocks = hidden // width
    aligned = part % 16 == 0
    rows = part if aligned else width
    pieces = count if aligned else 1
    sds = jax.ShapeDtypeStruct

    r, f = lax.axis_index("rows"), lax.axis_index("fsdp")
    a, x, c = r // PLANE, (r // 2) % 2, r % 2

    def swap_c(v):
        return lax.ppermute(v, "rows", [(i, i ^ 1) for i in range(R)])

    def swap_x(v):
        return lax.ppermute(v, "rows", [(i, i ^ 2) for i in range(R)])

    def turn_a(v, s):
        return lax.ppermute(
            v, "rows", [(i, ((i // PLANE + s) % A) * PLANE + i % PLANE) for i in range(R)]
        )

    def turn_f(v, t):
        return lax.ppermute(v, "fsdp", [(i, (i + t) % F) for i in range(F)])

    def turn_xf(v, t):
        return lax.ppermute(
            v, ("rows", "fsdp"),
            [(i * F + j, (i ^ 2) * F + (j + t) % F) for i in range(R) for j in range(F)],
        )

    def owners(order):
        cr, t, xr, s = (np.array(list(z), np.int32) for z in zip(*order, strict=True))
        plane = lax.rem(a - s + A, A)
        return (((plane * 2 + (x ^ xr)) * 2 + (c ^ cr)) * F + lax.rem(f - t + F, F)).astype(I32)

    block_x, block_c = np.array([0, 0, 1, 1], np.int32), np.array([0, 1, 0, 1], np.int32)
    block_start = (a * 4 + (x ^ block_x) * 2 + (c ^ block_c)) * local
    unit_start = (lax.rem(a - np.arange(A, dtype=np.int32) + A, A) * 4 + 2 * x + c) * local
    sc = jnp.concatenate([(a * 4 * local)[None], block_start, unit_start]).astype(I32)
    tab = jnp.concatenate([table_start[0], support_count[0], query_count[0]])
    q_order = [(cr, t, xr, s) for cr in range(2) for t in range(F) for xr in range(2) for s in range(A)]
    parts = [slice(0, A // 2), slice(A // 2, A)]
    m_order = [
        (cr, t, xr, s)
        for cr in range(2)
        for planes in (range(2, A), range(2))
        for xr, t in [(0, 0), (1, 0)] + [(0, t) for t in range(1, F)] + [(1, t) for t in range(1, F)]
        for s in planes
    ]
    every_owner = owners(q_order + m_order)
    q_owner, m_owner = every_owner[:count], every_owner[count:]
    if aligned:
        q_idx, idx = q_owner, jnp.concatenate([m_owner, q_owner])
    else:
        q_idx, idx = jnp.zeros((1,), I32), jnp.zeros((2,), I32)

    near = list(range(1, A))
    early, late = near[:2], near[2:]
    own = tokens[0]
    vectors = [
        v.reshape(1, -1)
        for v in (
            norm1_gain, norm1_bias, query_bias, value_bias, out_bias, norm2_gain, norm2_bias, down_bias, up_bias
        )
    ]
    wide = 3 * width + HEAD_DIM
    pack_in = [w_qkv, w_out, w_up, w_down, *vectors]
    q_own, m_own = pl.pallas_call(
        pack_body,
        grid=(1,),
        out_shape=[sds((4, part, width), BF), sds((1 + 2 * blocks, part, width), BF)],
        in_specs=[pl.BlockSpec(v.shape, lambda i: (0, 0)) for v in pack_in],
        out_specs=[VMEM] * 2,
        scratch_shapes=[pltpu.VMEM((HEAD_DIM, HEAD_DIM), F32)],
        compiler_params=pltpu.CompilerParams(vmem_limit_bytes=56 * MIB),
        cost_estimate=pl.CostEstimate(flops=0, bytes_accessed=16 * part * width, transcendentals=0),
        name="pack",
    )(*pack_in)
    tok_z, m_z = {0: own}, {0: m_own}
    *q_z, tok_z[1], m_z[1], sc, tab, q_idx, idx = together(
        *(turn_a(q_own, s) for s in range(1, A)), turn_a(own, 1), turn_a(m_own, 1), sc, tab, q_idx, idx
    )
    q_z = jnp.stack([q_own] + q_z)
    moved = [swap_x(q_z)] + [v for t in range(1, F) for v in (turn_f(q_z, t), turn_xf(q_z, t))]
    *q_far, tok_z[2], m_z[2] = together(*moved, turn_a(tok_z[1], 1), turn_a(m_z[1], 1))
    tok_early, m_early = jnp.stack([tok_z[1], tok_z[2]]), jnp.stack([m_z[0], m_z[1]])
    early_x, early_f = swap_x(m_early), [turn_f(m_early, t) for t in range(1, F)]
    tok_z[3], m_z[3] = turn_a(tok_z[2], 1), turn_a(m_z[2], 1)
    q_four = jnp.stack([q_z] + q_far)
    q_other = swap_c(q_four)
    q_pieces = [q_four.reshape(count // 2, 4, part, width), q_other.reshape(count // 2, 4, part, width)]
    if not aligned:
        stacked = jnp.concatenate(q_pieces)
        by_owner = jnp.zeros_like(stacked).at[q_owner].set(stacked)
        q_pieces = [by_owner.transpose(1, 0, 2, 3).reshape(1, 4, width, width)]
    key_shape = (2 * HEADS, local, HEAD_DIM)
    w_all, row_vec, col_vec, up_row, kv_early, n_early, q, n_first = call(
        functools.partial(ready_body, rows=rows, count=len(q_pieces), part=part),
        [
            sds((3, width, width), BF), sds((16, width), F32), sds((width, HEAD_DIM), F32), sds((blocks, width), F32),
            sds((3,) + key_shape, BF), sds((3, local, width), BF), sds((HEADS, local, HEAD_DIM), BF),
            sds((1, local, width), BF),
        ],
        [q_idx, *q_pieces, own, tok_early], [SMEM] + [HBM] * len(q_pieces) + [VMEM] * 2, [VMEM] * 8,
        scratch=[pltpu.VMEM((width, HEAD_DIM), BF), pltpu.SemaphoreType.DMA((2,))],
        flops=4 * (A + 1) * local * width * width, moved=4 * width * wide, vmem=12, name="ready",
    )

    tok_z[3], m_z[3], early_x, q_x, *early_f = together(tok_z[3], m_z[3], early_x, swap_x(q), *early_f)
    for s in range(4, A):
        tok_z[s], m_z[s] = together(turn_a(tok_z[s - 1], 1), turn_a(m_z[s - 1], 1))
    q_blocks = [q, swap_c(q), q_x, swap_c(q_x)]
    late = list(range(3, A))
    tok_late = jnp.stack([tok_z[s] for s in late]) if A > 4 else tok_z[3][None]
    m_late = stack([m_z[s] for s in range(2, A)])
    late_x, late_f = swap_x(m_late), [turn_f(m_late, t) for t in range(1, F)]
    early_xf = [turn_f(early_x, t) for t in range(1, F)]
    kv_late, n_late = call(
        functools.partial(project_body, with_q=False, spots=[(0, i) for i in range(len(late))], count=1),
        [sds((len(late),) + key_shape, BF), sds((len(late), local, width), BF)],
        [after(tok_late, m_late), w_all, row_vec], [VMEM] * 3, [VMEM] * 2,
        flops=4 * len(late) * local * width * width, moved=8 * len(late) * local * width, vmem=8, name="project",
    )
    where = {s: (kv_early, n_early, s) if s < 3 else (kv_late, n_late, s - 3) for s in range(A)}

    unit = PLANE * local
    work = 4 * unit * A * local * width
    packet = width + HEAD_DIM
    att_keep, att_send, q_plane = call(
        functools.partial(attend_body, kv_units=list(range(A))),
        [sds((2, local, packet), F32)] * 2 + [sds((HEADS, unit, HEAD_DIM), BF)],
        [sc, tab, *q_blocks, kv_early, kv_late], [SMEM, SMEM] + [VMEM] * PLANE + [ANY] * 2, [VMEM] * 3,
        scratch=[
            pltpu.VMEM((A, HEADS, unit, local), F32),
            pltpu.VMEM((HEADS, unit, HEAD_DIM), F32), pltpu.VMEM((HEADS, unit, 2 * HEAD_DIM), F32),
            pltpu.VMEM((A, 2 * HEADS, local, HEAD_DIM), BF), pltpu.SemaphoreType.DMA((A,)),
        ],
        flops=work, moved=8 * A * local * width, trans=HEADS * unit * A * local, vmem=10 + 5 * A, name="attend",
    )
    early_side = [m_early, early_x, *early_f]
    att_keep, att_send, late_x, *more = together(
        att_keep, att_send, late_x, *late_f, *(swap_c(v) for v in early_side[:2])
    )
    late_f, early_c = list(more[: F - 1]), list(more[F - 1 :])
    att_recv = swap_c(att_send)
    late_xf = [turn_f(late_x, t) for t in range(1, F)]
    att_own, att_far = call(
        merge_body, [sds((local, packet), F32), sds((local, packet), BF)], [att_keep, att_recv], [VMEM] * 2,
        [VMEM] * 2, flops=32 * local * packet, moved=20 * local * packet, vmem=8, name="merge",
    )
    late_side = [m_late, late_x, *late_f]
    att_other, *more = together(
        swap_x(att_far), *late_xf, *(swap_c(v) for v in [*early_f, *early_xf, *late_side])
    )
    late_xf, more = list(more[: F - 1]), list(more[F - 1 :])
    early_c += more[: 2 * F - 2]
    late_c = more[2 * F - 2 :] + [swap_c(v) for v in late_xf]
    m_arrays = late_side + late_xf + early_side + early_xf + late_c + early_c
    if not aligned:
        stacked = jnp.concatenate(m_arrays)
        by_owner = jnp.zeros_like(stacked).at[m_owner].set(stacked)
        m_arrays = [
            jnp.concatenate(
                [
                    by_owner[:, 0].reshape(1, width, width),
                    by_owner[:, 1 : 1 + blocks].transpose(1, 0, 2, 3).reshape(blocks, width, width),
                    by_owner[:, 1 + blocks :].reshape(blocks, width, width),
                ]
            )[None]
        ]

    spots = [(t, xr) for t in range(F) for xr in range(2)]
    grad_count = 4 * F if aligned else 1
    g_shape = sds((pieces // grad_count, 1 + 2 * blocks, rows, width), BF)
    got = call(
        functools.partial(middle_body, rows=rows, m_count=len(m_arrays), grad_count=grad_count),
        [
            sds((local, width), BF), sds((local, width), F32), sds((local, packet), BF), sds((width, HEAD_DIM), F32),
        ] + [g_shape] * grad_count,
        [idx, sc, tab, *m_arrays, own, att_own, att_other, cotangent[0], row_vec, up_row],
        [SMEM] * 3 + [HBM] * len(m_arrays) + [VMEM] * 6,
        [VMEM] * 4 + [HBM] * grad_count,
        scratch=[
            pltpu.VMEM((width, width), BF), pltpu.VMEM((blocks, width, width), BF),
            pltpu.VMEM((pieces * blocks, rows, width), BF),
            pltpu.VMEM((width, width), BF), pltpu.VMEM((blocks, width, width), BF),
            pltpu.VMEM((pieces * blocks, rows, width), BF), pltpu.VMEM((blocks, local, width), F32),
            pltpu.SemaphoreType.DMA((3,)), pltpu.SemaphoreType.DMA,
        ],
        flops=6 * local * width * width * (1 + 2 * blocks), moved=4 * width * width * (1 + 2 * blocks),
        trans=local * hidden, vmem=52, name="middle",
    )
    *got, n_x = together(*got, swap_x(after(n_first, att_other)))
    outputs, d_middle, d_own, vec = got[:4]
    grads = got[4:]
    d_c = swap_c(d_own)

    lead = (A, 1 + 2 * blocks, part, width)
    if aligned:
        relative = [g.reshape(lead) for g in grads]
    else:
        whole = grads[0][0]
        by_owner = jnp.concatenate(
            [
                whole[0].reshape(count, 1, part, width),
                whole[1 : 1 + blocks].reshape(blocks, count, part, width).transpose(1, 0, 2, 3),
                whole[1 + blocks :].reshape(count, blocks, part, width),
            ],
            axis=1,
        )
        by_owner = by_owner[q_owner].reshape((4 * F,) + lead)
        relative = [by_owner[i] for i in range(4 * F)]
    g_near = {spot: relative[i] for i, spot in enumerate(spots)}
    g_far = {spot: swap_c(after(relative[2 * F + i], d_c)) for i, spot in reversed(list(enumerate(spots)))}

    def sums_of(keys, half, *others):
        arrays = [g_near[keys], g_far[keys], *others]
        return add_up(arrays, [[(0, (half,)), (1, (half,))] + [(2 + i, ()) for i in range(len(others))]])[0]

    first, second = parts
    half = A // 2
    ways = {}

    def joined(keys, planes):
        arrays = [v for key in keys for v in (g_near[key], g_far[key])]
        return join_up(arrays, [[(2 * i, (planes,)), (2 * i + 1, (planes,))] for i in range(len(keys))])[0]

    def start_ways(step):
        if step == 1:
            for t in range(1, F):
                ways["f", t] = turn_f(joined([(t, 1), (t, 0)], first), F - t)
            ways["x"] = swap_x(joined([(t, 1) for t in range(F)], second))
        if step == 2:
            return [("f", t) for t in range(1, F)] + ["x"]
        if step == 3:
            arrays = [g_near[0, 1], g_far[0, 1], *(ways["f", t] for t in range(1, F))]
            plan = [[(0, (first,)), (1, (first,))] + [(1 + t, (slice(0, half),)) for t in range(1, F)]]
            ways["x", F] = swap_x(add_up(arrays, plan)[0])
            for t in range(1, F):
                arrays = [g_near[t, 0], g_far[t, 0], ways["x"]]
                plan = [[(0, (second,)), (1, (second,)), (2, (slice(t * half, (t + 1) * half),))]]
                ways["f2", t] = turn_f(add_up(arrays, plan)[0], F - t)
            return [("x", F)] + [("f2", t) for t in range(1, F)]
        return []

    pair = [(s, where[s][2]) for s in (1, 2)]
    dq_shape = sds((HEADS, HEAD_DIM, 2 * local), F32)
    half_shapes = [sds((HEADS, 2 * local, HEAD_DIM), BF), sds((2 * HEADS, 2 * local), F32), dq_shape]
    keys = list(g_far)
    do_one, stat_one, dq_one, part_sums, d_x, *more = together(
        *call(
            functools.partial(open_body, units=pair), [*half_shapes, sds((2, local, 2 * width), F32)],
            [sc, tab, q_plane, d_own, d_c, kv_early], [SMEM] * 2 + [VMEM] * 4, [VMEM] * 4,
            flops=2 * work // A, moved=16 * unit * width, trans=HEADS * unit * local, vmem=16, name="open",
        ),
        swap_x(d_own), *(g_far[k] for k in keys),
    )
    g_far.update(zip(keys, more, strict=True))
    d_xc = swap_c(d_x)
    start_ways(1)
    got = together(
        *call(
            functools.partial(close_body, units=pair),
            [*half_shapes, sds((width, 2 * width), F32), sds((8, 2 * width), F32)] + [sds((local, width), BF)] * 2,
            [sc, tab, q_plane, d_x, d_xc, kv_early, n_early, w_all, part_sums],
            [SMEM] * 2 + [VMEM] * 7, [VMEM] * 7, scratch=[pltpu.VMEM((2, local, 2 * width), BF)],
            flops=3 * work // A, moved=16 * unit * width, trans=HEADS * unit * local, vmem=16, name="close",
        ),
    )
    do_two, stat_two, dq_two, n_product, sums, d_sum, d_next = got
    carried = [dq_one, dq_two, n_product, sums]
    q_now = q_plane
    for step, s in enumerate([*near[2:], 0], 1):
        kv_now, n_now, spot = where[s]
        outs = call(
            functools.partial(back_body, unit=(s, spot)),
            [sds((local, width), BF), dq_shape, dq_shape, sds((width, 2 * width), F32), sds((8, 2 * width), F32)],
            [sc, tab, q_now, do_one, do_two, stat_one, stat_two, kv_now, n_now, w_all, *carried],
            [SMEM] * 2 + [VMEM] * 12, [VMEM] * 5, scratch=[pltpu.VMEM((1, local, 2 * width), BF)],
            flops=work // A * 5 // 2 + 8 * local * width * width, moved=16 * unit * width,
            trans=HEADS * unit * local, name="back",
        )
        keys = start_ways(step + 1)
        got = together(*outs, turn_a(d_sum, 1), *(ways[k] for k in keys))
        outs, d_recv = got[:5], got[5]
        ways.update(zip(keys, got[6:], strict=True))
        (d_sum,) = add_up([d_next, d_recv], [[(0, ()), (1, ())]])
        d_next, *carried = outs
        q_now = after(q_plane, d_sum)

    dq_one, dq_two, n_product, sums = carried
    n_blocks = [n_first, swap_c(n_first), n_x, swap_c(n_x)]

    half_count = 2 * F
    msg_lead = (A, part, wide)
    msg_shape = [sds((pieces // 2, rows, wide), BF)] * 2 if aligned else [sds((1, rows, wide), BF)]
    message = call(
        functools.partial(message_body, rows=rows),
        msg_shape,
        [q_idx, *n_blocks, dq_one, dq_two, n_product, sums, w_all, col_vec, vec],
        [SMEM] + [VMEM] * (7 + PLANE), [VMEM] * len(msg_shape),
        scratch=[pltpu.VMEM((width, wide), BF), pltpu.VMEM((width, HEAD_DIM), F32)],
        flops=2 * local * width * width, moved=8 * width * wide, vmem=8, name="message",
    )
    g_sums = {}
    arrays = [g_near[0, 0], g_far[0, 0], ways["x", F], *(ways["f", t] for t in range(1, F))]
    plan = [
        [(0, (s,)), (1, (s,)), (2, (s,))] + [(2 + t, (half + s,)) for t in range(1, F)] for s in range(half)
    ]
    g_sums.update(zip(range(half), add_up(arrays, plan), strict=True))
    arrays = [g_near[0, 0], g_far[0, 0], ways["x"], *(ways["f2", t] for t in range(1, F))]
    plan = [
        [(0, (s,)), (1, (s,)), (2, (s - half,))] + [(2 + t, (s - half,)) for t in range(1, F)]
        for s in range(half, A)
    ]
    g_sums.update(zip(range(half, A), add_up(arrays, plan), strict=True))
    if not aligned:
        flat = message[0][0]
        at = slice(3 * width + 4, 3 * width + 4 + blocks)
        up_part = flat[:, at].T.reshape(count, blocks, part)
        by_owner = flat.reshape(count, part, wide)
        by_owner = by_owner.at[:, :, at].set(up_part.transpose(0, 2, 1))
        by_owner = by_owner[q_owner]
        message = [by_owner[: count // 2], by_owner[count // 2 :]]
    w_far = swap_c(message[1])
    w_far = w_far.reshape((half_count,) + msg_lead)
    w_near = message[0].reshape((half_count,) + msg_lead)
    w_both = add_up([w_near, w_far], [[(0, (i,)), (1, (i,))] for i in range(half_count)])
    got = []
    for (t, xr), sent in zip(spots, w_both, strict=True):
        if xr:
            sent = turn_xf(sent, F - t) if t else swap_x(sent)
        elif t:
            sent = turn_f(sent, F - t)
        got.append(sent)
    lines = local // part
    every = ()
    d_line = d_sum.reshape(lines, part, width)
    sent = lay_out([d_line, g_sums[A - 1]], [(False, [(0, every)]), (False, [(1, every)])], part, width)
    *got, arrived, g_two = together(*got, turn_a(sent, 1), turn_a(g_sums[2], A - 2))
    w_terms = {s: [(i, (s,)) for i in range(len(got))] for s in range(A)}
    w_blocks = -(-wide // width)
    packs = {}
    for s in near:
        arrays, plan = list(got), [(True, w_terms[s])]
        if s not in (2, A - 1):
            arrays.append(g_sums[s])
            plan.append((False, [(len(got), every)]))
        packs[s] = turn_a(lay_out(arrays, plan, part, width), A - s)
    (w_own,) = add_up(got, [w_terms[0]], F32)
    grad_qkv, *vector_grads, up_grad = call(
        functools.partial(unpack_body, w_blocks=w_blocks),
        [sds((part, 3 * width), F32)] + [sds((1, part), F32)] * 8 + [sds((blocks, part), F32)],
        [w_own, *packs.values()], [VMEM] * A, [VMEM] * 10, scratch=[pltpu.VMEM((HEAD_DIM, HEAD_DIM), F32)],
        moved=16 * part * width, vmem=8, name="unpack",
    )

    others = [s for s in near if s not in (2, A - 1)]
    starts = [0, lines, 0] + [w_blocks] * len(others)
    grad_out, grad_up, grad_down = call(
        functools.partial(matrices_body, starts=starts),
        [sds((part, width), F32), sds((part, hidden), F32), sds((blocks * part, width), F32)],
        [g_sums[0], arrived, g_two, *(packs[s] for s in others)], [VMEM] * A, [VMEM] * 3,
        moved=6 * A * g_sums[0].size, vmem=8, name="matrices",
    )
    d_last = arrived if aligned else arrived[:lines].reshape(local, width)
    query_keep, query_send = call(
        query_body, [sds((2, local, width), BF)] * 2, [after(dq_one, got[-1]), dq_two, w_all], [VMEM] * 3, [VMEM] * 2,
        flops=8 * local * width * width, moved=8 * local * width, vmem=8, name="query",
    )
    query_own, query_far = add_up([query_keep, swap_c(query_send)], [[(0, (b,)), (1, (b,))] for b in range(2)])
    grad_tokens = call(
        finish_body, sds((local, width), BF),
        [own, d_middle, row_vec, d_last, d_next, query_own, swap_x(query_far)],
        [VMEM] * 7, VMEM, flops=20 * local * width, moved=16 * local * width, vmem=8, name="finish",
    )
    return (
        outputs[None],
        grad_tokens[None],
        grad_qkv,
        grad_out,
        grad_up,
        grad_down,
        *(v.reshape(part) for v in vector_grads[:7]),
        up_grad.reshape(blocks * part),
        vector_grads[7].reshape(part),
    )


def solution(mesh):
    both = ("rows", "fsdp")
    matrix, vector, act, table = P(both, None), P(both), P("fsdp", "rows", None), P("fsdp", None)
    return jax.shard_map(
        functools.partial(shards, R=mesh.shape["rows"], F=mesh.shape["fsdp"]),
        mesh=mesh,
        in_specs=(act,) + (matrix,) * 4 + (vector,) * 9 + (act,) + (table,) * 3,
        out_specs=(act, act) + (matrix,) * 4 + (vector,) * 9,
        check_vma=False,
    )
```

```python
import functools
import math

import jax
import jax.numpy as jnp
import numpy as np
from jax import lax
from jax.experimental import pallas as pl
from jax.experimental.pallas import tpu as pltpu
from jax.sharding import PartitionSpec as P

HEADS = 4
HEAD_DIM = 128
EPS = 1e-05
NEG = -1e30
PLANE = 4
MIB = 1024 * 1024
BF = jnp.bfloat16
F32 = jnp.float32
I32 = jnp.int32
SCALE = 1.0 / math.sqrt(HEAD_DIM)
SCALE2 = SCALE * math.log2(math.e)
GELU_A = math.sqrt(2.0 / math.pi)
GELU_B = 0.044715

VMEM = pl.BlockSpec(memory_space=pltpu.VMEM)
SMEM = pl.BlockSpec(memory_space=pltpu.SMEM)
HBM = pl.BlockSpec(memory_space=pltpu.HBM)
ANY = pl.BlockSpec(memory_space=pl.ANY)


def after(value, *others):
    return lax.optimization_barrier((value, *others))[0]


def together(*values):
    return lax.optimization_barrier(values)


def mm(left, right):
    return jnp.dot(left, right, preferred_element_type=F32)


def mm_nt(left, right):
    return lax.dot_general(left, right, (((1,), (1,)), ((), ())), preferred_element_type=F32)


def mm_tn(left, right):
    return lax.dot_general(left, right, (((0,), (0,)), ((), ())), preferred_element_type=F32)


def call(body, outs, ins, in_specs, out_specs, scratch=(), flops=0, moved=0, trans=0, vmem=16, name=None):
    return pl.pallas_call(
        body,
        out_shape=outs,
        in_specs=in_specs,
        out_specs=out_specs,
        scratch_shapes=scratch,
        compiler_params=pltpu.CompilerParams(vmem_limit_bytes=vmem * MIB),
        cost_estimate=pl.CostEstimate(
            flops=int(flops), bytes_accessed=int(moved), transcendentals=int(trans)
        ),
        name=name,
    )(*ins)


def normalize(values):
    centre = values - jnp.mean(values, axis=-1, keepdims=True)
    spread = jnp.mean(centre * centre, axis=-1, keepdims=True)
    inverse = lax.rsqrt(spread + EPS)
    return centre * inverse, inverse


def norm_back(grad_out, plain, inverse, gain):
    scaled = grad_out * gain
    return inverse * (
        scaled
        - jnp.mean(scaled, axis=-1, keepdims=True)
        - plain * jnp.mean(scaled * plain, axis=-1, keepdims=True)
    )


def table_of(tab, count, pos):
    low = jnp.zeros_like(pos) + tab[0]
    high = low + tab[count]
    finish = high + tab[2 * count]
    for t in range(1, count):
        here = pos >= tab[t]
        top = tab[t] + tab[count + t]
        low = jnp.where(here, tab[t], low)
        high = jnp.where(here, top, high)
        finish = jnp.where(here, top + tab[2 * count + t], finish)
    return low, high, finish


def pack_body(qkv_ref, out_ref, up_ref, down_ref, *refs):
    vec_refs, (q_ref, m_ref, vec_scr) = refs[:-3], refs[-3:]
    part, width = out_ref.shape
    blocks = up_ref.shape[1] // width
    vec_scr[...] = jnp.zeros(vec_scr.shape, F32)
    for k, ref in enumerate(vec_refs[:-1]):
        vec_scr[k : k + 1, :part] = ref[...].astype(F32)
    for j in range(blocks):
        vec_scr[8 + j : 9 + j, :part] = vec_refs[-1][:, j * part : (j + 1) * part].astype(F32)
    for i in range(3):
        q_ref[i] = qkv_ref[:, i * width : (i + 1) * width]
    q_ref[3] = jnp.zeros((part, width), BF)
    q_ref[3, :, :HEAD_DIM] = jnp.transpose(vec_scr[...])[:part].astype(BF)
    m_ref[0] = out_ref[...]
    for j in range(blocks):
        m_ref[1 + j] = up_ref[:, j * width : (j + 1) * width]
        m_ref[1 + blocks + j] = down_ref[j * part : (j + 1) * part, :]


def sum_body(*refs, plan, count):
    for out_ref, terms in zip(refs[count:], plan, strict=True):
        total = None
        for which, spot in terms:
            term = refs[which][spot].astype(F32)
            total = term if total is None else total + term
        out_ref[...] = total.astype(out_ref.dtype)


def join_body(*refs, plan, count):
    out_ref, row = refs[count], 0
    for terms in plan:
        total = None
        for which, spot in terms:
            term = refs[which][spot].astype(F32)
            total = term if total is None else total + term
        out_ref[row : row + total.shape[0]] = total.astype(out_ref.dtype)
        row += total.shape[0]


def join_up(arrays, plan):
    shapes = [jax.eval_shape(lambda v: v[terms[0][1]], arrays[terms[0][0]]).shape for terms in plan]
    shape = (sum(v[0] for v in shapes),) + shapes[0][1:]
    moved = math.prod(shape) * 4
    return call(
        functools.partial(join_body, plan=plan, count=len(arrays)), [jax.ShapeDtypeStruct(shape, BF)], arrays,
        [VMEM] * len(arrays), [VMEM], flops=moved, moved=moved, vmem=16, name="join",
    )


def lay_body(*refs, plan, count):
    out_ref, row = refs[count], 0
    width = out_ref.shape[2]
    for wide, terms in plan:
        total = None
        for which, spot in terms:
            term = refs[which][spot].astype(F32)
            total = term if total is None else total + term
        total = total.astype(out_ref.dtype)
        if wide:
            for j in range(-(-total.shape[1] // width)):
                piece = total[:, j * width : (j + 1) * width]
                if piece.shape[1] < width:
                    out_ref[row] = jnp.zeros(out_ref.shape[1:], out_ref.dtype)
                out_ref[row, :, : piece.shape[1]] = piece
                row += 1
        else:
            out_ref[row : row + total.shape[0]] = total
            row += total.shape[0]


def lay_out(arrays, plan, part, width):
    blocks = 0
    for wide, terms in plan:
        shape = jax.eval_shape(lambda v: v[terms[0][1]], arrays[terms[0][0]]).shape
        blocks += -(-shape[1] // width) if wide else shape[0]
    moved = blocks * part * width * 4
    return call(
        functools.partial(lay_body, plan=plan, count=len(arrays)), [jax.ShapeDtypeStruct((blocks, part, width), BF)],
        arrays, [VMEM] * len(arrays), [VMEM], flops=moved, moved=moved, vmem=8, name="lay",
    )[0]


def add_up(arrays, plan, dtype=BF):
    outs = []
    for terms in plan:
        which, spot = terms[0]
        outs.append(jax.ShapeDtypeStruct(jax.eval_shape(lambda v: v[spot], arrays[which]).shape, dtype))
    moved = sum(o.size for o in outs) * 4
    return call(
        functools.partial(sum_body, plan=plan, count=len(arrays)), outs, arrays,
        [VMEM] * len(arrays), [VMEM] * len(outs), flops=moved, moved=moved, vmem=16, name="add",
    )


def copy_body(*refs, plan, count):
    outs, sem = refs[count:-1], refs[-1]
    copies = []
    for k, (which, source, out, spot) in enumerate(plan):
        copies.append(pltpu.make_async_copy(refs[which].at[source], outs[out].at[spot], sem.at[k]))
        copies[-1].start()
    for copy in copies:
        copy.wait()


def copy_out(arrays, shapes, plan):
    moved = sum(math.prod(shape) for shape in shapes) * 4
    return call(
        functools.partial(copy_body, plan=plan, count=len(arrays)),
        [jax.ShapeDtypeStruct(shape, arrays[0].dtype) for shape in shapes], arrays,
        [HBM] * len(arrays), [VMEM] * len(shapes),
        scratch=[pltpu.SemaphoreType.DMA((len(plan),))], moved=moved, vmem=4, name="copy",
    )


def stack(arrays):
    shape = (len(arrays),) + arrays[0].shape
    every = (slice(None),)
    (out,) = copy_out(arrays, [shape], [(i, every, 0, (i,)) for i in range(len(arrays))])
    return out


def assemble_body(idx, *refs, rows, count):
    pieces, (w_ref, row_ref, col_ref, low_scr, sem) = refs[:count], refs[count:]
    k = 0
    for piece in pieces:
        for j in range(piece.shape[0]):
            at = pl.ds(pl.multiple_of(idx[k] * rows, rows), rows)
            pltpu.make_async_copy(piece.at[j, pl.ds(0, 3)], w_ref.at[:, at, :], sem.at[0]).start()
            pltpu.make_async_copy(piece.at[j, 3, :, pl.ds(0, HEAD_DIM)], low_scr.at[at, :], sem.at[1]).start()
            k += 1
    pltpu.make_async_copy(low_scr, low_scr, sem.at[1]).wait()
    columns = low_scr[...].astype(F32)
    col_ref[...] = columns
    row_ref[...] = jnp.transpose(columns)[: row_ref.shape[0]]
    pltpu.make_async_copy(w_ref, w_ref, sem.at[0]).wait()


def project_body(*refs, with_q, spots, count):
    pieces, (w_ref, row_ref), outs = refs[:count], refs[count : count + 2], refs[count + 2 :]
    kv_ref, n_ref = outs[:2]
    gain, shift = row_ref[0:1, :], row_ref[1:2, :]
    for i, (which, lead) in enumerate(spots):
        plain, unused_inverse = normalize(pieces[which][lead].astype(F32))
        n_ref[i] = plain.astype(BF)
        normed = (plain * gain + shift).astype(BF)
        keys = mm(normed, w_ref[1])
        values = mm(normed, w_ref[2]) + row_ref[3:4, :]
        for h in range(HEADS):
            lanes = slice(h * HEAD_DIM, (h + 1) * HEAD_DIM)
            kv_ref[i, h] = keys[:, lanes].astype(BF)
            kv_ref[i, HEADS + h] = values[:, lanes].astype(BF)
        if with_q and i == 0:
            queries = (mm(normed, w_ref[0]) + row_ref[2:3, :]) * SCALE2
            for h in range(HEADS):
                outs[2][h] = queries[:, h * HEAD_DIM : (h + 1) * HEAD_DIM].astype(BF)


def ready_body(idx, *refs, rows, count, part):
    pieces, (own_ref, tok_ref) = refs[:count], refs[count : count + 2]
    w_ref, row_ref, col_ref, up_ref, kv_ref, n_ref, q_ref, n_first, low_scr, sem = refs[count + 2 :]
    assemble_body(idx, *pieces, w_ref, row_ref, col_ref, low_scr, sem, rows=rows, count=count)
    width = up_ref.shape[1]
    blocks = up_ref.shape[0]
    per = width // blocks
    source = lax.broadcasted_iota(I32, (per, width), 0)
    target = lax.broadcasted_iota(I32, (per, width), 1)
    total = jnp.zeros((blocks, width), F32)
    for k in range(blocks):
        spread = jnp.where(
            target == (source // part) * (blocks * part) + k * part + lax.rem(source, part), 1.0, 0.0
        ).astype(BF)
        mine = [row_ref[8 + k : 9 + k, j * per : (j + 1) * per] for j in range(blocks)]
        total += mm(jnp.concatenate(mine, axis=0).astype(BF), spread)
    up_ref[...] = total
    spots = [(0, slice(None))] + [(1, i) for i in range(tok_ref.shape[0])]
    project_body(own_ref, tok_ref, w_ref, row_ref, kv_ref, n_ref, q_ref, with_q=True, spots=spots, count=2)
    n_first[0] = n_ref[0]


def reach(sc, tab, rows):
    count = tab.shape[0] // 3
    min_low, min_high, unused = table_of(tab, count, sc[0])
    max_low, max_high, unused = table_of(tab, count, sc[0] + PLANE * rows - 1)
    return min_low, max_high, max_low, min_high


def plane_rows(sc, rows, shape, dim):
    spot = lax.broadcasted_iota(I32, shape, dim)
    place = spot + sc[1]
    for b in range(1, PLANE):
        place = jnp.where(spot >= b * rows, spot + (sc[1 + b] - b * rows), place)
    return place


def attend_body(sc, tab, *refs, kv_units):
    q_refs, kv_refs = refs[:PLANE], refs[PLANE:-8]
    keep_ref, send_ref, q_scr, s_scr, m_scr, acc_scr, kv_ref, sem = refs[-8:]
    count = tab.shape[0] // 3
    units, unused, rows, unused = kv_ref.shape
    k = 0
    for ref in kv_refs:
        for i in range(ref.shape[0]):
            pltpu.make_async_copy(ref.at[i], kv_ref.at[kv_units[k]], sem.at[kv_units[k]]).start()
            k += 1
    min_low, max_high, max_low, min_high = reach(sc, tab, rows)
    q_pos = plane_rows(sc, rows, (PLANE * rows, 1), 0)
    low, high, unused = table_of(tab, count, q_pos)
    ones = jnp.ones((rows, HEAD_DIM), BF)
    for b, ref in enumerate(q_refs):
        q_scr[:, b * rows : (b + 1) * rows] = ref[...]
    m_scr[...] = jnp.full(m_scr.shape, NEG, F32)
    acc_scr[...] = jnp.zeros(acc_scr.shape, F32)

    def keep_scores(u, allowed):
        for h in range(HEADS):
            scores = mm_nt(q_scr[h], kv_ref[u, h])
            if allowed is not None:
                scores = jnp.where(allowed, scores, NEG)
            s_scr[u, h] = scores
            top = m_scr[h]
            for j in range(rows // HEAD_DIM):
                top = jnp.maximum(top, scores[:, j * HEAD_DIM : (j + 1) * HEAD_DIM])
            m_scr[h] = top

    def score_step(u, carry):
        start = sc[1 + PLANE + u]
        pltpu.make_async_copy(kv_refs[0].at[0], kv_ref.at[u], sem.at[u]).wait()
        needed = (start < max_high) & (start + rows > min_low)
        whole = (start >= max_low) & (start + rows <= min_high)

        @pl.when(needed & whole)
        def _():
            keep_scores(u, None)

        @pl.when(needed & jnp.logical_not(whole))
        def _():
            k_pos = start + lax.broadcasted_iota(I32, (1, rows), 1)
            keep_scores(u, (k_pos >= low) & (k_pos < high))

        return carry

    lax.fori_loop(0, units, score_step, 0)
    for h in range(HEADS):
        top = jnp.max(m_scr[h], axis=-1, keepdims=True)
        m_scr[h] = jnp.broadcast_to(jnp.where(top > 0.5 * NEG, top, 0.0), m_scr.shape[1:])

    def value_step(u, carry):
        start = sc[1 + PLANE + u]
        needed = (start < max_high) & (start + rows > min_low)

        @pl.when(needed)
        def _():
            for h in range(HEADS):
                soft = jnp.exp2(s_scr[u, h] - m_scr[h][:, :1]).astype(BF)
                wide = jnp.concatenate([kv_ref[u, HEADS + h], ones], axis=1)
                acc_scr[h] += mm(soft, wide)

        return carry

    lax.fori_loop(0, units, value_step, 0)
    lane = lax.broadcasted_iota(I32, (1, HEAD_DIM), 1)
    width = HEADS * HEAD_DIM
    for b in range(PLANE):
        ref, spot = (keep_ref, send_ref)[b % 2], b // 2
        at = slice(b * rows, (b + 1) * rows)
        logs = jnp.zeros((rows, HEAD_DIM), F32)
        for h in range(HEADS):
            total = acc_scr[h, at, HEAD_DIM:]
            some = total > 0.0
            safe = jnp.where(some, total, 1.0)
            ref[spot, :, h * HEAD_DIM : (h + 1) * HEAD_DIM] = acc_scr[h, at, :HEAD_DIM] / safe
            logs = jnp.where(lane == h, jnp.where(some, m_scr[h, at] + jnp.log2(safe), NEG), logs)
        ref[spot, :, width:] = logs


def in_parts(value, lane, first):
    out = jnp.zeros((value[0].shape[0], HEAD_DIM), F32)
    for h, column in enumerate(value):
        high = column.astype(BF).astype(F32)
        rest = column - high
        middle = rest.astype(BF).astype(F32)
        for i, part in enumerate((high, middle, rest - middle)):
            out = jnp.where(lane == first + i * HEADS + h, part, out)
    return out


def merge_body(mine_ref, other_ref, own_ref, far_ref):
    width = HEADS * HEAD_DIM
    lane = lax.broadcasted_iota(I32, (1, HEAD_DIM), 1)
    for b in range(2):
        lse_mine, lse_other = mine_ref[b, :, width:], other_ref[b, :, width:]
        top = jnp.maximum(lse_mine, lse_other)
        share_mine, share_other = jnp.exp2(lse_mine - top), jnp.exp2(lse_other - top)
        share = share_mine + share_other
        log_total = top + jnp.log2(share)
        share_mine, share_other = share_mine / share, share_other / share
        for h in range(HEADS):
            lanes = slice(h * HEAD_DIM, (h + 1) * HEAD_DIM)
            mixed = mine_ref[b, :, lanes] * share_mine[:, h : h + 1] + other_ref[b, :, lanes] * share_other[:, h : h + 1]
            if b == 0:
                own_ref[:, lanes] = mixed
            else:
                far_ref[:, lanes] = mixed.astype(BF)
        if b == 0:
            own_ref[:, width:] = log_total
        else:
            columns = [log_total[:, h : h + 1] for h in range(HEADS)]
            far_ref[:, width:] = in_parts(columns, lane, 0).astype(BF)


def middle_body(idx, sc, tab, *refs, rows, m_count, grad_count):
    m_refs, (tok_ref, own_ref, other_ref, cot_ref, row_ref, up_row_ref) = refs[:m_count], refs[m_count : m_count + 6]
    outs = refs[m_count + 6 :]
    out_ref, dmid_ref, d_ref, vec_ref = outs[:4]
    g_refs = outs[4 : 4 + grad_count]
    (w_out, w_up, w_down, g_out, g_up, g_down, dh_scr, sem, g_sem) = outs[4 + grad_count :]
    blocks, width = w_up.shape[0], w_up.shape[2]
    pieces = w_down.shape[0] // blocks
    count = tab.shape[0] // 3
    local = tok_ref.shape[0]
    spots = []
    for m_ref in m_refs:
        for spot in range(m_ref.shape[0]):
            owner = idx[len(spots)]
            spots.append(
                (m_ref, spot, pl.ds(pl.multiple_of(owner * rows, rows), rows), pl.ds(owner * blocks, blocks))
            )
    for m_ref, spot, at, unused in spots:
        pltpu.make_async_copy(m_ref.at[spot, 0], w_out.at[at, :], sem.at[0]).start()
    for m_ref, spot, unused, at in spots:
        pltpu.make_async_copy(m_ref.at[spot, pl.ds(1 + blocks, blocks)], w_down.at[at], sem.at[2]).start()
    for m_ref, spot, at, unused in spots:
        pltpu.make_async_copy(m_ref.at[spot, pl.ds(1, blocks)], w_up.at[:, at, :], sem.at[1]).start()

    pos = sc[1] + lax.broadcasted_iota(I32, (local, 1), 0)
    unused_low, unused_high, finish = table_of(tab, count, pos)
    live = (pos < finish).astype(F32)
    gain, shift = row_ref[5:6, :], row_ref[6:7, :]
    lane = lax.broadcasted_iota(I32, (1, HEAD_DIM), 1)
    logs, mixed = [], []
    for h in range(HEADS):
        lanes = slice(h * HEAD_DIM, (h + 1) * HEAD_DIM)
        lse_own = own_ref[:, width + h : width + h + 1]
        lse_other = sum(
            other_ref[:, width + i * HEADS + h : width + i * HEADS + h + 1].astype(F32) for i in range(3)
        )
        top = jnp.maximum(lse_own, lse_other)
        share_own, share_other = jnp.exp2(lse_own - top), jnp.exp2(lse_other - top)
        share = share_own + share_other
        logs.append(top + jnp.log2(share))
        mixed.append(
            own_ref[:, lanes] * (share_own / share) + other_ref[:, lanes].astype(F32) * (share_other / share)
        )
    mixed = jnp.concatenate(mixed, axis=1)
    attended = (mixed * live).astype(BF)
    cot = cot_ref[...]
    pltpu.make_async_copy(w_out, w_out, sem.at[0]).wait()
    middle = tok_ref[...].astype(F32) + mm(attended, w_out[...]) + row_ref[4:5, :]
    pltpu.make_async_copy(w_down, w_down, sem.at[2]).wait()
    for j in range(blocks):
        dh_scr[j] = mm_nt(cot, w_down[j * pieces : (j + 1) * pieces].reshape(width, width))
    plain, inverse = normalize(middle)
    normed = (plain * gain + shift).astype(BF)
    pltpu.make_async_copy(w_up, w_up, sem.at[1]).wait()
    total = middle + row_ref[7:8, :]
    d_norm = jnp.zeros(middle.shape, F32)
    ones = jnp.ones((8, local), BF)
    up_sums = []
    for j in range(blocks):
        up = w_up[j]
        down = w_down[j * pieces : (j + 1) * pieces].reshape(width, width)
        pre = mm(normed, up) + up_row_ref[j : j + 1, :]
        square = pre * pre
        t = jnp.tanh(GELU_A * pre * (1.0 + GELU_B * square))
        half = 0.5 * (1.0 + t)
        hidden = (pre * half).astype(BF)
        slope = half + 0.5 * pre * (1.0 - t * t) * (GELU_A * (1.0 + 3.0 * GELU_B * square))
        total = total + mm(hidden, down)
        d_pre = (dh_scr[j] * slope).astype(BF)
        d_norm = d_norm + mm_nt(d_pre, up)
        g_down[j * pieces : (j + 1) * pieces] = mm_tn(hidden, cot).astype(BF).reshape(pieces, rows, width)
        g_up[j] = mm_tn(normed, d_pre).astype(BF)
        up_sums.append(mm(ones, d_pre)[0:1])
    g_pieces = g_refs[0].shape[0]
    spots = []
    for i in range(pieces):
        g_ref, spot, where = g_refs[i // g_pieces], i % g_pieces, idx[pieces + i]
        spots.append((g_ref, spot, pl.ds(pl.multiple_of(where * rows, rows), rows)))
        at = pl.ds(where * blocks, blocks)
        pltpu.make_async_copy(g_down.at[at], g_ref.at[spot, pl.ds(1 + blocks, blocks)], g_sem).start()
    for g_ref, spot, at in spots:
        pltpu.make_async_copy(g_up.at[:, at, :], g_ref.at[spot, pl.ds(1, blocks)], g_sem).start()
    out_ref[...] = total.astype(BF)
    cot_f = cot.astype(F32)
    d_middle = cot_f + norm_back(d_norm, plain, inverse, gain)
    dmid_ref[...] = d_middle
    d_branch = d_middle.astype(BF)
    g_out[...] = mm_tn(attended, d_branch).astype(BF)
    for g_ref, spot, at in spots:
        pltpu.make_async_copy(g_out.at[at, :], g_ref.at[spot, 0], g_sem).start()
    d_att = mm_nt(d_branch, w_out[...]).astype(BF) * live.astype(BF)
    d_ref[:, :width] = d_att
    product = d_att.astype(F32) * mixed
    deltas = [
        jnp.sum(product[:, h * HEAD_DIM : (h + 1) * HEAD_DIM], axis=-1, keepdims=True) for h in range(HEADS)
    ]
    d_ref[:, width:] = (in_parts(deltas, lane, 0) + in_parts(logs, lane, 3 * HEADS)).astype(BF)

    sums = [jnp.sum(v, axis=0, keepdims=True) for v in (d_middle, d_norm * plain, d_norm, cot_f)]
    sums = jnp.concatenate(sums + up_sums + [jnp.zeros((HEAD_DIM - 4 - blocks, width), F32)], axis=0)
    columns = jnp.transpose(sums)
    if pieces > 1:
        per = pieces // blocks
        vec_ref[...] = jnp.where(lane < 4, columns, 0.0)
        for j in range(blocks):
            column = jnp.broadcast_to(columns[:, 4 + j : 5 + j], (width, HEAD_DIM)).reshape(
                per, blocks, rows, HEAD_DIM
            )
            wide_lane = lane.reshape(1, 1, HEAD_DIM)
            placed = sum(jnp.where(wide_lane == 4 + i, column[:, i], 0.0) for i in range(blocks))
            vec_ref[j * per * rows : (j + 1) * per * rows, :] += placed.reshape(per * rows, HEAD_DIM)
    else:
        vec_ref[...] = jnp.where(lane < 4 + blocks, columns, 0.0)
    for g_ref in g_refs:
        pltpu.make_async_copy(g_ref, g_ref, g_sem).wait()


def back_unit(sc, tab, plane, kv_ref, spot, q_ref, do_refs, stat_refs, dq_refs, put, none):
    count = tab.shape[0] // 3
    rows = kv_ref.shape[2]
    min_low, max_high, max_low, min_high = reach(sc, tab, rows)
    low, high, unused = table_of(tab, count, plane_rows(sc, rows, (1, PLANE * rows), 1))
    start = sc[1 + PLANE + plane]
    needed = (start < max_high) & (start + rows > min_low)
    whole = (start >= max_low) & (start + rows <= min_high)

    def unit(masked):
        k_pos = start + lax.broadcasted_iota(I32, (rows, 1), 0)
        for h in range(HEADS):
            key, value = kv_ref[spot, h], kv_ref[spot, HEADS + h]
            d_key, d_value = 0.0, 0.0
            for half in do_refs:
                at = slice(2 * half * rows, 2 * (half + 1) * rows)
                q, do, stat_ref = q_ref[h, at], do_refs[half][h], stat_refs[half]
                soft = jnp.exp2(mm_nt(key, q) - stat_ref[HEADS + h : HEADS + h + 1, :])
                if masked:
                    soft = jnp.where((k_pos >= low[:, at]) & (k_pos < high[:, at]), soft, 0.0)
                d_soft = mm_nt(value, do)
                d_scores = (soft * (d_soft - stat_ref[h : h + 1, :])).astype(BF)
                d_value = d_value + mm(soft.astype(BF), do)
                d_key = d_key + mm(d_scores, q)
                dq_refs[half][h] += mm_tn(key, d_scores)
            put(slice(h * HEAD_DIM, (h + 1) * HEAD_DIM), d_key * (SCALE / SCALE2))
            put(slice((HEADS + h) * HEAD_DIM, (HEADS + h + 1) * HEAD_DIM), d_value)

    @pl.when(needed & whole)
    def _():
        unit(False)

    @pl.when(needed & jnp.logical_not(whole))
    def _():
        unit(True)

    @pl.when(jnp.logical_not(needed))
    def _():
        none()


def unpack_rows(packets, do_ref, stat_ref):
    rows, width = packets[0].shape[0], HEADS * HEAD_DIM
    for b, ref in enumerate(packets):
        at = slice(b * rows, (b + 1) * rows)
        for h in range(HEADS):
            do_ref[h, at] = ref[:, h * HEAD_DIM : (h + 1) * HEAD_DIM]
        tail = jnp.transpose(ref[:, width:].astype(F32))
        parts = [tail[i * HEADS : (i + 1) * HEADS] for i in range(6)]
        stat_ref[:, at] = jnp.concatenate([parts[0] + parts[1] + parts[2], parts[3] + parts[4] + parts[5]], axis=0)


def open_body(sc, tab, q_ref, d_own, d_c, kv_ref, do_ref, stat_ref, dq_ref, part_ref, *, units):
    unpack_rows((d_own, d_c), do_ref, stat_ref)
    dq_ref[...] = jnp.zeros(dq_ref.shape, F32)
    for j, (plane, spot) in enumerate(units):

        def put(lanes, value, j=j):
            part_ref[j, :, lanes] = value

        def none(j=j):
            part_ref[j] = jnp.zeros(part_ref.shape[1:], F32)

        back_unit(sc, tab, plane, kv_ref, spot, q_ref, {0: do_ref}, {0: stat_ref}, {0: dq_ref}, put, none)


def keep_planes(units, n_ref, w_ref, d_refs, nk_ref, sum_ref, nk_in, sum_in, dkv_scr):
    width = w_ref.shape[1]
    ones = jnp.ones((8, dkv_scr.shape[1]), BF)
    product = 0.0 if nk_in is None else nk_in[...]
    sums = 0.0 if sum_in is None else sum_in[...]
    for j, (unused, spot) in enumerate(units):
        d_refs[j][...] = (mm_nt(dkv_scr[j, :, :width], w_ref[1]) + mm_nt(dkv_scr[j, :, width:], w_ref[2])).astype(BF)
        product = product + mm_tn(n_ref[spot], dkv_scr[j])
        sums = sums + mm(ones, dkv_scr[j])
    nk_ref[...] = product
    sum_ref[...] = sums


def close_body(
    sc, tab, q_ref, d_x, d_xc, kv_ref, n_ref, w_ref, part_ref, do_ref, stat_ref, dq_ref, nk_ref, sum_ref, *refs, units
):
    d_refs, dkv_scr = refs[:-1], refs[-1]
    unpack_rows((d_x, d_xc), do_ref, stat_ref)
    dq_ref[...] = jnp.zeros(dq_ref.shape, F32)
    for j, (plane, spot) in enumerate(units):

        def put(lanes, value, j=j):
            dkv_scr[j, :, lanes] = (part_ref[j, :, lanes] + value).astype(BF)

        def none(j=j):
            dkv_scr[j] = jnp.zeros(dkv_scr.shape[1:], BF)

        back_unit(sc, tab, plane, kv_ref, spot, q_ref, {1: do_ref}, {1: stat_ref}, {1: dq_ref}, put, none)
    keep_planes(units, n_ref, w_ref, d_refs, nk_ref, sum_ref, None, None, dkv_scr)


def back_body(
    sc, tab, q_ref, do_one, do_two, stat_one, stat_two, kv_ref, n_ref, w_ref, one_in, two_in, nk_in, sum_in,
    d_ref, one_ref, two_ref, nk_ref, sum_ref, dkv_scr, *, unit,
):
    one_ref[...] = one_in[...]
    two_ref[...] = two_in[...]

    def put(lanes, value):
        dkv_scr[0, :, lanes] = value.astype(BF)

    def none():
        dkv_scr[0] = jnp.zeros(dkv_scr.shape[1:], BF)

    halves = {0: do_one, 1: do_two}, {0: stat_one, 1: stat_two}, {0: one_ref, 1: two_ref}
    back_unit(sc, tab, unit[0], kv_ref, unit[1], q_ref, *halves, put, none)
    keep_planes([unit], n_ref, w_ref, [d_ref], nk_ref, sum_ref, nk_in, sum_in, dkv_scr)


def query_block(dq_refs, b, rows):
    ref, at = dq_refs[b // 2], slice((b % 2) * rows, (b % 2 + 1) * rows)
    return jnp.concatenate([ref[h, :, at] * SCALE for h in range(HEADS)], axis=0).astype(BF)


def message_body(idx, *refs, rows):
    n_refs, dq_refs = refs[:PLANE], refs[PLANE : PLANE + 2]
    (nk_ref, sum_ref, w_ref, col_ref, vec_ref), (full, vec) = refs[PLANE + 2 : PLANE + 7], refs[-2:]
    msg_refs = refs[PLANE + 7 : -2]
    local = n_refs[0].shape[1]
    width = w_ref.shape[1]
    q_product = jnp.zeros((width, width), F32)
    q_sums = jnp.zeros((8, width), F32)
    ones = jnp.ones((8, local), BF)
    for b, n_ref in enumerate(n_refs):
        d_query = query_block(dq_refs, b, local)
        q_product += lax.dot_general(n_ref[0], d_query, (((0,), (1,)), ((), ())), preferred_element_type=F32)
        q_sums += mm_nt(ones, d_query)
    gain, shift = col_ref[:, 0:1], col_ref[:, 1:2]
    lane = lax.broadcasted_iota(I32, (1, HEAD_DIM), 1)
    gain_grad = jnp.zeros((width, 1), F32)
    shift_grad = jnp.zeros((width, 1), F32)
    columns = []
    for i in range(3):
        lanes = slice(i * width, (i + 1) * width)
        if i == 0:
            product, sums = q_product, q_sums[0:1]
        else:
            at = slice((i - 1) * width, i * width)
            product, sums = nk_ref[:, at], sum_ref[0:1, at]
        weight = w_ref[i].astype(F32)
        full[:, lanes] = (product * gain + shift * sums).astype(BF)
        gain_grad += jnp.sum(product * weight, axis=-1, keepdims=True)
        shift_grad += jnp.sum(weight * sums, axis=-1, keepdims=True)
        if i != 1:
            columns.append(jnp.transpose(jnp.broadcast_to(sums, (HEAD_DIM, width))))
    vec[...] = vec_ref[...]
    for at, column in ((8, gain_grad), (9, shift_grad), (10, columns[0]), (11, columns[1])):
        vec[...] += jnp.where(lane == at, column, 0.0)
    full[:, 3 * width :] = vec[...].astype(BF)
    k = 0
    for msg_ref in msg_refs:
        for i in range(msg_ref.shape[0]):
            msg_ref[i] = full[pl.ds(pl.multiple_of(idx[k] * rows, rows), rows), :]
            k += 1


def query_body(dq_one, dq_two, w_ref, keep_ref, send_ref):
    rows = keep_ref.shape[1]
    for b in range(PLANE):
        d_query = query_block((dq_one, dq_two), b, rows)
        out = lax.dot_general(d_query, w_ref[0], (((0,), (1,)), ((), ())), preferred_element_type=F32)
        (keep_ref, send_ref)[b % 2][b // 2] = out.astype(BF)


def finish_body(tok_ref, dmid_ref, row_ref, last_ref, *refs):
    plain, inverse = normalize(tok_ref[...].astype(F32))
    lines = 0 if len(last_ref.shape) == 2 else tok_ref.shape[0] // last_ref.shape[1]
    last = last_ref[:lines].reshape(tok_ref.shape) if lines else last_ref[...]
    total = last.astype(F32)
    for ref in refs[:-1]:
        total = total + ref[...].astype(F32)
    refs[-1][...] = (dmid_ref[...] + norm_back(total, plain, inverse, row_ref[0:1, :])).astype(BF)


def matrices_body(*refs, starts):
    terms, (out_ref, up_ref, down_ref) = refs[:-3], refs[-3:]
    width = out_ref.shape[1]
    part = out_ref.shape[0]
    blocks = up_ref.shape[1] // width

    def block(i):
        total = terms[0][starts[0] + i].astype(F32)
        for term, start in zip(terms[1:], starts[1:], strict=True):
            total = total + term[start + i].astype(F32)
        return total

    out_ref[...] = block(0)
    for j in range(blocks):
        up_ref[:, j * width : (j + 1) * width] = block(1 + j)
        down_ref[j * part : (j + 1) * part, :] = block(1 + blocks + j)


def unpack_body(*refs, w_blocks):
    terms, (qkv_ref, *vec_refs, up_ref, pad_ref) = refs[:-11], refs[-11:]
    total = terms[0][...]
    for term in terms[1:]:
        line = jnp.concatenate([term[j] for j in range(w_blocks)], axis=1)
        total = total + line[:, : total.shape[1]].astype(F32)
    width = qkv_ref.shape[1]
    part = qkv_ref.shape[0]
    qkv_ref[...] = total[:, :width]
    pad_ref[...] = jnp.zeros(pad_ref.shape, F32)
    pad_ref[:part] = total[:, width:]
    rows = jnp.transpose(pad_ref[...])
    for ref, row in zip(vec_refs, (8, 9, 10, 11, 0, 1, 2, 3), strict=True):
        ref[...] = rows[row : row + 1, :part]
    blocks = up_ref.shape[1] // part
    up_ref[...] = jnp.concatenate([rows[4 + j : 5 + j, :part] for j in range(blocks)], axis=1)


def shards(
    tokens, w_qkv, w_out, w_up, w_down,
    norm1_gain, norm1_bias, query_bias, value_bias, out_bias, norm2_gain, norm2_bias, up_bias, down_bias,
    cotangent, table_start, support_count, query_count, *, R, F,
):
    A = R // PLANE
    count = R * F
    local, width = tokens.shape[1], tokens.shape[2]
    part = w_qkv.shape[0]
    hidden = w_up.shape[1]
    blocks = hidden // width
    aligned = part % 16 == 0
    rows = part if aligned else width
    pieces = count if aligned else 1
    sds = jax.ShapeDtypeStruct

    r, f = lax.axis_index("rows"), lax.axis_index("fsdp")
    a, x, c = r // PLANE, (r // 2) % 2, r % 2

    def swap_c(v):
        return lax.ppermute(v, "rows", [(i, i ^ 1) for i in range(R)])

    def swap_x(v):
        return lax.ppermute(v, "rows", [(i, i ^ 2) for i in range(R)])

    def turn_a(v, s):
        return lax.ppermute(
            v, "rows", [(i, ((i // PLANE + s) % A) * PLANE + i % PLANE) for i in range(R)]
        )

    def turn_f(v, t):
        return lax.ppermute(v, "fsdp", [(i, (i + t) % F) for i in range(F)])

    def turn_xf(v, t):
        return lax.ppermute(
            v, ("rows", "fsdp"),
            [(i * F + j, (i ^ 2) * F + (j + t) % F) for i in range(R) for j in range(F)],
        )

    def owners(order):
        cr, t, xr, s = (np.array(list(z), np.int32) for z in zip(*order, strict=True))
        plane = lax.rem(a - s + A, A)
        return (((plane * 2 + (x ^ xr)) * 2 + (c ^ cr)) * F + lax.rem(f - t + F, F)).astype(I32)

    block_x, block_c = np.array([0, 0, 1, 1], np.int32), np.array([0, 1, 0, 1], np.int32)
    block_start = (a * 4 + (x ^ block_x) * 2 + (c ^ block_c)) * local
    unit_start = (lax.rem(a - np.arange(A, dtype=np.int32) + A, A) * 4 + 2 * x + c) * local
    sc = jnp.concatenate([(a * 4 * local)[None], block_start, unit_start]).astype(I32)
    tab = jnp.concatenate([table_start[0], support_count[0], query_count[0]])
    q_order = [(cr, t, xr, s) for cr in range(2) for t in range(F) for xr in range(2) for s in range(A)]
    parts = [slice(0, A // 2), slice(A // 2, A)]
    m_order = [
        (cr, t, xr, s)
        for cr in range(2)
        for planes in (range(2, A), range(2))
        for xr, t in [(0, 0), (1, 0)] + [(0, t) for t in range(1, F)] + [(1, t) for t in range(1, F)]
        for s in planes
    ]
    every_owner = owners(q_order + m_order)
    q_owner, m_owner = every_owner[:count], every_owner[count:]
    if aligned:
        q_idx, idx = q_owner, jnp.concatenate([m_owner, q_owner])
    else:
        q_idx, idx = jnp.zeros((1,), I32), jnp.zeros((2,), I32)

    near = list(range(1, A))
    early, late = near[:2], near[2:]
    own = tokens[0]
    vectors = [
        v.reshape(1, -1)
        for v in (
            norm1_gain, norm1_bias, query_bias, value_bias, out_bias, norm2_gain, norm2_bias, down_bias, up_bias
        )
    ]
    wide = 3 * width + HEAD_DIM
    pack_in = [w_qkv, w_out, w_up, w_down, *vectors]
    q_own, m_own = pl.pallas_call(
        pack_body,
        grid=(1,),
        out_shape=[sds((4, part, width), BF), sds((1 + 2 * blocks, part, width), BF)],
        in_specs=[pl.BlockSpec(v.shape, lambda i: (0, 0)) for v in pack_in],
        out_specs=[VMEM] * 2,
        scratch_shapes=[pltpu.VMEM((HEAD_DIM, HEAD_DIM), F32)],
        compiler_params=pltpu.CompilerParams(vmem_limit_bytes=56 * MIB),
        cost_estimate=pl.CostEstimate(flops=0, bytes_accessed=16 * part * width, transcendentals=0),
        name="pack",
    )(*pack_in)
    tok_z, m_z = {0: own}, {0: m_own}
    *q_z, tok_z[1], m_z[1], sc, tab, q_idx, idx = together(
        *(turn_a(q_own, s) for s in range(1, A)), turn_a(own, 1), turn_a(m_own, 1), sc, tab, q_idx, idx
    )
    q_z = jnp.stack([q_own] + q_z)
    moved = [swap_x(q_z)] + [v for t in range(1, F) for v in (turn_f(q_z, t), turn_xf(q_z, t))]
    *q_far, tok_z[2], m_z[2] = together(*moved, turn_a(tok_z[1], 1), turn_a(m_z[1], 1))
    tok_early, m_early = jnp.stack([tok_z[1], tok_z[2]]), jnp.stack([m_z[0], m_z[1]])
    early_x, early_f = swap_x(m_early), [turn_f(m_early, t) for t in range(1, F)]
    tok_z[3], m_z[3] = turn_a(tok_z[2], 1), turn_a(m_z[2], 1)
    q_four = jnp.stack([q_z] + q_far)
    q_other = swap_c(q_four)
    q_pieces = [q_four.reshape(count // 2, 4, part, width), q_other.reshape(count // 2, 4, part, width)]
    if not aligned:
        stacked = jnp.concatenate(q_pieces)
        by_owner = jnp.zeros_like(stacked).at[q_owner].set(stacked)
        q_pieces = [by_owner.transpose(1, 0, 2, 3).reshape(1, 4, width, width)]
    key_shape = (2 * HEADS, local, HEAD_DIM)
    w_all, row_vec, col_vec, up_row, kv_early, n_early, q, n_first = call(
        functools.partial(ready_body, rows=rows, count=len(q_pieces), part=part),
        [
            sds((3, width, width), BF), sds((16, width), F32), sds((width, HEAD_DIM), F32), sds((blocks, width), F32),
            sds((3,) + key_shape, BF), sds((3, local, width), BF), sds((HEADS, local, HEAD_DIM), BF),
            sds((1, local, width), BF),
        ],
        [q_idx, *q_pieces, own, tok_early], [SMEM] + [HBM] * len(q_pieces) + [VMEM] * 2, [VMEM] * 8,
        scratch=[pltpu.VMEM((width, HEAD_DIM), BF), pltpu.SemaphoreType.DMA((2,))],
        flops=4 * (A + 1) * local * width * width, moved=4 * width * wide, vmem=12, name="ready",
    )

    tok_z[3], m_z[3], early_x, q_x, *early_f = together(tok_z[3], m_z[3], early_x, swap_x(q), *early_f)
    for s in range(4, A):
        tok_z[s], m_z[s] = together(turn_a(tok_z[s - 1], 1), turn_a(m_z[s - 1], 1))
    q_blocks = [q, swap_c(q), q_x, swap_c(q_x)]
    late = list(range(3, A))
    tok_late = jnp.stack([tok_z[s] for s in late]) if A > 4 else tok_z[3][None]
    m_late = stack([m_z[s] for s in range(2, A)])
    late_x, late_f = swap_x(m_late), [turn_f(m_late, t) for t in range(1, F)]
    early_xf = [turn_f(early_x, t) for t in range(1, F)]
    kv_late, n_late = call(
        functools.partial(project_body, with_q=False, spots=[(0, i) for i in range(len(late))], count=1),
        [sds((len(late),) + key_shape, BF), sds((len(late), local, width), BF)],
        [after(tok_late, m_late), w_all, row_vec], [VMEM] * 3, [VMEM] * 2,
        flops=4 * len(late) * local * width * width, moved=8 * len(late) * local * width, vmem=8, name="project",
    )
    where = {s: (kv_early, n_early, s) if s < 3 else (kv_late, n_late, s - 3) for s in range(A)}

    unit = PLANE * local
    work = 4 * unit * A * local * width
    packet = width + HEAD_DIM
    att_keep, att_send, q_plane = call(
        functools.partial(attend_body, kv_units=list(range(A))),
        [sds((2, local, packet), F32)] * 2 + [sds((HEADS, unit, HEAD_DIM), BF)],
        [sc, tab, *q_blocks, kv_early, kv_late], [SMEM, SMEM] + [VMEM] * PLANE + [ANY] * 2, [VMEM] * 3,
        scratch=[
            pltpu.VMEM((A, HEADS, unit, local), F32),
            pltpu.VMEM((HEADS, unit, HEAD_DIM), F32), pltpu.VMEM((HEADS, unit, 2 * HEAD_DIM), F32),
            pltpu.VMEM((A, 2 * HEADS, local, HEAD_DIM), BF), pltpu.SemaphoreType.DMA((A,)),
        ],
        flops=work, moved=8 * A * local * width, trans=HEADS * unit * A * local, vmem=10 + 5 * A, name="attend",
    )
    early_side = [m_early, early_x, *early_f]
    att_keep, att_send, late_x, *more = together(
        att_keep, att_send, late_x, *late_f, *(swap_c(v) for v in early_side[:2])
    )
    late_f, early_c = list(more[: F - 1]), list(more[F - 1 :])
    att_recv = swap_c(att_send)
    late_xf = [turn_f(late_x, t) for t in range(1, F)]
    att_own, att_far = call(
        merge_body, [sds((local, packet), F32), sds((local, packet), BF)], [att_keep, att_recv], [VMEM] * 2,
        [VMEM] * 2, flops=32 * local * packet, moved=20 * local * packet, vmem=8, name="merge",
    )
    late_side = [m_late, late_x, *late_f]
    att_other, *more = together(
        swap_x(att_far), *late_xf, *(swap_c(v) for v in [*early_f, *early_xf, *late_side])
    )
    late_xf, more = list(more[: F - 1]), list(more[F - 1 :])
    early_c += more[: 2 * F - 2]
    late_c = more[2 * F - 2 :] + [swap_c(v) for v in late_xf]
    m_arrays = late_side + late_xf + early_side + early_xf + late_c + early_c
    if not aligned:
        stacked = jnp.concatenate(m_arrays)
        by_owner = jnp.zeros_like(stacked).at[m_owner].set(stacked)
        m_arrays = [
            jnp.concatenate(
                [
                    by_owner[:, 0].reshape(1, width, width),
                    by_owner[:, 1 : 1 + blocks].transpose(1, 0, 2, 3).reshape(blocks, width, width),
                    by_owner[:, 1 + blocks :].reshape(blocks, width, width),
                ]
            )[None]
        ]

    spots = [(t, xr) for t in range(F) for xr in range(2)]
    grad_count = 4 * F if aligned else 1
    g_shape = sds((pieces // grad_count, 1 + 2 * blocks, rows, width), BF)
    got = call(
        functools.partial(middle_body, rows=rows, m_count=len(m_arrays), grad_count=grad_count),
        [
            sds((local, width), BF), sds((local, width), F32), sds((local, packet), BF), sds((width, HEAD_DIM), F32),
        ] + [g_shape] * grad_count,
        [idx, sc, tab, *m_arrays, own, att_own, att_other, cotangent[0], row_vec, up_row],
        [SMEM] * 3 + [HBM] * len(m_arrays) + [VMEM] * 6,
        [VMEM] * 4 + [HBM] * grad_count,
        scratch=[
            pltpu.VMEM((width, width), BF), pltpu.VMEM((blocks, width, width), BF),
            pltpu.VMEM((pieces * blocks, rows, width), BF),
            pltpu.VMEM((width, width), BF), pltpu.VMEM((blocks, width, width), BF),
            pltpu.VMEM((pieces * blocks, rows, width), BF), pltpu.VMEM((blocks, local, width), F32),
            pltpu.SemaphoreType.DMA((3,)), pltpu.SemaphoreType.DMA,
        ],
        flops=6 * local * width * width * (1 + 2 * blocks), moved=4 * width * width * (1 + 2 * blocks),
        trans=local * hidden, vmem=52, name="middle",
    )
    *got, n_x = together(*got, swap_x(after(n_first, att_other)))
    outputs, d_middle, d_own, vec = got[:4]
    grads = got[4:]
    d_c = swap_c(d_own)

    lead = (A, 1 + 2 * blocks, part, width)
    if aligned:
        relative = [g.reshape(lead) for g in grads]
    else:
        whole = grads[0][0]
        by_owner = jnp.concatenate(
            [
                whole[0].reshape(count, 1, part, width),
                whole[1 : 1 + blocks].reshape(blocks, count, part, width).transpose(1, 0, 2, 3),
                whole[1 + blocks :].reshape(count, blocks, part, width),
            ],
            axis=1,
        )
        by_owner = by_owner[q_owner].reshape((4 * F,) + lead)
        relative = [by_owner[i] for i in range(4 * F)]
    g_near = {spot: relative[i] for i, spot in enumerate(spots)}
    g_far = {spot: swap_c(after(relative[2 * F + i], d_c)) for i, spot in reversed(list(enumerate(spots)))}

    def sums_of(keys, half, *others):
        arrays = [g_near[keys], g_far[keys], *others]
        return add_up(arrays, [[(0, (half,)), (1, (half,))] + [(2 + i, ()) for i in range(len(others))]])[0]

    first, second = parts
    half = A // 2
    ways = {}

    def joined(keys, planes):
        arrays = [v for key in keys for v in (g_near[key], g_far[key])]
        return join_up(arrays, [[(2 * i, (planes,)), (2 * i + 1, (planes,))] for i in range(len(keys))])[0]

    def start_ways(step):
        if step == 1:
            for t in range(1, F):
                ways["f", t] = turn_f(joined([(t, 1), (t, 0)], first), F - t)
            ways["x"] = swap_x(joined([(t, 1) for t in range(F)], second))
        if step == 2:
            return [("f", t) for t in range(1, F)] + ["x"]
        if step == 3:
            arrays = [g_near[0, 1], g_far[0, 1], *(ways["f", t] for t in range(1, F))]
            plan = [[(0, (first,)), (1, (first,))] + [(1 + t, (slice(0, half),)) for t in range(1, F)]]
            ways["x", F] = swap_x(add_up(arrays, plan)[0])
            for t in range(1, F):
                arrays = [g_near[t, 0], g_far[t, 0], ways["x"]]
                plan = [[(0, (second,)), (1, (second,)), (2, (slice(t * half, (t + 1) * half),))]]
                ways["f2", t] = turn_f(add_up(arrays, plan)[0], F - t)
            return [("x", F)] + [("f2", t) for t in range(1, F)]
        return []

    pair = [(s, where[s][2]) for s in (1, 2)]
    dq_shape = sds((HEADS, HEAD_DIM, 2 * local), F32)
    half_shapes = [sds((HEADS, 2 * local, HEAD_DIM), BF), sds((2 * HEADS, 2 * local), F32), dq_shape]
    keys = list(g_far)
    do_one, stat_one, dq_one, part_sums, d_x, *more = together(
        *call(
            functools.partial(open_body, units=pair), [*half_shapes, sds((2, local, 2 * width), F32)],
            [sc, tab, q_plane, d_own, d_c, kv_early], [SMEM] * 2 + [VMEM] * 4, [VMEM] * 4,
            flops=2 * work // A, moved=16 * unit * width, trans=HEADS * unit * local, vmem=16, name="open",
        ),
        swap_x(d_own), *(g_far[k] for k in keys),
    )
    g_far.update(zip(keys, more, strict=True))
    d_xc = swap_c(d_x)
    start_ways(1)
    got = together(
        *call(
            functools.partial(close_body, units=pair),
            [*half_shapes, sds((width, 2 * width), F32), sds((8, 2 * width), F32)] + [sds((local, width), BF)] * 2,
            [sc, tab, q_plane, d_x, d_xc, kv_early, n_early, w_all, part_sums],
            [SMEM] * 2 + [VMEM] * 7, [VMEM] * 7, scratch=[pltpu.VMEM((2, local, 2 * width), BF)],
            flops=3 * work // A, moved=16 * unit * width, trans=HEADS * unit * local, vmem=16, name="close",
        ),
    )
    do_two, stat_two, dq_two, n_product, sums, d_sum, d_next = got
    carried = [dq_one, dq_two, n_product, sums]
    q_now = q_plane
    for step, s in enumerate([*near[2:], 0], 1):
        kv_now, n_now, spot = where[s]
        outs = call(
            functools.partial(back_body, unit=(s, spot)),
            [sds((local, width), BF), dq_shape, dq_shape, sds((width, 2 * width), F32), sds((8, 2 * width), F32)],
            [sc, tab, q_now, do_one, do_two, stat_one, stat_two, kv_now, n_now, w_all, *carried],
            [SMEM] * 2 + [VMEM] * 12, [VMEM] * 5, scratch=[pltpu.VMEM((1, local, 2 * width), BF)],
            flops=work // A * 5 // 2 + 8 * local * width * width, moved=16 * unit * width,
            trans=HEADS * unit * local, name="back",
        )
        keys = start_ways(step + 1)
        got = together(*outs, turn_a(d_sum, 1), *(ways[k] for k in keys))
        outs, d_recv = got[:5], got[5]
        ways.update(zip(keys, got[6:], strict=True))
        (d_sum,) = add_up([d_next, d_recv], [[(0, ()), (1, ())]])
        d_next, *carried = outs
        q_now = after(q_plane, d_sum)

    dq_one, dq_two, n_product, sums = carried
    n_blocks = [n_first, swap_c(n_first), n_x, swap_c(n_x)]

    half_count = 2 * F
    msg_lead = (A, part, wide)
    msg_shape = [sds((pieces // 2, rows, wide), BF)] * 2 if aligned else [sds((1, rows, wide), BF)]
    message = call(
        functools.partial(message_body, rows=rows),
        msg_shape,
        [q_idx, *n_blocks, dq_one, dq_two, n_product, sums, w_all, col_vec, vec],
        [SMEM] + [VMEM] * (7 + PLANE), [VMEM] * len(msg_shape),
        scratch=[pltpu.VMEM((width, wide), BF), pltpu.VMEM((width, HEAD_DIM), F32)],
        flops=2 * local * width * width, moved=8 * width * wide, vmem=8, name="message",
    )
    g_sums = {}
    arrays = [g_near[0, 0], g_far[0, 0], ways["x", F], *(ways["f", t] for t in range(1, F))]
    plan = [
        [(0, (s,)), (1, (s,)), (2, (s,))] + [(2 + t, (half + s,)) for t in range(1, F)] for s in range(half)
    ]
    g_sums.update(zip(range(half), add_up(arrays, plan), strict=True))
    arrays = [g_near[0, 0], g_far[0, 0], ways["x"], *(ways["f2", t] for t in range(1, F))]
    plan = [
        [(0, (s,)), (1, (s,)), (2, (s - half,))] + [(2 + t, (s - half,)) for t in range(1, F)]
        for s in range(half, A)
    ]
    g_sums.update(zip(range(half, A), add_up(arrays, plan), strict=True))
    if not aligned:
        flat = message[0][0]
        at = slice(3 * width + 4, 3 * width + 4 + blocks)
        up_part = flat[:, at].T.reshape(count, blocks, part)
        by_owner = flat.reshape(count, part, wide)
        by_owner = by_owner.at[:, :, at].set(up_part.transpose(0, 2, 1))
        by_owner = by_owner[q_owner]
        message = [by_owner[: count // 2], by_owner[count // 2 :]]
    query_keep, query_send = call(
        query_body, [sds((2, local, width), BF)] * 2, [after(dq_one, message[0]), dq_two, w_all], [VMEM] * 3, [VMEM] * 2,
        flops=8 * local * width * width, moved=8 * local * width, vmem=8, name="query",
    )
    w_far, query_recv = together(swap_c(message[1]), swap_c(query_send))
    w_far = w_far.reshape((half_count,) + msg_lead)
    w_near = message[0].reshape((half_count,) + msg_lead)
    w_both = add_up([w_near, w_far], [[(0, (i,)), (1, (i,))] for i in range(half_count)])
    got = []
    for (t, xr), sent in zip(spots, w_both, strict=True):
        if xr:
            sent = turn_xf(sent, F - t) if t else swap_x(sent)
        elif t:
            sent = turn_f(sent, F - t)
        got.append(sent)
    lines = local // part
    every = ()
    sent = d_sum
    *got, arrived, g_two = together(*got, turn_a(sent, 1), turn_a(g_sums[2], A - 2))
    w_terms = {s: [(i, (s,)) for i in range(len(got))] for s in range(A)}
    w_blocks = -(-wide // width)
    packs = {}
    for s in near:
        arrays, plan = list(got), [(True, w_terms[s])]
        if s != 2:
            arrays.append(g_sums[s])
            plan.append((False, [(len(got), every)]))
        packs[s] = turn_a(lay_out(arrays, plan, part, width), A - s)
    (w_own,) = add_up(got, [w_terms[0]], F32)
    grad_qkv, *vector_grads, up_grad = call(
        functools.partial(unpack_body, w_blocks=w_blocks),
        [sds((part, 3 * width), F32)] + [sds((1, part), F32)] * 8 + [sds((1, blocks * part), F32)],
        [w_own, *packs.values()], [VMEM] * A, [VMEM] * 10, scratch=[pltpu.VMEM((HEAD_DIM, HEAD_DIM), F32)],
        moved=16 * part * width, vmem=8, name="unpack",
    )

    others = [s for s in near if s != 2]
    starts = [0, 0] + [w_blocks] * len(others)
    grad_out, grad_up, grad_down = call(
        functools.partial(matrices_body, starts=starts),
        [sds((part, width), F32), sds((part, hidden), F32), sds((blocks * part, width), F32)],
        [g_sums[0], g_two, *(packs[s] for s in others)], [VMEM] * A, [VMEM] * 3,
        moved=6 * A * g_sums[0].size, vmem=8, name="matrices",
    )
    d_last = arrived
    query_own, query_far = add_up([query_keep, query_recv], [[(0, (b,)), (1, (b,))] for b in range(2)])
    grad_tokens = call(
        finish_body, sds((local, width), BF),
        [own, d_middle, row_vec, d_last, d_next, query_own, swap_x(query_far)],
        [VMEM] * 7, VMEM, flops=20 * local * width, moved=16 * local * width, vmem=8, name="finish",
    )
    return (
        outputs[None],
        grad_tokens[None],
        grad_qkv,
        grad_out,
        grad_up,
        grad_down,
        *(v.reshape(part) for v in vector_grads[:7]),
        up_grad.reshape(blocks * part),
        vector_grads[7].reshape(part),
    )


def solution(mesh):
    both = ("rows", "fsdp")
    matrix, vector, act, table = P(both, None), P(both), P("fsdp", "rows", None), P("fsdp", None)
    return jax.shard_map(
        functools.partial(shards, R=mesh.shape["rows"], F=mesh.shape["fsdp"]),
        mesh=mesh,
        in_specs=(act,) + (matrix,) * 4 + (vector,) * 9 + (act,) + (table,) * 3,
        out_specs=(act, act) + (matrix,) * 4 + (vector,) * 9,
        check_vma=False,
    )
```

```python
import functools
import math

import jax
import jax.numpy as jnp
import numpy as np
from jax import lax
from jax.experimental import pallas as pl
from jax.experimental.pallas import tpu as pltpu
from jax.sharding import PartitionSpec as P

HEADS = 4
HEAD_DIM = 128
EPS = 1e-05
NEG = -1e30
PLANE = 4
MIB = 1024 * 1024
BF = jnp.bfloat16
F32 = jnp.float32
I32 = jnp.int32
SCALE = 1.0 / math.sqrt(HEAD_DIM)
SCALE2 = SCALE * math.log2(math.e)
GELU_A = math.sqrt(2.0 / math.pi)
GELU_B = 0.044715

VMEM = pl.BlockSpec(memory_space=pltpu.VMEM)
SMEM = pl.BlockSpec(memory_space=pltpu.SMEM)
HBM = pl.BlockSpec(memory_space=pltpu.HBM)
ANY = pl.BlockSpec(memory_space=pl.ANY)


def after(value, *others):
    return lax.optimization_barrier((value, *others))[0]


def together(*values):
    return lax.optimization_barrier(values)


def mm(left, right):
    return jnp.dot(left, right, preferred_element_type=F32)


def mm_nt(left, right):
    return lax.dot_general(left, right, (((1,), (1,)), ((), ())), preferred_element_type=F32)


def mm_tn(left, right):
    return lax.dot_general(left, right, (((0,), (0,)), ((), ())), preferred_element_type=F32)


def call(body, outs, ins, in_specs, out_specs, scratch=(), flops=0, moved=0, trans=0, vmem=16, name=None):
    return pl.pallas_call(
        body,
        out_shape=outs,
        in_specs=in_specs,
        out_specs=out_specs,
        scratch_shapes=scratch,
        compiler_params=pltpu.CompilerParams(vmem_limit_bytes=vmem * MIB),
        cost_estimate=pl.CostEstimate(
            flops=int(flops), bytes_accessed=int(moved), transcendentals=int(trans)
        ),
        name=name,
    )(*ins)


def normalize(values):
    centre = values - jnp.mean(values, axis=-1, keepdims=True)
    spread = jnp.mean(centre * centre, axis=-1, keepdims=True)
    inverse = lax.rsqrt(spread + EPS)
    return centre * inverse, inverse


def norm_back(grad_out, plain, inverse, gain):
    scaled = grad_out * gain
    return inverse * (
        scaled
        - jnp.mean(scaled, axis=-1, keepdims=True)
        - plain * jnp.mean(scaled * plain, axis=-1, keepdims=True)
    )


def table_of(tab, count, pos):
    low = jnp.zeros_like(pos) + tab[0]
    high = low + tab[count]
    finish = high + tab[2 * count]
    for t in range(1, count):
        here = pos >= tab[t]
        top = tab[t] + tab[count + t]
        low = jnp.where(here, tab[t], low)
        high = jnp.where(here, top, high)
        finish = jnp.where(here, top + tab[2 * count + t], finish)
    return low, high, finish


def pack_body(qkv_ref, out_ref, up_ref, down_ref, *refs):
    vec_refs, (q_ref, m_ref, vec_scr) = refs[:-3], refs[-3:]
    part, width = out_ref.shape
    blocks = up_ref.shape[1] // width
    vec_scr[...] = jnp.zeros(vec_scr.shape, F32)
    for k, ref in enumerate(vec_refs[:-1]):
        vec_scr[k : k + 1, :part] = ref[...].astype(F32)
    for j in range(blocks):
        vec_scr[8 + j : 9 + j, :part] = vec_refs[-1][:, j * part : (j + 1) * part].astype(F32)
    for i in range(3):
        q_ref[i] = qkv_ref[:, i * width : (i + 1) * width]
    q_ref[3] = jnp.zeros((part, width), BF)
    q_ref[3, :, :HEAD_DIM] = jnp.transpose(vec_scr[...])[:part].astype(BF)
    m_ref[0] = out_ref[...]
    for j in range(blocks):
        m_ref[1 + j] = up_ref[:, j * width : (j + 1) * width]
        m_ref[1 + blocks + j] = down_ref[j * part : (j + 1) * part, :]


def sum_body(*refs, plan, count):
    for out_ref, terms in zip(refs[count:], plan, strict=True):
        total = None
        for which, spot in terms:
            term = refs[which][spot].astype(F32)
            total = term if total is None else total + term
        out_ref[...] = total.astype(out_ref.dtype)


def join_body(*refs, plan, count):
    out_ref, row = refs[count], 0
    for terms in plan:
        total = None
        for which, spot in terms:
            term = refs[which][spot].astype(F32)
            total = term if total is None else total + term
        out_ref[row : row + total.shape[0]] = total.astype(out_ref.dtype)
        row += total.shape[0]


def join_up(arrays, plan):
    shapes = [jax.eval_shape(lambda v: v[terms[0][1]], arrays[terms[0][0]]).shape for terms in plan]
    shape = (sum(v[0] for v in shapes),) + shapes[0][1:]
    moved = math.prod(shape) * 4
    return call(
        functools.partial(join_body, plan=plan, count=len(arrays)), [jax.ShapeDtypeStruct(shape, BF)], arrays,
        [VMEM] * len(arrays), [VMEM], flops=moved, moved=moved, vmem=16, name="join",
    )


def lay_body(*refs, plan, count):
    out_ref, row = refs[count], 0
    width = out_ref.shape[2]
    for wide, terms in plan:
        total = None
        for which, spot in terms:
            term = refs[which][spot].astype(F32)
            total = term if total is None else total + term
        total = total.astype(out_ref.dtype)
        if wide:
            for j in range(-(-total.shape[1] // width)):
                piece = total[:, j * width : (j + 1) * width]
                if piece.shape[1] < width:
                    out_ref[row] = jnp.zeros(out_ref.shape[1:], out_ref.dtype)
                out_ref[row, :, : piece.shape[1]] = piece
                row += 1
        else:
            out_ref[row : row + total.shape[0]] = total
            row += total.shape[0]


def lay_out(arrays, plan, part, width):
    blocks = 0
    for wide, terms in plan:
        shape = jax.eval_shape(lambda v: v[terms[0][1]], arrays[terms[0][0]]).shape
        blocks += -(-shape[1] // width) if wide else shape[0]
    moved = blocks * part * width * 4
    return call(
        functools.partial(lay_body, plan=plan, count=len(arrays)), [jax.ShapeDtypeStruct((blocks, part, width), BF)],
        arrays, [VMEM] * len(arrays), [VMEM], flops=moved, moved=moved, vmem=8, name="lay",
    )[0]


def add_up(arrays, plan, dtype=BF):
    outs = []
    for terms in plan:
        which, spot = terms[0]
        outs.append(jax.ShapeDtypeStruct(jax.eval_shape(lambda v: v[spot], arrays[which]).shape, dtype))
    moved = sum(o.size for o in outs) * 4
    return call(
        functools.partial(sum_body, plan=plan, count=len(arrays)), outs, arrays,
        [VMEM] * len(arrays), [VMEM] * len(outs), flops=moved, moved=moved, vmem=16, name="add",
    )


def copy_body(*refs, plan, count):
    outs, sem = refs[count:-1], refs[-1]
    copies = []
    for k, (which, source, out, spot) in enumerate(plan):
        copies.append(pltpu.make_async_copy(refs[which].at[source], outs[out].at[spot], sem.at[k]))
        copies[-1].start()
    for copy in copies:
        copy.wait()


def copy_out(arrays, shapes, plan):
    moved = sum(math.prod(shape) for shape in shapes) * 4
    return call(
        functools.partial(copy_body, plan=plan, count=len(arrays)),
        [jax.ShapeDtypeStruct(shape, arrays[0].dtype) for shape in shapes], arrays,
        [HBM] * len(arrays), [VMEM] * len(shapes),
        scratch=[pltpu.SemaphoreType.DMA((len(plan),))], moved=moved, vmem=4, name="copy",
    )


def stack(arrays):
    shape = (len(arrays),) + arrays[0].shape
    every = (slice(None),)
    (out,) = copy_out(arrays, [shape], [(i, every, 0, (i,)) for i in range(len(arrays))])
    return out


def assemble_body(idx, *refs, rows, count):
    pieces, (w_ref, row_ref, col_ref, low_scr, sem) = refs[:count], refs[count:]
    k = 0
    for piece in pieces:
        for j in range(piece.shape[0]):
            at = pl.ds(pl.multiple_of(idx[k] * rows, rows), rows)
            pltpu.make_async_copy(piece.at[j, pl.ds(0, 3)], w_ref.at[:, at, :], sem.at[0]).start()
            pltpu.make_async_copy(piece.at[j, 3, :, pl.ds(0, HEAD_DIM)], low_scr.at[at, :], sem.at[1]).start()
            k += 1
    pltpu.make_async_copy(low_scr, low_scr, sem.at[1]).wait()
    columns = low_scr[...].astype(F32)
    col_ref[...] = columns
    row_ref[...] = jnp.transpose(columns)[: row_ref.shape[0]]
    pltpu.make_async_copy(w_ref, w_ref, sem.at[0]).wait()


def project_body(*refs, with_q, spots, count):
    pieces, (w_ref, row_ref), outs = refs[:count], refs[count : count + 2], refs[count + 2 :]
    kv_ref, n_ref = outs[:2]
    gain, shift = row_ref[0:1, :], row_ref[1:2, :]
    for i, (which, lead) in enumerate(spots):
        plain, unused_inverse = normalize(pieces[which][lead].astype(F32))
        n_ref[i] = plain.astype(BF)
        normed = (plain * gain + shift).astype(BF)
        keys = mm(normed, w_ref[1])
        values = mm(normed, w_ref[2]) + row_ref[3:4, :]
        for h in range(HEADS):
            lanes = slice(h * HEAD_DIM, (h + 1) * HEAD_DIM)
            kv_ref[i, h] = keys[:, lanes].astype(BF)
            kv_ref[i, HEADS + h] = values[:, lanes].astype(BF)
        if with_q and i == 0:
            queries = mm(normed, w_ref[0]) + row_ref[2:3, :]
            for h in range(HEADS):
                outs[2][h] = queries[:, h * HEAD_DIM : (h + 1) * HEAD_DIM].astype(BF)


def ready_body(idx, *refs, rows, count, part):
    pieces, (own_ref, tok_ref) = refs[:count], refs[count : count + 2]
    w_ref, row_ref, col_ref, up_ref, kv_ref, n_ref, q_ref, n_first, low_scr, sem = refs[count + 2 :]
    assemble_body(idx, *pieces, w_ref, row_ref, col_ref, low_scr, sem, rows=rows, count=count)
    width = up_ref.shape[1]
    blocks = up_ref.shape[0]
    per = width // blocks
    source = lax.broadcasted_iota(I32, (per, width), 0)
    target = lax.broadcasted_iota(I32, (per, width), 1)
    total = jnp.zeros((blocks, width), F32)
    for k in range(blocks):
        spread = jnp.where(
            target == (source // part) * (blocks * part) + k * part + lax.rem(source, part), 1.0, 0.0
        ).astype(BF)
        mine = [row_ref[8 + k : 9 + k, j * per : (j + 1) * per] for j in range(blocks)]
        total += mm(jnp.concatenate(mine, axis=0).astype(BF), spread)
    up_ref[...] = total
    spots = [(0, slice(None))] + [(1, i) for i in range(tok_ref.shape[0])]
    project_body(own_ref, tok_ref, w_ref, row_ref, kv_ref, n_ref, q_ref, with_q=True, spots=spots, count=2)
    n_first[0] = n_ref[0]


def reach(sc, tab, rows):
    count = tab.shape[0] // 3
    min_low, min_high, unused = table_of(tab, count, sc[0])
    max_low, max_high, unused = table_of(tab, count, sc[0] + PLANE * rows - 1)
    return min_low, max_high, max_low, min_high


def plane_rows(sc, rows, shape, dim):
    spot = lax.broadcasted_iota(I32, shape, dim)
    place = spot + sc[1]
    for b in range(1, PLANE):
        place = jnp.where(spot >= b * rows, spot + (sc[1 + b] - b * rows), place)
    return place


def attend_body(sc, tab, *refs, kv_units):
    q_refs, kv_refs = refs[:PLANE], refs[PLANE:-8]
    keep_ref, send_ref, q_scr, s_scr, m_scr, acc_scr, kv_ref, sem = refs[-8:]
    count = tab.shape[0] // 3
    units, unused, rows, unused = kv_ref.shape
    k = 0
    for ref in kv_refs:
        for i in range(ref.shape[0]):
            pltpu.make_async_copy(ref.at[i], kv_ref.at[kv_units[k]], sem.at[kv_units[k]]).start()
            k += 1
    min_low, max_high, max_low, min_high = reach(sc, tab, rows)
    q_pos = plane_rows(sc, rows, (PLANE * rows, 1), 0)
    low, high, unused = table_of(tab, count, q_pos)
    ones = jnp.ones((rows, HEAD_DIM), BF)
    for b, ref in enumerate(q_refs):
        q_scr[:, b * rows : (b + 1) * rows] = ref[...]
    m_scr[...] = jnp.full(m_scr.shape, NEG, F32)
    acc_scr[...] = jnp.zeros(acc_scr.shape, F32)

    def keep_scores(u, allowed):
        for h in range(HEADS):
            scores = mm_nt(q_scr[h], kv_ref[u, h]) * SCALE2
            if allowed is not None:
                scores = jnp.where(allowed, scores, NEG)
            s_scr[u, h] = scores
            top = m_scr[h]
            for j in range(rows // HEAD_DIM):
                top = jnp.maximum(top, scores[:, j * HEAD_DIM : (j + 1) * HEAD_DIM])
            m_scr[h] = top

    def score_step(u, carry):
        start = sc[1 + PLANE + u]
        pltpu.make_async_copy(kv_refs[0].at[0], kv_ref.at[u], sem.at[u]).wait()
        needed = (start < max_high) & (start + rows > min_low)
        whole = (start >= max_low) & (start + rows <= min_high)

        @pl.when(needed & whole)
        def _():
            keep_scores(u, None)

        @pl.when(needed & jnp.logical_not(whole))
        def _():
            k_pos = start + lax.broadcasted_iota(I32, (1, rows), 1)
            keep_scores(u, (k_pos >= low) & (k_pos < high))

        return carry

    lax.fori_loop(0, units, score_step, 0)
    for h in range(HEADS):
        top = jnp.max(m_scr[h], axis=-1, keepdims=True)
        m_scr[h] = jnp.broadcast_to(jnp.where(top > 0.5 * NEG, top, 0.0), m_scr.shape[1:])

    def value_step(u, carry):
        start = sc[1 + PLANE + u]
        needed = (start < max_high) & (start + rows > min_low)

        @pl.when(needed)
        def _():
            for h in range(HEADS):
                soft = jnp.exp2(s_scr[u, h] - m_scr[h][:, :1]).astype(BF)
                wide = jnp.concatenate([kv_ref[u, HEADS + h], ones], axis=1)
                acc_scr[h] += mm(soft, wide)

        return carry

    lax.fori_loop(0, units, value_step, 0)
    lane = lax.broadcasted_iota(I32, (1, HEAD_DIM), 1)
    width = HEADS * HEAD_DIM
    for b in range(PLANE):
        ref, spot = (keep_ref, send_ref)[b % 2], b // 2
        at = slice(b * rows, (b + 1) * rows)
        logs = jnp.zeros((rows, HEAD_DIM), F32)
        for h in range(HEADS):
            total = acc_scr[h, at, HEAD_DIM:]
            some = total > 0.0
            safe = jnp.where(some, total, 1.0)
            ref[spot, :, h * HEAD_DIM : (h + 1) * HEAD_DIM] = acc_scr[h, at, :HEAD_DIM] / safe
            logs = jnp.where(lane == h, jnp.where(some, m_scr[h, at] + jnp.log2(safe), NEG), logs)
        ref[spot, :, width:] = logs


def in_parts(value, lane, first):
    out = jnp.zeros((value[0].shape[0], HEAD_DIM), F32)
    for h, column in enumerate(value):
        high = column.astype(BF).astype(F32)
        rest = column - high
        middle = rest.astype(BF).astype(F32)
        for i, part in enumerate((high, middle, rest - middle)):
            out = jnp.where(lane == first + i * HEADS + h, part, out)
    return out


def merge_body(mine_ref, other_ref, own_ref, far_ref):
    width = HEADS * HEAD_DIM
    lane = lax.broadcasted_iota(I32, (1, HEAD_DIM), 1)
    for b in range(2):
        lse_mine, lse_other = mine_ref[b, :, width:], other_ref[b, :, width:]
        top = jnp.maximum(lse_mine, lse_other)
        share_mine, share_other = jnp.exp2(lse_mine - top), jnp.exp2(lse_other - top)
        share = share_mine + share_other
        log_total = top + jnp.log2(share)
        share_mine, share_other = share_mine / share, share_other / share
        for h in range(HEADS):
            lanes = slice(h * HEAD_DIM, (h + 1) * HEAD_DIM)
            mixed = mine_ref[b, :, lanes] * share_mine[:, h : h + 1] + other_ref[b, :, lanes] * share_other[:, h : h + 1]
            if b == 0:
                own_ref[:, lanes] = mixed
            else:
                far_ref[:, lanes] = mixed.astype(BF)
        if b == 0:
            own_ref[:, width:] = log_total
        else:
            columns = [log_total[:, h : h + 1] for h in range(HEADS)]
            far_ref[:, width:] = in_parts(columns, lane, 0).astype(BF)


def middle_body(idx, sc, tab, *refs, rows, m_count, grad_count):
    m_refs, (tok_ref, own_ref, other_ref, cot_ref, row_ref, up_row_ref) = refs[:m_count], refs[m_count : m_count + 6]
    outs = refs[m_count + 6 :]
    out_ref, dmid_ref, d_ref, vec_ref = outs[:4]
    g_refs = outs[4 : 4 + grad_count]
    (w_out, w_up, w_down, g_out, g_up, g_down, dh_scr, sem, g_sem) = outs[4 + grad_count :]
    blocks, width = w_up.shape[0], w_up.shape[2]
    pieces = w_down.shape[0] // blocks
    count = tab.shape[0] // 3
    local = tok_ref.shape[0]
    spots = []
    for m_ref in m_refs:
        for spot in range(m_ref.shape[0]):
            owner = idx[len(spots)]
            spots.append(
                (m_ref, spot, pl.ds(pl.multiple_of(owner * rows, rows), rows), pl.ds(owner * blocks, blocks))
            )
    for m_ref, spot, at, unused in spots:
        pltpu.make_async_copy(m_ref.at[spot, 0], w_out.at[at, :], sem.at[0]).start()
    for m_ref, spot, unused, at in spots:
        pltpu.make_async_copy(m_ref.at[spot, pl.ds(1 + blocks, blocks)], w_down.at[at], sem.at[2]).start()
    for m_ref, spot, at, unused in spots:
        pltpu.make_async_copy(m_ref.at[spot, pl.ds(1, blocks)], w_up.at[:, at, :], sem.at[1]).start()

    pos = sc[1] + lax.broadcasted_iota(I32, (local, 1), 0)
    unused_low, unused_high, finish = table_of(tab, count, pos)
    live = (pos < finish).astype(F32)
    gain, shift = row_ref[5:6, :], row_ref[6:7, :]
    lane = lax.broadcasted_iota(I32, (1, HEAD_DIM), 1)
    logs, mixed = [], []
    for h in range(HEADS):
        lanes = slice(h * HEAD_DIM, (h + 1) * HEAD_DIM)
        lse_own = own_ref[:, width + h : width + h + 1]
        lse_other = sum(
            other_ref[:, width + i * HEADS + h : width + i * HEADS + h + 1].astype(F32) for i in range(3)
        )
        top = jnp.maximum(lse_own, lse_other)
        share_own, share_other = jnp.exp2(lse_own - top), jnp.exp2(lse_other - top)
        share = share_own + share_other
        logs.append(top + jnp.log2(share))
        mixed.append(
            own_ref[:, lanes] * (share_own / share) + other_ref[:, lanes].astype(F32) * (share_other / share)
        )
    mixed = jnp.concatenate(mixed, axis=1)
    attended = (mixed * live).astype(BF)
    cot = cot_ref[...]
    pltpu.make_async_copy(w_out, w_out, sem.at[0]).wait()
    middle = tok_ref[...].astype(F32) + mm(attended, w_out[...]) + row_ref[4:5, :]
    pltpu.make_async_copy(w_down, w_down, sem.at[2]).wait()
    for j in range(blocks):
        dh_scr[j] = mm_nt(cot, w_down[j * pieces : (j + 1) * pieces].reshape(width, width))
    plain, inverse = normalize(middle)
    normed = (plain * gain + shift).astype(BF)
    pltpu.make_async_copy(w_up, w_up, sem.at[1]).wait()
    total = middle + row_ref[7:8, :]
    d_norm = jnp.zeros(middle.shape, F32)
    ones = jnp.ones((8, local), BF)
    up_sums = []
    for j in range(blocks):
        up = w_up[j]
        down = w_down[j * pieces : (j + 1) * pieces].reshape(width, width)
        pre = mm(normed, up) + up_row_ref[j : j + 1, :]
        square = pre * pre
        t = jnp.tanh(GELU_A * pre * (1.0 + GELU_B * square))
        half = 0.5 * (1.0 + t)
        hidden = (pre * half).astype(BF)
        slope = half + 0.5 * pre * (1.0 - t * t) * (GELU_A * (1.0 + 3.0 * GELU_B * square))
        total = total + mm(hidden, down)
        d_pre = (dh_scr[j] * slope).astype(BF)
        d_norm = d_norm + mm_nt(d_pre, up)
        g_down[j * pieces : (j + 1) * pieces] = mm_tn(hidden, cot).astype(BF).reshape(pieces, rows, width)
        g_up[j] = mm_tn(normed, d_pre).astype(BF)
        up_sums.append(mm(ones, d_pre)[0:1])
    g_pieces = g_refs[0].shape[0]
    spots = []
    for i in range(pieces):
        g_ref, spot, where = g_refs[i // g_pieces], i % g_pieces, idx[pieces + i]
        spots.append((g_ref, spot, pl.ds(pl.multiple_of(where * rows, rows), rows)))
        at = pl.ds(where * blocks, blocks)
        pltpu.make_async_copy(g_down.at[at], g_ref.at[spot, pl.ds(1 + blocks, blocks)], g_sem).start()
    for g_ref, spot, at in spots:
        pltpu.make_async_copy(g_up.at[:, at, :], g_ref.at[spot, pl.ds(1, blocks)], g_sem).start()
    out_ref[...] = total.astype(BF)
    cot_f = cot.astype(F32)
    d_middle = cot_f + norm_back(d_norm, plain, inverse, gain)
    dmid_ref[...] = d_middle
    d_branch = d_middle.astype(BF)
    g_out[...] = mm_tn(attended, d_branch).astype(BF)
    for g_ref, spot, at in spots:
        pltpu.make_async_copy(g_out.at[at, :], g_ref.at[spot, 0], g_sem).start()
    d_att = mm_nt(d_branch, w_out[...]).astype(BF) * live.astype(BF)
    d_ref[:, :width] = d_att
    product = d_att.astype(F32) * mixed
    deltas = [
        jnp.sum(product[:, h * HEAD_DIM : (h + 1) * HEAD_DIM], axis=-1, keepdims=True) for h in range(HEADS)
    ]
    d_ref[:, width:] = (in_parts(deltas, lane, 0) + in_parts(logs, lane, 3 * HEADS)).astype(BF)

    sums = [jnp.sum(v, axis=0, keepdims=True) for v in (d_middle, d_norm * plain, d_norm, cot_f)]
    sums = jnp.concatenate(sums + up_sums + [jnp.zeros((HEAD_DIM - 4 - blocks, width), F32)], axis=0)
    columns = jnp.transpose(sums)
    if pieces > 1:
        per = pieces // blocks
        vec_ref[...] = jnp.where(lane < 4, columns, 0.0)
        for j in range(blocks):
            column = jnp.broadcast_to(columns[:, 4 + j : 5 + j], (width, HEAD_DIM)).reshape(
                per, blocks, rows, HEAD_DIM
            )
            wide_lane = lane.reshape(1, 1, HEAD_DIM)
            placed = sum(jnp.where(wide_lane == 4 + i, column[:, i], 0.0) for i in range(blocks))
            vec_ref[j * per * rows : (j + 1) * per * rows, :] += placed.reshape(per * rows, HEAD_DIM)
    else:
        vec_ref[...] = jnp.where(lane < 4 + blocks, columns, 0.0)
    for g_ref in g_refs:
        pltpu.make_async_copy(g_ref, g_ref, g_sem).wait()


def back_unit(sc, tab, plane, kv_ref, spot, q_ref, do_refs, stat_refs, dq_refs, put, none):
    count = tab.shape[0] // 3
    rows = kv_ref.shape[2]
    min_low, max_high, max_low, min_high = reach(sc, tab, rows)
    low, high, unused = table_of(tab, count, plane_rows(sc, rows, (1, PLANE * rows), 1))
    start = sc[1 + PLANE + plane]
    needed = (start < max_high) & (start + rows > min_low)
    whole = (start >= max_low) & (start + rows <= min_high)

    def unit(masked):
        k_pos = start + lax.broadcasted_iota(I32, (rows, 1), 0)
        for h in range(HEADS):
            key, value = kv_ref[spot, h], kv_ref[spot, HEADS + h]
            d_key, d_value = 0.0, 0.0
            for half in do_refs:
                at = slice(2 * half * rows, 2 * (half + 1) * rows)
                q, do, stat_ref = q_ref[h, at], do_refs[half][h], stat_refs[half]
                soft = jnp.exp2(mm_nt(key, q) * SCALE2 - stat_ref[HEADS + h : HEADS + h + 1, :])
                if masked:
                    soft = jnp.where((k_pos >= low[:, at]) & (k_pos < high[:, at]), soft, 0.0)
                d_soft = mm_nt(value, do)
                d_scores = (soft * (d_soft - stat_ref[h : h + 1, :])).astype(BF)
                d_value = d_value + mm(soft.astype(BF), do)
                d_key = d_key + mm(d_scores, q)
                dq_refs[half][h] += mm_tn(key, d_scores)
            put(slice(h * HEAD_DIM, (h + 1) * HEAD_DIM), d_key * SCALE)
            put(slice((HEADS + h) * HEAD_DIM, (HEADS + h + 1) * HEAD_DIM), d_value)

    @pl.when(needed & whole)
    def _():
        unit(False)

    @pl.when(needed & jnp.logical_not(whole))
    def _():
        unit(True)

    @pl.when(jnp.logical_not(needed))
    def _():
        none()


def unpack_rows(packets, do_ref, stat_ref):
    rows, width = packets[0].shape[0], HEADS * HEAD_DIM
    for b, ref in enumerate(packets):
        at = slice(b * rows, (b + 1) * rows)
        for h in range(HEADS):
            do_ref[h, at] = ref[:, h * HEAD_DIM : (h + 1) * HEAD_DIM]
        tail = jnp.transpose(ref[:, width:].astype(F32))
        parts = [tail[i * HEADS : (i + 1) * HEADS] for i in range(6)]
        stat_ref[:, at] = jnp.concatenate([parts[0] + parts[1] + parts[2], parts[3] + parts[4] + parts[5]], axis=0)


def open_body(sc, tab, q_ref, d_own, d_c, kv_ref, do_ref, stat_ref, dq_ref, part_ref, *, units):
    unpack_rows((d_own, d_c), do_ref, stat_ref)
    dq_ref[...] = jnp.zeros(dq_ref.shape, F32)
    for j, (plane, spot) in enumerate(units):

        def put(lanes, value, j=j):
            part_ref[j, :, lanes] = value

        def none(j=j):
            part_ref[j] = jnp.zeros(part_ref.shape[1:], F32)

        back_unit(sc, tab, plane, kv_ref, spot, q_ref, {0: do_ref}, {0: stat_ref}, {0: dq_ref}, put, none)


def keep_planes(units, n_ref, w_ref, d_refs, nk_ref, sum_ref, nk_in, sum_in, dkv_scr):
    width = w_ref.shape[1]
    ones = jnp.ones((8, dkv_scr.shape[1]), BF)
    product = 0.0 if nk_in is None else nk_in[...]
    sums = 0.0 if sum_in is None else sum_in[...]
    for j, (unused, spot) in enumerate(units):
        d_refs[j][...] = (mm_nt(dkv_scr[j, :, :width], w_ref[1]) + mm_nt(dkv_scr[j, :, width:], w_ref[2])).astype(BF)
        product = product + mm_tn(n_ref[spot], dkv_scr[j])
        sums = sums + mm(ones, dkv_scr[j])
    nk_ref[...] = product
    sum_ref[...] = sums


def close_body(
    sc, tab, q_ref, d_x, d_xc, kv_ref, n_ref, w_ref, part_ref, do_ref, stat_ref, dq_ref, nk_ref, sum_ref, *refs, units
):
    d_refs, dkv_scr = refs[:-1], refs[-1]
    unpack_rows((d_x, d_xc), do_ref, stat_ref)
    dq_ref[...] = jnp.zeros(dq_ref.shape, F32)
    for j, (plane, spot) in enumerate(units):

        def put(lanes, value, j=j):
            dkv_scr[j, :, lanes] = (part_ref[j, :, lanes] + value).astype(BF)

        def none(j=j):
            dkv_scr[j] = jnp.zeros(dkv_scr.shape[1:], BF)

        back_unit(sc, tab, plane, kv_ref, spot, q_ref, {1: do_ref}, {1: stat_ref}, {1: dq_ref}, put, none)
    keep_planes(units, n_ref, w_ref, d_refs, nk_ref, sum_ref, None, None, dkv_scr)


def back_body(
    sc, tab, q_ref, do_one, do_two, stat_one, stat_two, kv_ref, n_ref, w_ref, one_in, two_in, nk_in, sum_in,
    d_ref, one_ref, two_ref, nk_ref, sum_ref, dkv_scr, *, unit,
):
    one_ref[...] = one_in[...]
    two_ref[...] = two_in[...]

    def put(lanes, value):
        dkv_scr[0, :, lanes] = value.astype(BF)

    def none():
        dkv_scr[0] = jnp.zeros(dkv_scr.shape[1:], BF)

    halves = {0: do_one, 1: do_two}, {0: stat_one, 1: stat_two}, {0: one_ref, 1: two_ref}
    back_unit(sc, tab, unit[0], kv_ref, unit[1], q_ref, *halves, put, none)
    keep_planes([unit], n_ref, w_ref, [d_ref], nk_ref, sum_ref, nk_in, sum_in, dkv_scr)


def query_block(dq_refs, b, rows):
    ref, at = dq_refs[b // 2], slice((b % 2) * rows, (b % 2 + 1) * rows)
    return jnp.concatenate([ref[h, :, at] * SCALE for h in range(HEADS)], axis=0).astype(BF)


def message_body(idx, *refs, rows):
    n_refs, dq_refs = refs[:PLANE], refs[PLANE : PLANE + 2]
    (nk_ref, sum_ref, w_ref, col_ref, vec_ref), (full, vec) = refs[PLANE + 2 : PLANE + 7], refs[-2:]
    msg_refs = refs[PLANE + 7 : -2]
    local = n_refs[0].shape[1]
    width = w_ref.shape[1]
    q_product = jnp.zeros((width, width), F32)
    q_sums = jnp.zeros((8, width), F32)
    ones = jnp.ones((8, local), BF)
    for b, n_ref in enumerate(n_refs):
        d_query = query_block(dq_refs, b, local)
        q_product += lax.dot_general(n_ref[0], d_query, (((0,), (1,)), ((), ())), preferred_element_type=F32)
        q_sums += mm_nt(ones, d_query)
    gain, shift = col_ref[:, 0:1], col_ref[:, 1:2]
    lane = lax.broadcasted_iota(I32, (1, HEAD_DIM), 1)
    gain_grad = jnp.zeros((width, 1), F32)
    shift_grad = jnp.zeros((width, 1), F32)
    columns = []
    for i in range(3):
        lanes = slice(i * width, (i + 1) * width)
        if i == 0:
            product, sums = q_product, q_sums[0:1]
        else:
            at = slice((i - 1) * width, i * width)
            product, sums = nk_ref[:, at], sum_ref[0:1, at]
        weight = w_ref[i].astype(F32)
        full[:, lanes] = (product * gain + shift * sums).astype(BF)
        gain_grad += jnp.sum(product * weight, axis=-1, keepdims=True)
        shift_grad += jnp.sum(weight * sums, axis=-1, keepdims=True)
        if i != 1:
            columns.append(jnp.transpose(jnp.broadcast_to(sums, (HEAD_DIM, width))))
    vec[...] = vec_ref[...]
    for at, column in ((8, gain_grad), (9, shift_grad), (10, columns[0]), (11, columns[1])):
        vec[...] += jnp.where(lane == at, column, 0.0)
    full[:, 3 * width :] = vec[...].astype(BF)
    k = 0
    for msg_ref in msg_refs:
        for i in range(msg_ref.shape[0]):
            msg_ref[i] = full[pl.ds(pl.multiple_of(idx[k] * rows, rows), rows), :]
            k += 1


def query_body(dq_one, dq_two, w_ref, keep_ref, send_ref):
    rows = keep_ref.shape[1]
    for b in range(PLANE):
        d_query = query_block((dq_one, dq_two), b, rows)
        out = lax.dot_general(d_query, w_ref[0], (((0,), (1,)), ((), ())), preferred_element_type=F32)
        (keep_ref, send_ref)[b % 2][b // 2] = out.astype(BF)


def finish_body(tok_ref, dmid_ref, row_ref, last_ref, *refs):
    plain, inverse = normalize(tok_ref[...].astype(F32))
    lines = 0 if len(last_ref.shape) == 2 else tok_ref.shape[0] // last_ref.shape[1]
    last = last_ref[:lines].reshape(tok_ref.shape) if lines else last_ref[...]
    total = last.astype(F32)
    for ref in refs[:-1]:
        total = total + ref[...].astype(F32)
    refs[-1][...] = (dmid_ref[...] + norm_back(total, plain, inverse, row_ref[0:1, :])).astype(BF)


def matrices_body(*refs, starts):
    terms, (out_ref, up_ref, down_ref) = refs[:-3], refs[-3:]
    width = out_ref.shape[1]
    part = out_ref.shape[0]
    blocks = up_ref.shape[1] // width

    def block(i):
        total = terms[0][starts[0] + i].astype(F32)
        for term, start in zip(terms[1:], starts[1:], strict=True):
            total = total + term[start + i].astype(F32)
        return total

    out_ref[...] = block(0)
    for j in range(blocks):
        up_ref[:, j * width : (j + 1) * width] = block(1 + j)
        down_ref[j * part : (j + 1) * part, :] = block(1 + blocks + j)


def unpack_body(*refs, w_blocks):
    terms, (qkv_ref, *vec_refs, up_ref, pad_ref) = refs[:-11], refs[-11:]
    total = terms[0][...]
    for term in terms[1:]:
        line = jnp.concatenate([term[j] for j in range(w_blocks)], axis=1)
        total = total + line[:, : total.shape[1]].astype(F32)
    width = qkv_ref.shape[1]
    part = qkv_ref.shape[0]
    qkv_ref[...] = total[:, :width]
    pad_ref[...] = jnp.zeros(pad_ref.shape, F32)
    pad_ref[:part] = total[:, width:]
    rows = jnp.transpose(pad_ref[...])
    for ref, row in zip(vec_refs, (8, 9, 10, 11, 0, 1, 2, 3), strict=True):
        ref[...] = rows[row : row + 1, :part]
    blocks = up_ref.shape[1] // part
    up_ref[...] = jnp.concatenate([rows[4 + j : 5 + j, :part] for j in range(blocks)], axis=1)


def shards(
    tokens, w_qkv, w_out, w_up, w_down,
    norm1_gain, norm1_bias, query_bias, value_bias, out_bias, norm2_gain, norm2_bias, up_bias, down_bias,
    cotangent, table_start, support_count, query_count, *, R, F,
):
    A = R // PLANE
    count = R * F
    local, width = tokens.shape[1], tokens.shape[2]
    part = w_qkv.shape[0]
    hidden = w_up.shape[1]
    blocks = hidden // width
    aligned = part % 16 == 0
    rows = part if aligned else width
    pieces = count if aligned else 1
    sds = jax.ShapeDtypeStruct

    r, f = lax.axis_index("rows"), lax.axis_index("fsdp")
    a, x, c = r // PLANE, (r // 2) % 2, r % 2

    def swap_c(v):
        return lax.ppermute(v, "rows", [(i, i ^ 1) for i in range(R)])

    def swap_x(v):
        return lax.ppermute(v, "rows", [(i, i ^ 2) for i in range(R)])

    def turn_a(v, s):
        return lax.ppermute(
            v, "rows", [(i, ((i // PLANE + s) % A) * PLANE + i % PLANE) for i in range(R)]
        )

    def turn_f(v, t):
        return lax.ppermute(v, "fsdp", [(i, (i + t) % F) for i in range(F)])

    def turn_xf(v, t):
        return lax.ppermute(
            v, ("rows", "fsdp"),
            [(i * F + j, (i ^ 2) * F + (j + t) % F) for i in range(R) for j in range(F)],
        )

    def owners(order):
        cr, t, xr, s = (np.array(list(z), np.int32) for z in zip(*order, strict=True))
        plane = lax.rem(a - s + A, A)
        return (((plane * 2 + (x ^ xr)) * 2 + (c ^ cr)) * F + lax.rem(f - t + F, F)).astype(I32)

    block_x, block_c = np.array([0, 0, 1, 1], np.int32), np.array([0, 1, 0, 1], np.int32)
    block_start = (a * 4 + (x ^ block_x) * 2 + (c ^ block_c)) * local
    unit_start = (lax.rem(a - np.arange(A, dtype=np.int32) + A, A) * 4 + 2 * x + c) * local
    sc = jnp.concatenate([(a * 4 * local)[None], block_start, unit_start]).astype(I32)
    tab = jnp.concatenate([table_start[0], support_count[0], query_count[0]])
    q_order = [(cr, t, xr, s) for cr in range(2) for t in range(F) for xr in range(2) for s in range(A)]
    parts = [slice(0, A // 2), slice(A // 2, A)]
    m_order = [
        (cr, t, xr, s)
        for cr in range(2)
        for planes in (range(2, A), range(2))
        for xr, t in [(0, 0), (1, 0)] + [(0, t) for t in range(1, F)] + [(1, t) for t in range(1, F)]
        for s in planes
    ]
    every_owner = owners(q_order + m_order)
    q_owner, m_owner = every_owner[:count], every_owner[count:]
    if aligned:
        q_idx, idx = q_owner, jnp.concatenate([m_owner, q_owner])
    else:
        q_idx, idx = jnp.zeros((1,), I32), jnp.zeros((2,), I32)

    near = list(range(1, A))
    early, late = near[:2], near[2:]
    own = tokens[0]
    vectors = [
        v.reshape(1, -1)
        for v in (
            norm1_gain, norm1_bias, query_bias, value_bias, out_bias, norm2_gain, norm2_bias, down_bias, up_bias
        )
    ]
    wide = 3 * width + HEAD_DIM
    pack_in = [w_qkv, w_out, w_up, w_down, *vectors]
    q_own, m_own = pl.pallas_call(
        pack_body,
        grid=(1,),
        out_shape=[sds((4, part, width), BF), sds((1 + 2 * blocks, part, width), BF)],
        in_specs=[pl.BlockSpec(v.shape, lambda i: (0, 0)) for v in pack_in],
        out_specs=[VMEM] * 2,
        scratch_shapes=[pltpu.VMEM((HEAD_DIM, HEAD_DIM), F32)],
        compiler_params=pltpu.CompilerParams(vmem_limit_bytes=56 * MIB),
        cost_estimate=pl.CostEstimate(flops=0, bytes_accessed=16 * part * width, transcendentals=0),
        name="pack",
    )(*pack_in)
    tok_z, m_z = {0: own}, {0: m_own}
    *q_z, tok_z[1], m_z[1], sc, tab, q_idx, idx = together(
        *(turn_a(q_own, s) for s in range(1, A)), turn_a(own, 1), turn_a(m_own, 1), sc, tab, q_idx, idx
    )
    q_z = jnp.stack([q_own] + q_z)
    moved = [swap_x(q_z)] + [v for t in range(1, F) for v in (turn_f(q_z, t), turn_xf(q_z, t))]
    *q_far, tok_z[2], m_z[2] = together(*moved, turn_a(tok_z[1], 1), turn_a(m_z[1], 1))
    tok_early, m_early = jnp.stack([tok_z[1], tok_z[2]]), jnp.stack([m_z[0], m_z[1]])
    early_x, early_f = swap_x(m_early), [turn_f(m_early, t) for t in range(1, F)]
    tok_z[3], m_z[3] = turn_a(tok_z[2], 1), turn_a(m_z[2], 1)
    q_four = jnp.stack([q_z] + q_far)
    q_other = swap_c(q_four)
    q_pieces = [q_four.reshape(count // 2, 4, part, width), q_other.reshape(count // 2, 4, part, width)]
    if not aligned:
        stacked = jnp.concatenate(q_pieces)
        by_owner = jnp.zeros_like(stacked).at[q_owner].set(stacked)
        q_pieces = [by_owner.transpose(1, 0, 2, 3).reshape(1, 4, width, width)]
    key_shape = (2 * HEADS, local, HEAD_DIM)
    w_all, row_vec, col_vec, up_row, kv_early, n_early, q, n_first = call(
        functools.partial(ready_body, rows=rows, count=len(q_pieces), part=part),
        [
            sds((3, width, width), BF), sds((16, width), F32), sds((width, HEAD_DIM), F32), sds((blocks, width), F32),
            sds((3,) + key_shape, BF), sds((3, local, width), BF), sds((HEADS, local, HEAD_DIM), BF),
            sds((1, local, width), BF),
        ],
        [q_idx, *q_pieces, own, tok_early], [SMEM] + [HBM] * len(q_pieces) + [VMEM] * 2, [VMEM] * 8,
        scratch=[pltpu.VMEM((width, HEAD_DIM), BF), pltpu.SemaphoreType.DMA((2,))],
        flops=4 * (A + 1) * local * width * width, moved=4 * width * wide, vmem=12, name="ready",
    )

    tok_z[3], m_z[3], early_x, q_x, *early_f = together(tok_z[3], m_z[3], early_x, swap_x(q), *early_f)
    for s in range(4, A):
        tok_z[s], m_z[s] = together(turn_a(tok_z[s - 1], 1), turn_a(m_z[s - 1], 1))
    q_blocks = [q, swap_c(q), q_x, swap_c(q_x)]
    late = list(range(3, A))
    tok_late = jnp.stack([tok_z[s] for s in late]) if A > 4 else tok_z[3][None]
    m_late = stack([m_z[s] for s in range(2, A)])
    late_x, late_f = swap_x(m_late), [turn_f(m_late, t) for t in range(1, F)]
    early_xf = [turn_f(early_x, t) for t in range(1, F)]
    kv_late, n_late = call(
        functools.partial(project_body, with_q=False, spots=[(0, i) for i in range(len(late))], count=1),
        [sds((len(late),) + key_shape, BF), sds((len(late), local, width), BF)],
        [after(tok_late, m_late), w_all, row_vec], [VMEM] * 3, [VMEM] * 2,
        flops=4 * len(late) * local * width * width, moved=8 * len(late) * local * width, vmem=8, name="project",
    )
    where = {s: (kv_early, n_early, s) if s < 3 else (kv_late, n_late, s - 3) for s in range(A)}

    unit = PLANE * local
    work = 4 * unit * A * local * width
    packet = width + HEAD_DIM
    att_keep, att_send, q_plane = call(
        functools.partial(attend_body, kv_units=list(range(A))),
        [sds((2, local, packet), F32)] * 2 + [sds((HEADS, unit, HEAD_DIM), BF)],
        [sc, tab, *q_blocks, kv_early, kv_late], [SMEM, SMEM] + [VMEM] * PLANE + [ANY] * 2, [VMEM] * 3,
        scratch=[
            pltpu.VMEM((A, HEADS, unit, local), F32),
            pltpu.VMEM((HEADS, unit, HEAD_DIM), F32), pltpu.VMEM((HEADS, unit, 2 * HEAD_DIM), F32),
            pltpu.VMEM((A, 2 * HEADS, local, HEAD_DIM), BF), pltpu.SemaphoreType.DMA((A,)),
        ],
        flops=work, moved=8 * A * local * width, trans=HEADS * unit * A * local, vmem=10 + 5 * A, name="attend",
    )
    early_side = [m_early, early_x, *early_f]
    att_keep, att_send, late_x, *more = together(
        att_keep, att_send, late_x, *late_f, *(swap_c(v) for v in early_side[:2])
    )
    late_f, early_c = list(more[: F - 1]), list(more[F - 1 :])
    att_recv = swap_c(att_send)
    late_xf = [turn_f(late_x, t) for t in range(1, F)]
    att_own, att_far = call(
        merge_body, [sds((local, packet), F32), sds((local, packet), BF)], [att_keep, att_recv], [VMEM] * 2,
        [VMEM] * 2, flops=32 * local * packet, moved=20 * local * packet, vmem=8, name="merge",
    )
    late_side = [m_late, late_x, *late_f]
    att_other, *more = together(
        swap_x(att_far), *late_xf, *(swap_c(v) for v in [*early_f, *early_xf, *late_side])
    )
    late_xf, more = list(more[: F - 1]), list(more[F - 1 :])
    early_c += more[: 2 * F - 2]
    late_c = more[2 * F - 2 :] + [swap_c(v) for v in late_xf]
    m_arrays = late_side + late_xf + early_side + early_xf + late_c + early_c
    if not aligned:
        stacked = jnp.concatenate(m_arrays)
        by_owner = jnp.zeros_like(stacked).at[m_owner].set(stacked)
        m_arrays = [
            jnp.concatenate(
                [
                    by_owner[:, 0].reshape(1, width, width),
                    by_owner[:, 1 : 1 + blocks].transpose(1, 0, 2, 3).reshape(blocks, width, width),
                    by_owner[:, 1 + blocks :].reshape(blocks, width, width),
                ]
            )[None]
        ]

    spots = [(t, xr) for t in range(F) for xr in range(2)]
    grad_count = 4 * F if aligned else 1
    g_shape = sds((pieces // grad_count, 1 + 2 * blocks, rows, width), BF)
    got = call(
        functools.partial(middle_body, rows=rows, m_count=len(m_arrays), grad_count=grad_count),
        [
            sds((local, width), BF), sds((local, width), F32), sds((local, packet), BF), sds((width, HEAD_DIM), F32),
        ] + [g_shape] * grad_count,
        [idx, sc, tab, *m_arrays, own, att_own, att_other, cotangent[0], row_vec, up_row],
        [SMEM] * 3 + [HBM] * len(m_arrays) + [VMEM] * 6,
        [VMEM] * 4 + [HBM] * grad_count,
        scratch=[
            pltpu.VMEM((width, width), BF), pltpu.VMEM((blocks, width, width), BF),
            pltpu.VMEM((pieces * blocks, rows, width), BF),
            pltpu.VMEM((width, width), BF), pltpu.VMEM((blocks, width, width), BF),
            pltpu.VMEM((pieces * blocks, rows, width), BF), pltpu.VMEM((blocks, local, width), F32),
            pltpu.SemaphoreType.DMA((3,)), pltpu.SemaphoreType.DMA,
        ],
        flops=6 * local * width * width * (1 + 2 * blocks), moved=4 * width * width * (1 + 2 * blocks),
        trans=local * hidden, vmem=52, name="middle",
    )
    *got, n_x = together(*got, swap_x(after(n_first, att_other)))
    outputs, d_middle, d_own, vec = got[:4]
    grads = got[4:]
    d_c = swap_c(d_own)

    lead = (A, 1 + 2 * blocks, part, width)
    if aligned:
        relative = [g.reshape(lead) for g in grads]
    else:
        whole = grads[0][0]
        by_owner = jnp.concatenate(
            [
                whole[0].reshape(count, 1, part, width),
                whole[1 : 1 + blocks].reshape(blocks, count, part, width).transpose(1, 0, 2, 3),
                whole[1 + blocks :].reshape(count, blocks, part, width),
            ],
            axis=1,
        )
        by_owner = by_owner[q_owner].reshape((4 * F,) + lead)
        relative = [by_owner[i] for i in range(4 * F)]
    g_near = {spot: relative[i] for i, spot in enumerate(spots)}
    g_far = {spot: swap_c(after(relative[2 * F + i], d_c)) for i, spot in reversed(list(enumerate(spots)))}

    def sums_of(keys, half, *others):
        arrays = [g_near[keys], g_far[keys], *others]
        return add_up(arrays, [[(0, (half,)), (1, (half,))] + [(2 + i, ()) for i in range(len(others))]])[0]

    first, second = parts
    half = A // 2
    ways = {}

    def joined(keys, planes):
        arrays = [v for key in keys for v in (g_near[key], g_far[key])]
        return join_up(arrays, [[(2 * i, (planes,)), (2 * i + 1, (planes,))] for i in range(len(keys))])[0]

    def start_ways(step):
        if step == 1:
            for t in range(1, F):
                ways["f", t] = turn_f(joined([(t, 1), (t, 0)], first), F - t)
            ways["x"] = swap_x(joined([(t, 1) for t in range(F)], second))
        if step == 2:
            return [("f", t) for t in range(1, F)] + ["x"]
        if step == 3:
            arrays = [g_near[0, 1], g_far[0, 1], *(ways["f", t] for t in range(1, F))]
            plan = [[(0, (first,)), (1, (first,))] + [(1 + t, (slice(0, half),)) for t in range(1, F)]]
            ways["x", F] = swap_x(add_up(arrays, plan)[0])
            for t in range(1, F):
                arrays = [g_near[t, 0], g_far[t, 0], ways["x"]]
                plan = [[(0, (second,)), (1, (second,)), (2, (slice(t * half, (t + 1) * half),))]]
                ways["f2", t] = turn_f(add_up(arrays, plan)[0], F - t)
            return [("x", F)] + [("f2", t) for t in range(1, F)]
        return []

    pair = [(s, where[s][2]) for s in (1, 2)]
    dq_shape = sds((HEADS, HEAD_DIM, 2 * local), F32)
    half_shapes = [sds((HEADS, 2 * local, HEAD_DIM), BF), sds((2 * HEADS, 2 * local), F32), dq_shape]
    keys = list(g_far)
    do_one, stat_one, dq_one, part_sums, d_x, *more = together(
        *call(
            functools.partial(open_body, units=pair), [*half_shapes, sds((2, local, 2 * width), F32)],
            [sc, tab, q_plane, d_own, d_c, kv_early], [SMEM] * 2 + [VMEM] * 4, [VMEM] * 4,
            flops=2 * work // A, moved=16 * unit * width, trans=HEADS * unit * local, vmem=16, name="open",
        ),
        swap_x(d_own), *(g_far[k] for k in keys),
    )
    g_far.update(zip(keys, more, strict=True))
    d_xc = swap_c(d_x)
    start_ways(1)
    got = together(
        *call(
            functools.partial(close_body, units=pair),
            [*half_shapes, sds((width, 2 * width), F32), sds((8, 2 * width), F32)] + [sds((local, width), BF)] * 2,
            [sc, tab, q_plane, d_x, d_xc, kv_early, n_early, w_all, part_sums],
            [SMEM] * 2 + [VMEM] * 7, [VMEM] * 7, scratch=[pltpu.VMEM((2, local, 2 * width), BF)],
            flops=3 * work // A, moved=16 * unit * width, trans=HEADS * unit * local, vmem=16, name="close",
        ),
    )
    do_two, stat_two, dq_two, n_product, sums, d_sum, d_next = got
    carried = [dq_one, dq_two, n_product, sums]
    q_now = q_plane
    for step, s in enumerate([*near[2:], 0], 1):
        kv_now, n_now, spot = where[s]
        outs = call(
            functools.partial(back_body, unit=(s, spot)),
            [sds((local, width), BF), dq_shape, dq_shape, sds((width, 2 * width), F32), sds((8, 2 * width), F32)],
            [sc, tab, q_now, do_one, do_two, stat_one, stat_two, kv_now, n_now, w_all, *carried],
            [SMEM] * 2 + [VMEM] * 12, [VMEM] * 5, scratch=[pltpu.VMEM((1, local, 2 * width), BF)],
            flops=work // A * 5 // 2 + 8 * local * width * width, moved=16 * unit * width,
            trans=HEADS * unit * local, name="back",
        )
        keys = start_ways(step + 1)
        got = together(*outs, turn_a(d_sum, 1), *(ways[k] for k in keys))
        outs, d_recv = got[:5], got[5]
        ways.update(zip(keys, got[6:], strict=True))
        (d_sum,) = add_up([d_next, d_recv], [[(0, ()), (1, ())]])
        d_next, *carried = outs
        q_now = after(q_plane, d_sum)

    dq_one, dq_two, n_product, sums = carried
    n_blocks = [n_first, swap_c(n_first), n_x, swap_c(n_x)]

    half_count = 2 * F
    msg_lead = (A, part, wide)
    msg_shape = [sds((pieces // 2, rows, wide), BF)] * 2 if aligned else [sds((1, rows, wide), BF)]
    message = call(
        functools.partial(message_body, rows=rows),
        msg_shape,
        [q_idx, *n_blocks, dq_one, dq_two, n_product, sums, w_all, col_vec, vec],
        [SMEM] + [VMEM] * (7 + PLANE), [VMEM] * len(msg_shape),
        scratch=[pltpu.VMEM((width, wide), BF), pltpu.VMEM((width, HEAD_DIM), F32)],
        flops=2 * local * width * width, moved=8 * width * wide, vmem=8, name="message",
    )
    g_sums = {}
    arrays = [g_near[0, 0], g_far[0, 0], ways["x", F], *(ways["f", t] for t in range(1, F))]
    plan = [
        [(0, (s,)), (1, (s,)), (2, (s,))] + [(2 + t, (half + s,)) for t in range(1, F)] for s in range(half)
    ]
    g_sums.update(zip(range(half), add_up(arrays, plan), strict=True))
    arrays = [g_near[0, 0], g_far[0, 0], ways["x"], *(ways["f2", t] for t in range(1, F))]
    plan = [
        [(0, (s,)), (1, (s,)), (2, (s - half,))] + [(2 + t, (s - half,)) for t in range(1, F)]
        for s in range(half, A)
    ]
    g_sums.update(zip(range(half, A), add_up(arrays, plan), strict=True))
    if not aligned:
        flat = message[0][0]
        at = slice(3 * width + 4, 3 * width + 4 + blocks)
        up_part = flat[:, at].T.reshape(count, blocks, part)
        by_owner = flat.reshape(count, part, wide)
        by_owner = by_owner.at[:, :, at].set(up_part.transpose(0, 2, 1))
        by_owner = by_owner[q_owner]
        message = [by_owner[: count // 2], by_owner[count // 2 :]]
    query_keep, query_send = call(
        query_body, [sds((2, local, width), BF)] * 2, [after(dq_one, message[0]), dq_two, w_all], [VMEM] * 3, [VMEM] * 2,
        flops=8 * local * width * width, moved=8 * local * width, vmem=8, name="query",
    )
    w_far, query_recv = together(swap_c(message[1]), swap_c(query_send))
    w_far = w_far.reshape((half_count,) + msg_lead)
    w_near = message[0].reshape((half_count,) + msg_lead)
    w_both = add_up([w_near, w_far], [[(0, (i,)), (1, (i,))] for i in range(half_count)])
    got = []
    for (t, xr), sent in zip(spots, w_both, strict=True):
        if xr:
            sent = turn_xf(sent, F - t) if t else swap_x(sent)
        elif t:
            sent = turn_f(sent, F - t)
        got.append(sent)
    lines = local // part
    every = ()
    sent = d_sum
    *got, arrived, g_two = together(*got, turn_a(sent, 1), turn_a(g_sums[2], A - 2))
    w_terms = {s: [(i, (s,)) for i in range(len(got))] for s in range(A)}
    w_blocks = -(-wide // width)
    packs = {}
    for s in near:
        arrays, plan = list(got), [(True, w_terms[s])]
        if s != 2:
            arrays.append(g_sums[s])
            plan.append((False, [(len(got), every)]))
        packs[s] = turn_a(lay_out(arrays, plan, part, width), A - s)
    (w_own,) = add_up(got, [w_terms[0]], F32)
    grad_qkv, *vector_grads, up_grad = call(
        functools.partial(unpack_body, w_blocks=w_blocks),
        [sds((part, 3 * width), F32)] + [sds((1, part), F32)] * 8 + [sds((1, blocks * part), F32)],
        [w_own, *packs.values()], [VMEM] * A, [VMEM] * 10, scratch=[pltpu.VMEM((HEAD_DIM, HEAD_DIM), F32)],
        moved=16 * part * width, vmem=8, name="unpack",
    )

    others = [s for s in near if s != 2]
    starts = [0, 0] + [w_blocks] * len(others)
    grad_out, grad_up, grad_down = call(
        functools.partial(matrices_body, starts=starts),
        [sds((part, width), F32), sds((part, hidden), F32), sds((blocks * part, width), F32)],
        [g_sums[0], g_two, *(packs[s] for s in others)], [VMEM] * A, [VMEM] * 3,
        moved=6 * A * g_sums[0].size, vmem=8, name="matrices",
    )
    d_last = arrived
    query_own, query_far = add_up([query_keep, query_recv], [[(0, (b,)), (1, (b,))] for b in range(2)])
    grad_tokens = call(
        finish_body, sds((local, width), BF),
        [own, d_middle, row_vec, d_last, d_next, query_own, swap_x(query_far)],
        [VMEM] * 7, VMEM, flops=20 * local * width, moved=16 * local * width, vmem=8, name="finish",
    )
    return (
        outputs[None],
        grad_tokens[None],
        grad_qkv,
        grad_out,
        grad_up,
        grad_down,
        *(v.reshape(part) for v in vector_grads[:7]),
        up_grad.reshape(blocks * part),
        vector_grads[7].reshape(part),
    )


def solution(mesh):
    both = ("rows", "fsdp")
    matrix, vector, act, table = P(both, None), P(both), P("fsdp", "rows", None), P("fsdp", None)
    return jax.shard_map(
        functools.partial(shards, R=mesh.shape["rows"], F=mesh.shape["fsdp"]),
        mesh=mesh,
        in_specs=(act,) + (matrix,) * 4 + (vector,) * 9 + (act,) + (table,) * 3,
        out_specs=(act, act) + (matrix,) * 4 + (vector,) * 9,
        check_vma=False,
    )
```
